128 devices in a mesh: seq: 32 (over x, y, core), head: 4 (over z).
Axes of the slice: x: 4, y: 4, z: 4, core: 2. Of those that a mesh axis runs over, the one named last changes fastest.
Arguments:
- query: bfloat16 [32768, 256], P('seq', 'head'), may hold values from -6 to 6
- key_feat: bfloat16 [32768, 256], P('seq', 'head'), may hold values from -6 to 6
- values: bfloat16 [32768, 2048], P('seq', 'head'), may hold values from -6 to 6
- conv_w: float32 [3, 2048], P(None, 'head'), may hold values from -3 to 3
- gain: float32 [2048], P('head'), may hold values from 0.1 to 1.9
- w_out: bfloat16 [4096, 2048], P(None, 'head'), may hold values from -0.125 to 0.125
- cotangent: bfloat16 [32768, 4096], P('seq', 'head'), may hold values from -6 to 6
Outputs:
- mixed: bfloat16 [32768, 4096], P('seq', 'head')
- grad_query: bfloat16 [32768, 256], P('seq', 'head')
- grad_key: bfloat16 [32768, 256], P('seq', 'head')
- grad_values: bfloat16 [32768, 2048], P('seq', 'head')
- grad_w_out: bfloat16 [4096, 2048], P('seq', 'head')
The draws below stay inside these ranges and needn't reach their ends.
All inputs are finite; a program needn't handle non-finite values.
Results may differ from the reference program's by a relative error of at most 0.024.
Values may be sent and summed in bfloat16 or wider, within the bound.
A program may use at most 192 MiB of HBM per device.

```python
import jax
import jax.numpy as jnp
from jax import lax

D = 4096
HEADS = 16
FD = 16
DV = 128
KW = 3
BLOCK = 256
TOKENS = 32768
HD = 2048
N_HEAD = 4


def with_spikes(drawn, rng, source, target, shards_of, factor):
    owner, partner = [(jnp.arange(drawn.shape[axis_at]) // (drawn.shape[axis_at] // shards_of)).reshape([-1 if axis == axis_at else 1 for axis in range(drawn.ndim)]) for axis_at in (source, target)]
    chosen = jax.random.permutation(rng, shards_of)[partner]
    strong = (owner == chosen) | (owner == (partner + shards_of // 2) % shards_of)
    return jnp.where(strong, factor * drawn, drawn)


def block_levels(key, shape, pieces, smallest, largest):
    factor_of, own = 1.0, jax.random.fold_in(key, 6)
    for dim, blocks in pieces:
        draws = jnp.exp(jax.random.uniform(jax.random.fold_in(own, dim), (blocks,), jnp.float32, smallest / len(pieces), largest / len(pieces)))
        factor_of = factor_of * jnp.repeat(draws, shape[dim] // blocks).reshape([-1 if axis == dim else 1 for axis in range(len(shape))])
    return factor_of


def bell_draw(rng, shape, scale, most, split=(), held_as=jnp.bfloat16):
    entries = jax.random.normal(rng, shape, jnp.float32) * scale
    if len(split) > 0:
        entries = block_levels(rng, shape, split, -0.22, 0.18) * entries
    return jnp.clip(entries, min=-most, max=most).astype(held_as)


def bell_draw_with(own_key, dims, spread, limit, cuts, heavy, held_as=jnp.bfloat16):
    entries = spread * jax.random.normal(own_key, dims, jnp.float32)
    if cuts:
        entries = entries * block_levels(own_key, dims, cuts, -0.22, 0.18)
    return jnp.clip(with_spikes(entries, jax.random.fold_in(own_key, 3), *heavy), -limit, limit).astype(held_as)


def setup_inputs(seed: int = 0) -> dict:
    splits = jax.random.split(jax.random.key(seed), 8)
    query = bell_draw(splits[0], (TOKENS, HEADS * FD), 1.0, 6.0, ((0, 32), (1, 4)))
    key_feat = bell_draw(splits[1], (TOKENS, HEADS * FD), 1.0, 6.0, ((0, 32), (1, 4)))
    values = bell_draw(splits[2], (TOKENS, HD), 1.0, 6.0, ((0, 32), (1, 4)))
    conv_w = bell_draw(splits[3], (KW, HD), 0.5, 3.0, ((1, 4),), jnp.float32)
    gain = jnp.clip(1.0 + 0.18 * jax.random.normal(splits[4], (HD,), jnp.float32), 0.1, 1.9)
    w_out = bell_draw(splits[5], (D, HD), HD ** -0.5, 0.125, ((1, 4),))
    cotangent = bell_draw_with(splits[6], (TOKENS, D), 1.0, 6.0, ((0, 32), (1, 4)), (0, 1, 32, 2.75))
    return {"query": query, "key_feat": key_feat, "values": values, "conv_w": conv_w, "gain": gain, "w_out": w_out, "cotangent": cotangent}


EPSILON = 1e-05

def features(inputs, width):
    first = width ** (-0.25)
    second = (2.0 * width) ** (-0.5)
    outer = (inputs[..., :, None] * inputs[..., None, :]).reshape(inputs.shape[:-1] + (width * width,))
    ones = jnp.ones(inputs.shape[:-1] + (1,), inputs.dtype)
    return jnp.concatenate([ones, inputs * first, outer * second], axis=-1)

def feature_grad(upstream, inputs, width):
    first = width ** (-0.25)
    second = (2.0 * width) ** (-0.5)
    linear = upstream[..., 1:1 + width] * first
    square = upstream[..., 1 + width:].reshape(upstream.shape[:-1] + (width, width)) * second
    return linear + jnp.einsum('...ij,...j->...i', square, inputs) + jnp.einsum('...ji,...j->...i', square, inputs)

def to_blocks(array, block, heads):
    rows, cols = array.shape
    return array.reshape(rows // block, block, heads, cols // heads).transpose(0, 2, 1, 3)

def from_blocks(array):
    count, heads, block, cols = array.shape
    return array.transpose(0, 2, 1, 3).reshape(count * block, heads * cols)

def exclusive_forward(states):
    totals = jnp.cumsum(states, axis=0)
    return jnp.concatenate([jnp.zeros_like(states[:1]), totals[:-1]], axis=0)

def exclusive_backward(states):
    totals = jnp.cumsum(states[::-1], axis=0)[::-1]
    return jnp.concatenate([totals[1:], jnp.zeros_like(states[:1])], axis=0)

def reference(query, key_feat, values, conv_w, gain, w_out, cotangent):
    span = KW - 1
    f32 = jnp.float32
    mask = jnp.tril(jnp.ones((BLOCK, BLOCK), f32))
    values_f = values.astype(f32)
    padded = jnp.concatenate([jnp.zeros((span, HD), f32), values_f], axis=0)
    conv_acc = conv_w[0] * values_f
    for lag in range(1, KW):
        conv_acc = conv_acc + conv_w[lag] * padded[span - lag:span - lag + TOKENS]
    conv_out = conv_acc.astype(jnp.bfloat16)
    query_blocks = to_blocks(query.astype(f32), BLOCK, HEADS)
    key_blocks = to_blocks(key_feat.astype(f32), BLOCK, HEADS)
    fq = features(query_blocks, FD).astype(jnp.bfloat16).astype(f32)
    fk = features(key_blocks, FD).astype(jnp.bfloat16).astype(f32)
    vc = to_blocks(conv_out, BLOCK, HEADS).astype(f32)
    attend = (jnp.einsum('nhif,nhjf->nhij', fq, fk) * mask).astype(jnp.bfloat16).astype(f32)
    block_states = jnp.einsum('nhjf,nhjd->nhfd', fk, vc)
    previous = exclusive_forward(block_states).astype(jnp.bfloat16).astype(f32)
    hidden = jnp.einsum('nhij,nhjd->nhid', attend, vc) + jnp.einsum('nhif,nhfd->nhid', fq, previous)
    scale = lax.rsqrt(lax.optimization_barrier(jnp.mean(hidden * hidden, axis=-1, keepdims=True)) + EPSILON)
    normed = hidden * scale
    gain_blocks = gain.reshape(HEADS, 1, DV)
    out_heads = from_blocks((normed * gain_blocks).astype(jnp.bfloat16))
    group = HD // N_HEAD
    mixed = jnp.zeros((TOKENS, D), f32)
    for index in range(N_HEAD):
        term = jnp.dot(out_heads[:, index * group:(index + 1) * group], w_out[:, index * group:(index + 1) * group].T, preferred_element_type=f32)
        rounded = lax.optimization_barrier(term.astype(jnp.bfloat16))
        mixed = mixed + rounded.astype(f32)
    mixed = mixed.astype(jnp.bfloat16)
    grad_out = jnp.dot(cotangent, w_out, preferred_element_type=f32)
    grad_w_out = jnp.dot(cotangent.T, out_heads, preferred_element_type=f32).astype(jnp.bfloat16)
    grad_normed = to_blocks(grad_out, BLOCK, HEADS) * gain_blocks
    grad_hidden = (scale * (grad_normed - normed * lax.optimization_barrier(jnp.mean(grad_normed * normed, axis=-1, keepdims=True)))).astype(jnp.bfloat16).astype(f32)
    block_grads = jnp.einsum('nhif,nhid->nhfd', fq, grad_hidden)
    following = exclusive_backward(block_grads).astype(jnp.bfloat16).astype(f32)
    grad_conv = from_blocks(jnp.einsum('nhij,nhid->nhjd', attend, grad_hidden) + jnp.einsum('nhjf,nhfd->nhjd', fk, following))
    products = (jnp.einsum('nhid,nhjd->nhij', grad_hidden, vc) * mask).astype(jnp.bfloat16).astype(f32)
    grad_fq = jnp.einsum('nhij,nhjf->nhif', products, fk) + jnp.einsum('nhid,nhfd->nhif', grad_hidden, previous)
    grad_fk = jnp.einsum('nhij,nhif->nhjf', products, fq) + jnp.einsum('nhjd,nhfd->nhjf', vc, following)
    grad_query = from_blocks(feature_grad(grad_fq, query_blocks, FD)).astype(jnp.bfloat16)
    grad_key = from_blocks(feature_grad(grad_fk, key_blocks, FD)).astype(jnp.bfloat16)
    extended = jnp.concatenate([grad_conv, jnp.zeros((span, HD), f32)], axis=0)
    grad_acc = conv_w[0] * grad_conv
    for lag in range(1, KW):
        grad_acc = grad_acc + conv_w[lag] * extended[lag:lag + TOKENS]
    grad_values = grad_acc.astype(jnp.bfloat16)
    return (mixed, grad_query, grad_key, grad_values, grad_w_out)
```

```python
import functools

import jax
import jax.numpy as jnp
from jax import lax
from jax.experimental import pallas as pl
from jax.experimental.pallas import tpu as pltpu
from jax.sharding import PartitionSpec as P

f32 = jnp.float32
bf16 = jnp.bfloat16
FD = 16
BLOCK = 256
ROWS = 1024
HEADS = 4
NB = ROWS // BLOCK
DV = 128
CH = HEADS * DV
FEAT = 1024
NF = 160
EPSILON = 1e-05
VMEM_LIMIT = 56 * 1024 * 1024


def nn(a, b):
    return lax.dot_general(a, b, (((1,), (0,)), ((), ())), preferred_element_type=f32)


def nt(a, b):
    return lax.dot_general(a, b, (((1,), (1,)), ((), ())), preferred_element_type=f32)


def tn(a, b):
    return lax.dot_general(a, b, (((0,), (0,)), ((), ())), preferred_element_type=f32)


def place():
    s = lax.axis_index("seq")
    z = lax.axis_index("head")
    return s, z, s // 8, (s // 2) % 4, s % 2


def seq_of(x, y, c):
    return (x * 4 + y) * 2 + c


def remote(src, dst, send_sem, recv_sem, seq, head):
    copy = pltpu.make_async_remote_copy(
        src_ref=src,
        dst_ref=dst,
        send_sem=send_sem,
        recv_sem=recv_sem,
        device_id={"seq": seq, "head": head},
        device_id_type=pl.DeviceIdType.MESH,
    )
    copy.start()
    return copy


def greet(devices):
    barrier = pltpu.get_barrier_semaphore()
    for seq, head in devices:
        pl.semaphore_signal(
            barrier, inc=1, device_id={"seq": seq, "head": head}, device_id_type=pl.DeviceIdType.MESH
        )
    pl.semaphore_wait(barrier, len(devices))


def plane_peers(s, z, x, y, c):
    out = [(seq_of(x, y, 1 - c), z)]
    for j in (1, 2, 3):
        out.append((seq_of((x + j) % 4, y, c), z))
        out.append((seq_of(x, (y + j) % 4, c), z))
    return out


def eye64():
    r = lax.broadcasted_iota(jnp.int32, (64, 64), 0)
    c = lax.broadcasted_iota(jnp.int32, (64, 64), 1)
    return (r == c).astype(bf16)


def spread(x_ref, x2_ref):
    xt = nt(eye64(), x_ref[...])
    for h in range(HEADS):
        x2_ref[h, 0:16, :] = xt[16 * h : 16 * h + 16]
        x2_ref[h, 16:32, :] = xt[16 * h : 16 * h + 16]


def phi(x2_ref, h, cols):
    x = x2_ref[h, 0:16, cols]
    parts = [x * x]
    for d in range(1, 8):
        parts.append(x * x2_ref[h, d : d + 16, cols])
    parts.append(x[0:8] * x2_ref[h, 8:16, cols])
    parts.append((lax.broadcasted_iota(jnp.int32, (8, BLOCK), 0) == 0).astype(f32))
    parts.append(x)
    return jnp.concatenate(parts, axis=0).astype(bf16)


def phi_back(g, x2_ref, t2_ref, h, cols):
    x = x2_ref[h, 0:16, cols]
    acc = g[144:160] + 2.0 * g[0:16] * x
    for d in range(1, 8):
        gd = g[16 * d : 16 * d + 16]
        acc = acc + gd * x2_ref[h, d : d + 16, cols]
        t = gd * x
        t2_ref[d - 1, 0:16, :] = t
        t2_ref[d - 1, 16:32, :] = t
        acc = acc + t2_ref[d - 1, 16 - d : 32 - d, :]
    g8 = g[128:136]
    low = g8 * x2_ref[h, 8:16, cols]
    high = g8 * x[0:8]
    return acc + jnp.concatenate([low, high], axis=0)


def weights():
    r = lax.broadcasted_iota(jnp.int32, (NF, DV), 0)
    return jnp.where(
        r < 16, 1.0 / 32, jnp.where(r < 136, 1.0 / 16, jnp.where(r < 144, 1.0, 0.25))
    ).astype(f32)


def head_lanes(h):
    lane = lax.broadcasted_iota(jnp.int32, (BLOCK, HEADS * FD), 1)
    return (lane >= 16 * h) & (lane < 16 * h + 16)


def lower():
    r = lax.broadcasted_iota(jnp.int32, (BLOCK, BLOCK), 0)
    c = lax.broadcasted_iota(jnp.int32, (BLOCK, BLOCK), 1)
    return r >= c


def only(x, mask):
    return jnp.where(mask, x.astype(f32), 0.0).astype(bf16)


SCAN_SCRATCH = [
    pltpu.VMEM((HEADS, NF, DV), f32),
    pltpu.VMEM((2, NF, DV), f32),
    pltpu.VMEM((2, NF, DV), bf16),
    pltpu.VMEM((3, 2, NF, DV), bf16),
    pltpu.VMEM((2, NF, DV), bf16),
    pltpu.VMEM((3, 2, NF, DV), bf16),
    pltpu.VMEM((2, NF, DV), f32),
    pltpu.VMEM((2, NF, DV), f32),
    pltpu.VMEM((2, NF, DV), f32),
    pltpu.VMEM((HEADS, NF, DV), f32),
    pltpu.SemaphoreType.DMA((8,)),
    pltpu.SemaphoreType.DMA((8,)),
]


def scan_steps(refs, forward):
    tot, ra, ys, yr, xs, xr, py, fs, fr, ent, ssem, rsem = refs
    s, z, x, y, c = place()
    sibling = seq_of(x, y, 1 - c)
    mine = pl.ds(2 * c, 2)
    copies = {}

    def counts(me, j):
        met = (me - j >= 0) if forward else (me - j < 0)
        return jnp.where(met, 1.0, 0.0).astype(f32)

    def pair():
        copies["a"] = remote(tot.at[pl.ds(2 * (1 - c), 2)], ra, ssem.at[0], rsem.at[0], sibling, z)

    def along_y():
        copies["a"].wait_recv()
        ys[...] = (tot[mine] + ra[...]).astype(bf16)
        for j in (1, 2, 3):
            copies["y", j] = remote(
                ys, yr.at[j - 1], ssem.at[j], rsem.at[j], seq_of(x, (y + j) % 4, c), z
            )

    def along_x():
        row = tot[mine] + ra[...]
        before = jnp.zeros((2, NF, DV), f32)
        for j in (1, 3, 2):
            copies["y", j].wait_recv()
            got = yr[j - 1].astype(f32)
            row = row + got
            before = before + got * counts(y, j)
        xs[...] = row.astype(bf16)
        py[...] = before
        for j in (1, 2, 3):
            copies["x", j] = remote(
                xs, xr.at[j - 1], ssem.at[3 + j], rsem.at[3 + j], seq_of((x + j) % 4, y, c), z
            )

    def back():
        before = py[...]
        for j in (1, 3, 2):
            copies["x", j].wait_recv()
            before = before + xr[j - 1].astype(f32) * counts(x, j)
        first = jnp.where(c == 0, 1.0, 0.0).astype(f32)
        other = first if forward else 1.0 - first
        fs[...] = before + tot[mine] * other
        ent[mine] = before + ra[...] * (1.0 - other)
        copies["f"] = remote(fs, fr, ssem.at[7], rsem.at[7], sibling, z)

    def done():
        copies["f"].wait_recv()
        ent[pl.ds(2 * (1 - c), 2)] = fr[...]
        for copy in copies.values():
            copy.wait_send()

    return pair, along_y, along_x, back, done


def forward_kernel(
    q_ref, k_ref, v_ref, cw_ref, gain_ref,
    o_ref, hid_ref, conv_ref, prev_ref,
    halo, vx, qx, kx, st, hsem, *scan_refs,
):
    s, z, x, y, c = place()
    tot, ent = scan_refs[0], scan_refs[9]
    after, before = (s + 1) % 32, (s + 31) % 32
    greet(plane_peers(s, z, x, y, c) + [(after, z), (before, z)])
    edge = remote(v_ref.at[pl.ds(ROWS - 16, 16)], halo, hsem.at[0], hsem.at[1], after, z)
    spread(k_ref, kx)
    spread(q_ref, qx)
    vx[8 : 8 + ROWS, :] = v_ref[...].astype(f32)
    edge.wait_recv()
    inside = jnp.where(s > 0, 1.0, 0.0).astype(f32)
    vx[0:8, :] = halo[...].astype(f32)[8:16] * inside
    for n in range(NB):
        at = 8 + n * BLOCK
        acc = cw_ref[0:1, :] * vx[at : at + BLOCK, :]
        for j in (1, 2):
            acc = acc + cw_ref[j : j + 1, :] * vx[at - j : at - j + BLOCK, :]
        conv_ref[n * BLOCK : (n + 1) * BLOCK, :] = acc.astype(bf16)
    tot[...] = jnp.zeros_like(tot)

    def states(n, carry):
        rows = pl.ds(pl.multiple_of(n * BLOCK, BLOCK), BLOCK)
        for h in range(HEADS):
            own = nn(phi(kx, h, rows), conv_ref[rows, h * DV : (h + 1) * DV])
            st[n, h] = own
            tot[h] += own
        return carry

    lax.fori_loop(0, NB, states, 0)
    pair, along_y, along_x, back, done = scan_steps(scan_refs, True)
    mask = lower()

    def intra(n, carry):
        rows = pl.ds(pl.multiple_of(n * BLOCK, BLOCK), BLOCK)
        q = q_ref[rows, :]
        k = k_ref[rows, :]
        for h in range(HEADS):
            sc = nt(q, only(k, head_lanes(h)))
            att = jnp.where(mask, 1.0 + sc * (0.25 + sc * (1.0 / 32)), 0.0).astype(bf16)
            hid_ref[rows, h * DV : (h + 1) * DV] = nn(att, conv_ref[rows, h * DV : (h + 1) * DV])
        return carry

    pair()
    lax.fori_loop(0, 1, intra, 0)
    along_y()
    lax.fori_loop(1, 3, intra, 0)
    along_x()
    lax.fori_loop(3, 4, intra, 0)
    back()
    done()
    wts = weights()

    def finish(n, carry):
        rows = pl.ds(pl.multiple_of(n * BLOCK, BLOCK), BLOCK)
        for h in range(HEADS):
            lanes = slice(h * DV, (h + 1) * DV)
            state = ent[h]
            ent[h] = state + st[n, h]
            prev = (state * wts).astype(bf16)
            prev_ref[n, h] = prev
            hidden = hid_ref[rows, lanes] + tn(phi(qx, h, rows), prev)
            hid_ref[rows, lanes] = hidden
            scale = lax.rsqrt(jnp.mean(hidden * hidden, axis=-1, keepdims=True) + EPSILON)
            o_ref[rows, lanes] = (hidden * scale * gain_ref[0:1, lanes]).astype(bf16)
        return carry

    lax.fori_loop(0, NB, finish, 0)
    edge.wait_send()


def forward_call(q, k, v, cw, gain):
    vm = pl.BlockSpec(memory_space=pltpu.VMEM)
    return pl.pallas_call(
        forward_kernel,
        out_shape=(
            jax.ShapeDtypeStruct((ROWS, CH), bf16),
            jax.ShapeDtypeStruct((ROWS, CH), f32),
            jax.ShapeDtypeStruct((ROWS, CH), bf16),
            jax.ShapeDtypeStruct((NB, HEADS, NF, DV), bf16),
        ),
        in_specs=[vm] * 5,
        out_specs=(vm,) * 4,
        scratch_shapes=[
            pltpu.VMEM((16, CH), bf16),
            pltpu.VMEM((8 + ROWS, CH), f32),
            pltpu.VMEM((HEADS, 32, ROWS), f32),
            pltpu.VMEM((HEADS, 32, ROWS), f32),
            pltpu.VMEM((NB, HEADS, NF, DV), f32),
            pltpu.SemaphoreType.DMA((2,)),
        ]
        + SCAN_SCRATCH,
        compiler_params=pltpu.CompilerParams(
            collective_id=0, has_side_effects=True, vmem_limit_bytes=VMEM_LIMIT
        ),
        name="forward_attention",
    )(q, k, v, cw, gain)


def project_kernel(
    o_hbm, w_hbm, cot_hbm,
    mixed_ref, gw_ref, go_ref,
    oall, wt, cot, cott, opp, to_r, to_l, opp_l, opp_r, from_r, from_l,
    gwp, r1, gsum, yr, xs, xr, fin, lsem, zs, zr, ws, wr, gs, gr,
):
    s, z, x, y, c = place()
    right, left = (z + 1) % 4, (z + 3) % 4
    sibling = seq_of(x, y, 1 - c)
    partner = (seq_of(z, y, c), x)
    greet(
        plane_peers(s, z, x, y, c)
        + [(s, (z + k) % 4) for k in (1, 2, 3)]
        + [partner]
    )
    sends = []

    def go(*args):
        copy = remote(*args)
        sends.append(copy)
        return copy

    ag = {}
    for b in (0, 1, 2, 3):
        to_right = pl.ds(b * BLOCK, BLOCK)
        ag["l", b] = go(o_hbm.at[to_right], oall.at[3, to_right], zs.at[b], zr.at[b], s, right)
        e = (b + 2) % 4
        to_left = pl.ds(e * BLOCK, BLOCK)
        ag["r", e] = go(
            o_hbm.at[to_left], oall.at[1, to_left], zs.at[4 + e], zr.at[4 + e], s, left
        )
    row = c * 512 + x * 128 + y * 32
    wz = {}
    for k in (1, 2, 3):
        there = (z + k) % 4
        wz[k] = go(
            w_hbm.at[pl.ds(pl.multiple_of(there * FEAT + row, 32), 32)],
            wt.at[4 - k, pl.ds(pl.multiple_of(row, 32), 32)],
            ws.at[k - 1],
            wr.at[k - 1],
            s,
            there,
        )
    load_cot = pltpu.make_async_copy(cot_hbm, cot, lsem.at[0])
    load_cot.start()
    load_w = pltpu.make_async_copy(
        w_hbm.at[pl.ds(pl.multiple_of(z * FEAT, FEAT), FEAT)], wt.at[0], lsem.at[1]
    )
    load_w.start()
    load_o = pltpu.make_async_copy(o_hbm, oall.at[0], lsem.at[2])
    load_o.start()

    def piece(px, py, half):
        at = pl.multiple_of(c * 512 + px * 128 + py * 32, 32)
        return wt.at[pl.ds(1, 3), pl.ds(at, 32), pl.ds(half * 256, 256)]

    for k in (1, 2, 3):
        wz[k].wait_recv()
    w1 = {}
    for j in (1, 2, 3):
        own = piece(x, y, 0)
        w1[0, j] = go(own, own, ws.at[2 + j], wr.at[2 + j], seq_of((x + j) % 4, y, c), z)
        own = piece(x, y, 1)
        w1[1, j] = go(own, own, ws.at[5 + j], wr.at[5 + j], seq_of(x, (y + j) % 4, c), z)

    load_cot.wait()

    def flip(b, carry):
        at = pl.ds(pl.multiple_of(b * BLOCK, BLOCK), BLOCK)
        cott[:, at] = jnp.transpose(cot[at, :], (1, 0))
        return carry

    lax.fori_loop(0, NB, flip, 0)

    w2 = {}
    index = 9
    for i in (0, 1, 3, 2):
        for half in (0, 1):
            if i:
                w1[half, i].wait_recv()
            block = piece((x - i + 4) % 4, y, 0) if half == 0 else piece(x, (y - i + 4) % 4, 1)
            for j in (1, 2, 3):
                to = seq_of(x, (y + j) % 4, c) if half == 0 else seq_of((x + j) % 4, y, c)
                w2[half, i, j] = go(block, block, ws.at[index], wr.at[index], to, z)
                index += 1

    def gw_term(k):
        group = (z + k) % 4

        def part(t, carry):
            rows = pl.ds(pl.multiple_of(t * 256, 256), 256)
            term = nn(cott[rows, :], oall[k]).astype(bf16)
            gwp[0, group, t] = term[0:128]
            gwp[1, group, t] = term[128:256]
            return carry

        lax.fori_loop(0, 4, part, 0)
        return go(gwp.at[1 - c, group], r1.at[group], gs.at[k], gr.at[k], sibling, z)

    gy = {}

    def gw_pair(k, copy):
        group = (z + k) % 4
        copy.wait_recv()

        def part(t, carry):
            gsum[group, t] = (gwp[c, group, t].astype(f32) + r1[group, t].astype(f32)).astype(bf16)
            return carry

        lax.fori_loop(0, 4, part, 0)
        for j in (1, 2, 3):
            there = (y + j) % 4
            at = 4 + 3 * k + j - 1
            gy[k, j] = go(
                gsum.at[group, there], yr.at[group, j - 1], gs.at[at], gr.at[at], seq_of(x, there, c), z
            )

    def gw_rows(k):
        group = (z + k) % 4
        acc = gsum[group, y].astype(f32)
        for j in (1, 2, 3):
            gy[k, j].wait_recv()
            acc = acc + yr[group, j - 1].astype(f32)
        xs[group] = acc.astype(bf16)

    load_o.wait()
    gw0 = gw_term(0)
    for copy in w2.values():
        copy.wait_recv()
    half_w = wt.at[pl.ds(1, 3), pl.ds(pl.multiple_of(c * 512, 512), 512)]
    w3 = go(half_w, half_w, ws.at[index], wr.at[index], sibling, z)
    gw_pair(0, gw0)

    for b in (0, 1):
        ag["l", b].wait_recv()
        block = pl.ds(b * BLOCK, BLOCK)
        ag["f", b] = go(oall.at[3, block], oall.at[2, block], zs.at[8 + b], zr.at[8 + b], s, right)
        e = b + 2
        ag["r", e].wait_recv()
        block = pl.ds(e * BLOCK, BLOCK)
        ag["f", e] = go(oall.at[1, block], oall.at[2, block], zs.at[8 + e], zr.at[8 + e], s, left)
    w3.wait_recv()
    load_w.wait()

    def go_term(k, b):
        return nn(cot[b * BLOCK : (b + 1) * BLOCK, :], wt[k])

    rs = {}

    def rows_of(b):
        return pl.ds(b * BLOCK, BLOCK)

    def fill(k, dst, lo, hi):
        def part(b, carry):
            rows = pl.ds(pl.multiple_of(b * BLOCK, BLOCK), BLOCK)
            dst[rows, :] = nn(cot[rows, :], wt[k]).astype(bf16)
            return carry

        lax.fori_loop(lo, hi, part, 0)

    half_a, half_b = pl.ds(0, 512), pl.ds(512, 512)
    fill(2, opp, 0, 4)
    rs["or"] = go(opp.at[half_a], opp_l, zs.at[12], zr.at[12], s, right)
    rs["ol"] = go(opp.at[half_b], opp_r, zs.at[13], zr.at[13], s, left)
    fill(1, to_r, 2, 4)
    rs["dr"] = go(to_r.at[half_b], from_l.at[half_b], zs.at[14], zr.at[14], s, right)
    fill(3, to_l, 0, 2)
    rs["dl"] = go(to_l.at[half_a], from_r.at[half_a], zs.at[15], zr.at[15], s, left)

    for b in (2, 3):
        ag["l", b].wait_recv()
        ag["r", b - 2].wait_recv()
    gw1 = gw_term(1)
    gw3 = gw_term(3)
    gw_rows(0)
    gw_pair(1, gw1)
    gw_pair(3, gw3)
    for b in (0, 1, 2, 3):
        ag["f", b].wait_recv()
    gw2 = gw_term(2)

    def mix(t, carry):
        rows = pl.ds(pl.multiple_of((t // 2) * BLOCK, BLOCK), BLOCK)
        for u in (0, 1):
            cols = slice(512 * u, 512 * u + 512)
            acc = nt(oall[0, rows, :], wt[0, cols, :])
            for k in (1, 2, 3):
                acc = acc + nt(oall[k, rows, :], wt[k, cols, :])
            mixed_ref[rows, cols] = acc.astype(bf16)
        return carry

    gw_rows(1)
    gw_rows(3)
    gw_pair(2, gw2)

    def add_in(k, dst, got, lo):
        def part(b, carry):
            rows = pl.ds(pl.multiple_of(lo + b * BLOCK, BLOCK), BLOCK)
            here = pl.ds(pl.multiple_of(b * BLOCK, BLOCK), BLOCK)
            dst[rows, :] = (nn(cot[rows, :], wt[k]) + got[here, :].astype(f32)).astype(bf16)
            return carry

        lax.fori_loop(0, 2, part, 0)

    rs["or"].wait_recv()
    add_in(1, to_r, opp_l, 0)
    rs["ar"] = go(to_r.at[half_a], from_l.at[half_a], zs.at[16], zr.at[16], s, right)
    rs["ol"].wait_recv()
    add_in(3, to_l, opp_r, 512)
    rs["al"] = go(to_l.at[half_b], from_r.at[half_b], zs.at[17], zr.at[17], s, left)

    gw_rows(2)
    gx = {}
    for j in (1, 2, 3):
        there = (x + j) % 4
        gx[j] = go(
            xs.at[there], xr.at[j - 1], gs.at[15 + j], gr.at[15 + j], seq_of(there, y, c), z
        )

    def mix_rows(t, carry):
        return mix(2 * t, carry)

    lax.fori_loop(0, NB, mix_rows, 0)

    total = xs[x].astype(f32)
    for j in (1, 2, 3):
        gx[j].wait_recv()
        total = total + xr[j - 1].astype(f32)
    fin[...] = total.astype(bf16)
    stays = x == z

    @pl.when(stays)
    def _():
        gw_ref[...] = fin[...]

    @pl.when(jnp.logical_not(stays))
    def _():
        move = remote(fin, gw_ref, gs.at[19], gr.at[19], partner[0], partner[1])
        move.wait()

    def own(b, carry):
        rows = pl.ds(pl.multiple_of(b * BLOCK, BLOCK), BLOCK)
        go_ref[rows, :] = nn(cot[rows, :], wt[0])
        return carry

    lax.fori_loop(0, NB, own, 0)
    for name in ("dr", "dl", "ar", "al"):
        rs[name].wait_recv()

    def gather(b, carry):
        rows = pl.ds(pl.multiple_of(b * BLOCK, BLOCK), BLOCK)
        go_ref[rows, :] += from_r[rows, :].astype(f32) + from_l[rows, :].astype(f32)
        return carry

    lax.fori_loop(0, NB, gather, 0)
    for copy in sends:
        copy.wait_send()


def project_call(o, w, cot):
    vm = pl.BlockSpec(memory_space=pltpu.VMEM)
    hbm = pl.BlockSpec(memory_space=pl.ANY)
    dma = pltpu.SemaphoreType.DMA
    return pl.pallas_call(
        project_kernel,
        out_shape=(
            jax.ShapeDtypeStruct((ROWS, FEAT), bf16),
            jax.ShapeDtypeStruct((128, CH), bf16),
            jax.ShapeDtypeStruct((ROWS, CH), f32),
        ),
        in_specs=[hbm] * 3,
        out_specs=(vm,) * 3,
        scratch_shapes=[
            pltpu.VMEM((4, ROWS, CH), bf16),
            pltpu.VMEM((4, FEAT, CH), bf16),
            pltpu.VMEM((ROWS, FEAT), bf16),
            pltpu.VMEM((FEAT, ROWS), bf16),
            pltpu.VMEM((ROWS, CH), bf16),
            pltpu.VMEM((ROWS, CH), bf16),
            pltpu.VMEM((ROWS, CH), bf16),
            pltpu.VMEM((512, CH), bf16),
            pltpu.VMEM((512, CH), bf16),
            pltpu.VMEM((ROWS, CH), bf16),
            pltpu.VMEM((ROWS, CH), bf16),
            pltpu.VMEM((2, 4, 4, 128, CH), bf16),
            pltpu.VMEM((4, 4, 128, CH), bf16),
            pltpu.VMEM((4, 4, 128, CH), bf16),
            pltpu.VMEM((4, 3, 128, CH), bf16),
            pltpu.VMEM((4, 128, CH), bf16),
            pltpu.VMEM((3, 128, CH), bf16),
            pltpu.VMEM((128, CH), bf16),
            dma((3,)),
            dma((18,)),
            dma((18,)),
            dma((34,)),
            dma((34,)),
            dma((20,)),
            dma((20,)),
        ],
        compiler_params=pltpu.CompilerParams(
            collective_id=1, has_side_effects=True, vmem_limit_bytes=VMEM_LIMIT
        ),
        name="projections",
    )(o, w, cot)


def backward_kernel(
    q_ref, k_ref, conv_ref, cw_ref, gain_ref, hid_ref, go_ref, prev_ref,
    gq_ref, gk_ref, gv_ref,
    halo, edge_rows, qx, kx, t2, gh, bg, fw, gc, gi, dx, hsem, *scan_refs,
):
    s, z, x, y, c = place()
    tot, ent = scan_refs[0], scan_refs[9]
    after, before = (s + 1) % 32, (s + 31) % 32
    greet(plane_peers(s, z, x, y, c) + [(after, z), (before, z)])
    spread(k_ref, kx)
    spread(q_ref, qx)
    tot[...] = jnp.zeros_like(tot)

    def states(n, carry):
        rows = pl.ds(pl.multiple_of(n * BLOCK, BLOCK), BLOCK)
        for h in range(HEADS):
            lanes = slice(h * DV, (h + 1) * DV)
            hidden = hid_ref[rows, lanes]
            scale = lax.rsqrt(jnp.mean(hidden * hidden, axis=-1, keepdims=True) + EPSILON)
            normed = hidden * scale
            up = go_ref[rows, lanes] * gain_ref[0:1, lanes]
            grad = scale * (up - normed * jnp.mean(up * normed, axis=-1, keepdims=True))
            grad = grad.astype(bf16)
            gh[rows, lanes] = grad
            own = nn(phi(qx, h, rows), grad)
            bg[n, h] = own
            tot[h] += own
        return carry

    lax.fori_loop(0, NB, states, 0)
    pair, along_y, along_x, back, done = scan_steps(scan_refs, False)
    mask = lower()
    mask_t = jnp.logical_not(mask) | (
        lax.broadcasted_iota(jnp.int32, (BLOCK, BLOCK), 0)
        == lax.broadcasted_iota(jnp.int32, (BLOCK, BLOCK), 1)
    )

    def intra(n, carry):
        rows = pl.ds(pl.multiple_of(n * BLOCK, BLOCK), BLOCK)
        q = q_ref[rows, :]
        k = k_ref[rows, :]
        to_q = jnp.zeros((BLOCK, HEADS * FD), f32)
        to_k = jnp.zeros((BLOCK, HEADS * FD), f32)
        for h in range(HEADS):
            lanes = slice(h * DV, (h + 1) * DV)
            kh = only(k, head_lanes(h))
            qh = only(q, head_lanes(h))
            g = gh[rows, lanes]
            v = conv_ref[rows, lanes]
            sc = nt(qh, kh)
            ds = jnp.where(mask, nt(g, v) * (0.25 + sc * (1.0 / 16)), 0.0).astype(bf16)
            to_q = to_q + nn(ds, kh)
            sc_t = nt(kh, qh)
            ds_t = jnp.where(mask_t, nt(v, g) * (0.25 + sc_t * (1.0 / 16)), 0.0).astype(bf16)
            to_k = to_k + nn(ds_t, qh)
            att = jnp.where(mask_t, 1.0 + sc_t * (0.25 + sc_t * (1.0 / 32)), 0.0).astype(bf16)
            gc[rows, lanes] = nn(att, g)
            dx[16 * h : 16 * h + 16, rows] = phi_back(nt(prev_ref[n, h], g), qx, t2, h, rows)
        gi[rows, 0:64] = to_q
        gi[rows, 64:128] = to_k
        return carry

    pair()
    lax.fori_loop(0, 1, intra, 0)
    along_y()
    lax.fori_loop(1, 3, intra, 0)
    along_x()
    lax.fori_loop(3, 4, intra, 0)
    back()
    done()
    wts = weights()

    def suffix(t, carry):
        n = NB - 1 - t
        for h in range(HEADS):
            state = ent[h]
            ent[h] = state + bg[n, h]
            fw[n, h] = (state * wts).astype(bf16)
        return carry

    lax.fori_loop(0, NB, suffix, 0)

    def finish(n, carry):
        rows = pl.ds(pl.multiple_of(n * BLOCK, BLOCK), BLOCK)
        for h in range(HEADS):
            lanes = slice(h * DV, (h + 1) * DV)
            gc[rows, lanes] += tn(phi(kx, h, rows), fw[n, h])
            grad = nt(fw[n, h], conv_ref[rows, lanes])
            dx[64 + 16 * h : 64 + 16 * h + 16, rows] = phi_back(grad, kx, t2, h, rows)
        both = gi[rows, :] + jnp.transpose(dx[:, rows], (1, 0))
        gq_ref[rows, :] = both[:, 0:64].astype(bf16)
        gk_ref[rows, :] = both[:, 64:128].astype(bf16)
        return carry

    lax.fori_loop(0, 1, finish, 0)
    edge_rows[...] = gc[0:8, :]
    edge = remote(edge_rows, halo, hsem.at[0], hsem.at[1], before, z)
    lax.fori_loop(1, NB, finish, 0)
    edge.wait()
    inside = jnp.where(s < 31, 1.0, 0.0).astype(f32)
    gc[ROWS : ROWS + 8, :] = halo[...] * inside
    for n in range(NB):
        at = n * BLOCK
        acc = cw_ref[0:1, :] * gc[at : at + BLOCK, :]
        for j in (1, 2):
            acc = acc + cw_ref[j : j + 1, :] * gc[at + j : at + j + BLOCK, :]
        gv_ref[at : at + BLOCK, :] = acc.astype(bf16)


def backward_call(q, k, conv, cw, gain, hid, go, prev):
    vm = pl.BlockSpec(memory_space=pltpu.VMEM)
    return pl.pallas_call(
        backward_kernel,
        out_shape=(
            jax.ShapeDtypeStruct((ROWS, HEADS * FD), bf16),
            jax.ShapeDtypeStruct((ROWS, HEADS * FD), bf16),
            jax.ShapeDtypeStruct((ROWS, CH), bf16),
        ),
        in_specs=[vm] * 8,
        out_specs=(vm,) * 3,
        scratch_shapes=[
            pltpu.VMEM((8, CH), f32),
            pltpu.VMEM((8, CH), f32),
            pltpu.VMEM((HEADS, 32, ROWS), f32),
            pltpu.VMEM((HEADS, 32, ROWS), f32),
            pltpu.VMEM((7, 32, BLOCK), f32),
            pltpu.VMEM((ROWS, CH), bf16),
            pltpu.VMEM((NB, HEADS, NF, DV), f32),
            pltpu.VMEM((NB, HEADS, NF, DV), bf16),
            pltpu.VMEM((ROWS + 8, CH), f32),
            pltpu.VMEM((ROWS, 128), f32),
            pltpu.VMEM((128, ROWS), f32),
            pltpu.SemaphoreType.DMA((2,)),
        ]
        + SCAN_SCRATCH,
        compiler_params=pltpu.CompilerParams(
            collective_id=2, has_side_effects=True, vmem_limit_bytes=VMEM_LIMIT
        ),
        name="backward_attention",
    )(q, k, conv, cw, gain, hid, go, prev)


def on_device(query, key_feat, values, conv_w, gain, w_out, cotangent):
    gain = gain.reshape(1, CH)
    heads_out, hidden, conv, prev = forward_call(query, key_feat, values, conv_w, gain)
    mixed, grad_w, grad_out = project_call(heads_out, w_out, cotangent)
    grad_q, grad_k, grad_v = backward_call(
        query, key_feat, conv, conv_w, gain, hidden, grad_out, prev
    )
    return mixed, grad_q, grad_k, grad_v, grad_w


def solution(mesh):
    both = P("seq", "head")
    return jax.shard_map(
        on_device,
        mesh=mesh,
        in_specs=(both, both, both, P(None, "head"), P("head"), P(None, "head"), both),
        out_specs=(both,) * 5,
        check_vma=False,
    )
```

```python
import functools

import jax
import jax.numpy as jnp
from jax import lax
from jax.experimental import pallas as pl
from jax.experimental.pallas import tpu as pltpu
from jax.sharding import PartitionSpec as P

f32 = jnp.float32
bf16 = jnp.bfloat16
FD = 16
BLOCK = 256
ROWS = 1024
HEADS = 4
NB = ROWS // BLOCK
DV = 128
CH = HEADS * DV
FEAT = 1024
NF = 160
EPSILON = 1e-05
VMEM_LIMIT = 60 * 1024 * 1024


def nn(a, b):
    return lax.dot_general(a, b, (((1,), (0,)), ((), ())), preferred_element_type=f32)


def nt(a, b):
    return lax.dot_general(a, b, (((1,), (1,)), ((), ())), preferred_element_type=f32)


def tn(a, b):
    return lax.dot_general(a, b, (((0,), (0,)), ((), ())), preferred_element_type=f32)


def place():
    s = lax.axis_index("seq")
    z = lax.axis_index("head")
    return s, z, s // 8, (s // 2) % 4, s % 2


def seq_of(x, y, c):
    return (x * 4 + y) * 2 + c


def remote(src, dst, send_sem, recv_sem, seq, head):
    copy = pltpu.make_async_remote_copy(
        src_ref=src,
        dst_ref=dst,
        send_sem=send_sem,
        recv_sem=recv_sem,
        device_id={"seq": seq, "head": head},
        device_id_type=pl.DeviceIdType.MESH,
    )
    copy.start()
    return copy


def greet(devices):
    barrier = pltpu.get_barrier_semaphore()
    for seq, head in devices:
        pl.semaphore_signal(
            barrier, inc=1, device_id={"seq": seq, "head": head}, device_id_type=pl.DeviceIdType.MESH
        )
    pl.semaphore_wait(barrier, len(devices))


def plane_peers(s, z, x, y, c):
    out = [(seq_of(x, y, 1 - c), z)]
    for j in (1, 2, 3):
        out.append((seq_of((x + j) % 4, y, c), z))
        out.append((seq_of(x, (y + j) % 4, c), z))
    return out


def spread(xt_ref, x2_ref):
    for h in range(HEADS):
        x = xt_ref[16 * h : 16 * h + 16, :].astype(f32)
        x2_ref[h, 0:16, :] = x
        x2_ref[h, 16:32, :] = x


def phi(x2_ref, h, cols):
    x = x2_ref[h, 0:16, cols]
    parts = [x * x]
    for d in range(1, 8):
        parts.append(x * x2_ref[h, d : d + 16, cols])
    parts.append(x[0:8] * x2_ref[h, 8:16, cols])
    parts.append((lax.broadcasted_iota(jnp.int32, (8, BLOCK), 0) == 0).astype(f32))
    parts.append(x)
    return jnp.concatenate(parts, axis=0).astype(bf16)


def phi_back(g, x2_ref, t2_ref, h, cols):
    x = x2_ref[h, 0:16, cols]
    acc = g[144:160] + 2.0 * g[0:16] * x
    for d in range(1, 8):
        gd = g[16 * d : 16 * d + 16]
        acc = acc + gd * x2_ref[h, d : d + 16, cols]
        t = gd * x
        t2_ref[d - 1, 0:16, :] = t
        t2_ref[d - 1, 16:32, :] = t
        acc = acc + t2_ref[d - 1, 16 - d : 32 - d, :]
    g8 = g[128:136]
    low = g8 * x2_ref[h, 8:16, cols]
    high = g8 * x[0:8]
    return acc + jnp.concatenate([low, high], axis=0)


def weights():
    r = lax.broadcasted_iota(jnp.int32, (NF, DV), 0)
    return jnp.where(
        r < 16, 1.0 / 32, jnp.where(r < 136, 1.0 / 16, jnp.where(r < 144, 1.0, 0.25))
    ).astype(f32)


def lower():
    r = lax.broadcasted_iota(jnp.int32, (BLOCK, BLOCK), 0)
    c = lax.broadcasted_iota(jnp.int32, (BLOCK, BLOCK), 1)
    return r >= c


SCAN_SCRATCH = [
    pltpu.VMEM((HEADS, NF, DV), f32),
    pltpu.VMEM((2, NF, DV), f32),
    pltpu.VMEM((2, NF, DV), bf16),
    pltpu.VMEM((3, 2, NF, DV), bf16),
    pltpu.VMEM((2, NF, DV), bf16),
    pltpu.VMEM((3, 2, NF, DV), bf16),
    pltpu.VMEM((2, NF, DV), f32),
    pltpu.VMEM((2, NF, DV), f32),
    pltpu.VMEM((2, NF, DV), f32),
    pltpu.VMEM((HEADS, NF, DV), f32),
    pltpu.SemaphoreType.DMA((8,)),
    pltpu.SemaphoreType.DMA((8,)),
]


def scan_steps(refs, forward):
    tot, ra, ys, yr, xs, xr, py, fs, fr, ent, ssem, rsem = refs
    s, z, x, y, c = place()
    sibling = seq_of(x, y, 1 - c)
    mine = pl.ds(2 * c, 2)
    copies = {}

    def counts(me, j):
        met = (me - j >= 0) if forward else (me - j < 0)
        return jnp.where(met, 1.0, 0.0).astype(f32)

    def pair():
        copies["a"] = remote(tot.at[pl.ds(2 * (1 - c), 2)], ra, ssem.at[0], rsem.at[0], sibling, z)

    def along_y():
        copies["a"].wait_recv()
        ys[...] = (tot[mine] + ra[...]).astype(bf16)
        for j in (1, 2, 3):
            copies["y", j] = remote(
                ys, yr.at[j - 1], ssem.at[j], rsem.at[j], seq_of(x, (y + j) % 4, c), z
            )

    def along_x():
        row = tot[mine] + ra[...]
        before = jnp.zeros((2, NF, DV), f32)
        for j in (1, 3, 2):
            copies["y", j].wait_recv()
            got = yr[j - 1].astype(f32)
            row = row + got
            before = before + got * counts(y, j)
        xs[...] = row.astype(bf16)
        py[...] = before
        for j in (1, 2, 3):
            copies["x", j] = remote(
                xs, xr.at[j - 1], ssem.at[3 + j], rsem.at[3 + j], seq_of((x + j) % 4, y, c), z
            )

    def back():
        before = py[...]
        for j in (1, 3, 2):
            copies["x", j].wait_recv()
            before = before + xr[j - 1].astype(f32) * counts(x, j)
        first = jnp.where(c == 0, 1.0, 0.0).astype(f32)
        other = first if forward else 1.0 - first
        fs[...] = before + tot[mine] * other
        ent[mine] = before + ra[...] * (1.0 - other)
        copies["f"] = remote(fs, fr, ssem.at[7], rsem.at[7], sibling, z)

    def done():
        copies["f"].wait_recv()
        ent[pl.ds(2 * (1 - c), 2)] = fr[...]
        for copy in copies.values():
            copy.wait_send()

    return pair, along_y, along_x, back, done


SLOT = {2: 0, 1: 1, 3: 2, 0: 3}
GROUPS = ((2,), (1, 3))


def row_block(n):
    return pl.ds(pl.multiple_of(n * BLOCK, BLOCK), BLOCK)


def kernel(
    qt_ref, kt_ref, v_ref, cw_ref, gain_ref, w_hbm, cot_hbm,
    mixed_ref, gq_ref, gk_ref, gv_ref, gw_ref,
    halo, halo_back, edge_rows, wide, qx, kx, conv, st, hid, prev, oall,
    wt, cot, cott, opp, to_r, to_l, opp_l, opp_r, from_r, from_l,
    gwp, r1, gsum, p1a, p1b, s2a, s2b, p2a, p2b, fin, macc,
    gh, bg, fw, dx, t2,
    lsem, hsem, zs, zr, ws, wr, gs, gr, ms, mr, *scans,
):
    s, z, x, y, c = place()
    right, left = (z + 1) % 4, (z + 3) % 4
    sibling = seq_of(x, y, 1 - c)
    after, before = (s + 1) % 32, (s + 31) % 32
    sends = []

    def go(*args):
        copy = remote(*args)
        sends.append(copy)
        return copy

    barrier = pltpu.get_barrier_semaphore()

    def signal(seq, head):
        pl.semaphore_signal(
            barrier, inc=1, device_id={"seq": seq, "head": head}, device_id_type=pl.DeviceIdType.MESH
        )

    known = plane_peers(s, z, x, y, c) + [(s, (z + k) % 4) for k in (1, 2, 3)]
    known += [(after, z), (before, z)]
    known += [(seq_of(z, y, c), (z + k) % 4) for k in (1, 2, 3)]
    known += [(seq_of((x + j) % 4, y, c), x) for j in (1, 2, 3)]
    for seq, head in known:
        signal(seq, head)
    stays = x == z

    @pl.when(jnp.logical_not(stays))
    def _():
        signal(seq_of(z, y, c), z)
        signal(s, x)

    pl.semaphore_wait(barrier, len(known) + jnp.where(stays, 0, 2))

    row = c * 512 + x * 128 + y * 32
    wz = {}
    for k in (2, 1, 3):
        there = (z + k) % 4
        wz[k] = go(
            w_hbm.at[pl.ds(pl.multiple_of(there * FEAT + row, 32), 32)],
            wt.at[SLOT[4 - k], pl.ds(pl.multiple_of(row, 32), 32)],
            ws.at[k - 1],
            wr.at[k - 1],
            s,
            there,
        )
    edge = go(v_ref.at[pl.ds(ROWS - 16, 16)], halo, hsem.at[0], hsem.at[1], after, z)
    load_cot = pltpu.make_async_copy(cot_hbm, cot, lsem.at[0])
    load_cot.start()
    load_w = pltpu.make_async_copy(
        w_hbm.at[pl.ds(pl.multiple_of(z * FEAT, FEAT), FEAT)], wt.at[SLOT[0]], lsem.at[1]
    )
    load_w.start()

    def piece(group, px, py, half):
        at = pl.multiple_of(c * 512 + px * 128 + py * 32, 32)
        slots = pl.ds(0, 1) if group == 0 else pl.ds(1, 2)
        return wt.at[slots, pl.ds(at, 32), pl.ds(half * 256, 256)]

    w1, w2, w3 = {}, {}, {}

    def w_first(group):
        for k in GROUPS[group]:
            wz[4 - k].wait_recv()
        at = 3 + 31 * group
        for j in (1, 2, 3):
            own = piece(group, x, y, 0)
            i = at + j - 1
            w1[group, 0, j] = go(own, own, ws.at[i], wr.at[i], seq_of((x + j) % 4, y, c), z)
            own = piece(group, x, y, 1)
            i = at + j + 2
            w1[group, 1, j] = go(own, own, ws.at[i], wr.at[i], seq_of(x, (y + j) % 4, c), z)

    def w_second(group):
        at = 9 + 31 * group
        for i in (0, 1, 3, 2):
            for half in (0, 1):
                if i:
                    w1[group, half, i].wait_recv()
                if half == 0:
                    block = piece(group, (x - i + 4) % 4, y, 0)
                else:
                    block = piece(group, x, (y - i + 4) % 4, 1)
                for j in (1, 2, 3):
                    to = seq_of(x, (y + j) % 4, c) if half == 0 else seq_of((x + j) % 4, y, c)
                    w2[group, half, i, j] = go(block, block, ws.at[at], wr.at[at], to, z)
                    at += 1

    def w_third(group):
        for (which, *_), copy in w2.items():
            if which == group:
                copy.wait_recv()
        slots = pl.ds(0, 1) if group == 0 else pl.ds(1, 2)
        half = wt.at[slots, pl.ds(pl.multiple_of(c * 512, 512), 512)]
        i = 33 + 31 * group
        w3[group] = go(half, half, ws.at[i], wr.at[i], sibling, z)

    spread(kt_ref, kx)
    spread(qt_ref, qx)
    w_first(0)
    wide[8 : 8 + ROWS, :] = v_ref[...].astype(f32)
    w_first(1)
    edge.wait_recv()
    inside = jnp.where(s > 0, 1.0, 0.0).astype(f32)
    wide[0:8, :] = halo[...].astype(f32)[8:16] * inside

    def convolve(n):
        at = 8 + n * BLOCK
        acc = cw_ref[0:1, :] * wide[at : at + BLOCK, :]
        for j in (1, 2):
            acc = acc + cw_ref[j : j + 1, :] * wide[at - j : at - j + BLOCK, :]
        conv[n * BLOCK : (n + 1) * BLOCK, :] = acc.astype(bf16)

    convolve(0)
    w_second(0)
    for n in (1, 2, 3):
        convolve(n)
    w_second(1)
    load_cot.wait()

    def flip(b, carry):
        cott[:, row_block(b)] = jnp.transpose(cot[row_block(b), :], (1, 0))
        return carry

    lax.fori_loop(0, NB, flip, 0)
    w_third(0)

    scan_a, scan_b = scans[: len(scans) // 2], scans[len(scans) // 2 :]
    tot, ent = scan_a[0], scan_a[9]
    tot[...] = jnp.zeros_like(tot)

    def states(n, carry):
        rows = row_block(n)
        for h in range(HEADS):
            own = nn(phi(kx, h, rows), conv[rows, h * DV : (h + 1) * DV])
            st[n, h] = own
            tot[h] += own
        return carry

    lax.fori_loop(0, NB, states, 0)
    pair, along_y, along_x, back, done = scan_steps(scan_a, True)
    pair()

    def fill(k, dst, lo, hi):
        def part(b, carry):
            rows = row_block(b)
            dst[rows, :] = nn(cot[rows, :], wt[SLOT[k]]).astype(bf16)
            return carry

        lax.fori_loop(lo, hi, part, 0)

    half_a, half_b = pl.ds(0, 512), pl.ds(512, 512)
    rs = {}
    w3[0].wait_recv()
    fill(2, opp, 0, 4)
    rs["or"] = go(opp.at[half_a], opp_l, zs.at[12], zr.at[12], s, right)
    rs["ol"] = go(opp.at[half_b], opp_r, zs.at[13], zr.at[13], s, left)
    w_third(1)
    along_y()
    mask = lower()
    mask_t = jnp.logical_not(mask) | (
        lax.broadcasted_iota(jnp.int32, (BLOCK, BLOCK), 0)
        == lax.broadcasted_iota(jnp.int32, (BLOCK, BLOCK), 1)
    )

    def intra(n, carry):
        rows = row_block(n)
        for h in range(HEADS):
            entries = slice(16 * h, 16 * h + 16)
            sc = tn(qt_ref[entries, rows], kt_ref[entries, rows])
            att = jnp.where(mask, 1.0 + sc * (0.25 + sc * (1.0 / 32)), 0.0).astype(bf16)
            hid[rows, h * DV : (h + 1) * DV] = nn(att, conv[rows, h * DV : (h + 1) * DV])
        return carry

    lax.fori_loop(0, 2, intra, 0)
    w3[1].wait_recv()
    fill(1, to_r, 2, 4)
    rs["dr"] = go(to_r.at[half_b], from_l.at[half_b], zs.at[14], zr.at[14], s, right)
    fill(3, to_l, 0, 2)
    rs["dl"] = go(to_l.at[half_a], from_r.at[half_a], zs.at[15], zr.at[15], s, left)
    along_x()
    lax.fori_loop(2, 4, intra, 0)
    back()
    done()
    wts = weights()

    def finish(n, carry):
        rows = row_block(n)
        for h in range(HEADS):
            lanes = slice(h * DV, (h + 1) * DV)
            state = ent[h]
            ent[h] = state + st[n, h]
            before_block = (state * wts).astype(bf16)
            prev[n, h] = before_block
            hidden = hid[rows, lanes] + tn(phi(qx, h, rows), before_block)
            hid[rows, lanes] = hidden
            scale = lax.rsqrt(jnp.mean(hidden * hidden, axis=-1, keepdims=True) + EPSILON)
            oall[0, h, rows, :] = (hidden * scale * gain_ref[0:1, lanes]).astype(bf16)
        return carry

    lax.fori_loop(0, NB, finish, 0)

    def add_in(k, dst, got, lo):
        def part(b, carry):
            rows = row_block(lo + b)
            here = row_block(b)
            term = nn(cot[rows, :], wt[SLOT[k]]) + got[here, :].astype(f32)
            dst[rows, :] = term.astype(bf16)
            return carry

        lax.fori_loop(0, 2, part, 0)

    rs["or"].wait_recv()
    add_in(1, to_r, opp_l, 0)
    rs["ar"] = go(to_r.at[half_a], from_l.at[half_a], zs.at[16], zr.at[16], s, right)
    rs["ol"].wait_recv()
    add_in(3, to_l, opp_r, 2)
    rs["al"] = go(to_l.at[half_b], from_r.at[half_b], zs.at[17], zr.at[17], s, left)

    ag = {}
    for h in range(HEADS):
        ag["l", h] = go(oall.at[0, h], oall.at[3, h], zs.at[h], zr.at[h], s, right)
        e = (h + 2) % 4
        ag["r", e] = go(oall.at[0, e], oall.at[1, e], zs.at[4 + e], zr.at[4 + e], s, left)

    def hand_on(h):
        ag["l", h].wait_recv()
        ag["f", h] = go(oall.at[3, h], oall.at[2, h], zs.at[8 + h], zr.at[8 + h], s, right)
        e = h + 2
        ag["r", e].wait_recv()
        ag["f", e] = go(oall.at[1, e], oall.at[2, e], zs.at[8 + e], zr.at[8 + e], s, left)

    def four(k, rows):
        return jnp.concatenate([oall[k, h, rows, :] for h in range(HEADS)], axis=1)

    g1, g2, g3, g4 = {}, {}, {}, {}

    def gw_term(k):
        def part(t, carry):
            term = nn(cott[row_block(t), :], four(k, slice(None))).astype(bf16)
            gwp[0, k, t] = term[0:128]
            gwp[1, k, t] = term[128:256]
            return carry

        lax.fori_loop(0, 4, part, 0)
        g1[k] = go(gwp.at[1 - c, k], r1.at[k], gs.at[k], gr.at[k], sibling, z)

    def gw_first(k):
        g1[k].wait_recv()

        def part(t, carry):
            gsum[k, t] = (gwp[c, k, t].astype(f32) + r1[k, t].astype(f32)).astype(bf16)
            return carry

        lax.fori_loop(0, 4, part, 0)
        for j in (1, 2, 3):
            nx, ny = (x + j) % 4, (y + j) % 4
            i = 4 + 12 * k + j - 1
            rows = pl.ds(pl.multiple_of(nx * 32, 32), 32)
            g2[k, 0, j] = go(
                gsum.at[k, :, rows, pl.ds(0, 256)],
                p1a.at[k, j - 1], gs.at[i], gr.at[i], seq_of(nx, y, c), z,
            )
            i += 3
            g2[k, 1, j] = go(
                gsum.at[k, ny, :, pl.ds(256, 256)],
                p1b.at[k, j - 1], gs.at[i], gr.at[i], seq_of(x, ny, c), z,
            )

    my_rows = pl.ds(pl.multiple_of(x * 32, 32), 32)

    def gw_second(k):
        sum_a = gsum[k, :, my_rows, 0:256].astype(f32)
        sum_b = gsum[k, y, :, 256:512].astype(f32)
        for j in (1, 3, 2):
            g2[k, 0, j].wait_recv()
            sum_a = sum_a + p1a[k, j - 1].astype(f32)
            g2[k, 1, j].wait_recv()
            sum_b = sum_b + p1b[k, j - 1].astype(f32)
        s2a[k] = sum_a.astype(bf16)
        s2b[k] = sum_b.astype(bf16)
        for j in (1, 2, 3):
            nx, ny = (x + j) % 4, (y + j) % 4
            i = 4 + 12 * k + 6 + j - 1
            rows = pl.ds(pl.multiple_of(nx * 32, 32), 32)
            g3[k, 0, j] = go(
                s2a.at[k, ny], p2a.at[k, j - 1], gs.at[i], gr.at[i], seq_of(x, ny, c), z
            )
            i += 3
            g3[k, 1, j] = go(
                s2b.at[k, rows], p2b.at[k, j - 1], gs.at[i], gr.at[i], seq_of(nx, y, c), z
            )

    def gw_third(k):
        sum_a = s2a[k, y].astype(f32)
        sum_b = s2b[k, my_rows, :].astype(f32)
        for j in (1, 3, 2):
            g3[k, 0, j].wait_recv()
            sum_a = sum_a + p2a[k, j - 1].astype(f32)
            g3[k, 1, j].wait_recv()
            sum_b = sum_b + p2b[k, j - 1].astype(f32)
        fin[k, :, 0:256] = sum_a.astype(bf16)
        fin[k, :, 256:512] = sum_b.astype(bf16)

        def move():
            return pltpu.make_async_remote_copy(
                src_ref=fin.at[k],
                dst_ref=gw_ref.at[my_rows],
                send_sem=ms.at[k],
                recv_sem=mr.at[x],
                device_id={"seq": seq_of(z, y, c), "head": (z + k) % 4},
                device_id_type=pl.DeviceIdType.MESH,
            )

        if k:
            g4[k] = move
            move().start()
        else:

            @pl.when(stays)
            def _():
                gw_ref[my_rows, :] = fin[0]

            @pl.when(jnp.logical_not(stays))
            def _():
                move().start()
                move().wait_send()

    def gw_done():
        for k in (1, 2, 3):
            g4[k]().wait_send()
        for xs in range(4):

            @pl.when(jnp.logical_not(stays & (x == xs)))
            def _():
                pltpu.make_async_remote_copy(
                    src_ref=fin.at[0],
                    dst_ref=gw_ref.at[pl.ds(32 * xs, 32)],
                    send_sem=ms.at[0],
                    recv_sem=mr.at[xs],
                    device_id={"seq": seq_of(z, y, c), "head": (z + 1) % 4},
                    device_id_type=pl.DeviceIdType.MESH,
                ).wait_recv()

    def mix(ks, first, last):
        def part(b, carry):
            rows = row_block(b)
            for u in (0, 1):
                cols = slice(512 * u, 512 * u + 512)
                acc = None if first else macc[rows, cols]
                for k in ks:
                    term = nt(four(k, rows), wt[SLOT[k], cols, :])
                    acc = term if acc is None else acc + term
                if last:
                    mixed_ref[rows, cols] = acc.astype(bf16)
                else:
                    macc[rows, cols] = acc
            return carry

        lax.fori_loop(0, NB, part, 0)

    gw_term(0)
    load_w.wait()
    mix((0,), True, False)
    gw_first(0)

    for name in ("dr", "dl", "ar", "al"):
        rs[name].wait_recv()
    tot_b, ent_b = scan_b[0], scan_b[9]
    tot_b[...] = jnp.zeros_like(tot_b)

    def back_states(n, carry):
        rows = row_block(n)
        grad_out = nn(cot[rows, :], wt[SLOT[0]])
        grad_out = grad_out + from_r[rows, :].astype(f32) + from_l[rows, :].astype(f32)
        for h in range(HEADS):
            lanes = slice(h * DV, (h + 1) * DV)
            hidden = hid[rows, lanes]
            scale = lax.rsqrt(jnp.mean(hidden * hidden, axis=-1, keepdims=True) + EPSILON)
            normed = hidden * scale
            up = grad_out[:, lanes] * gain_ref[0:1, lanes]
            grad = scale * (up - normed * jnp.mean(up * normed, axis=-1, keepdims=True))
            grad = grad.astype(bf16)
            gh[rows, lanes] = grad
            own = nn(phi(qx, h, rows), grad)
            bg[n, h] = own
            tot_b[h] += own
        return carry

    lax.fori_loop(0, NB, back_states, 0)
    pair, along_y, along_x, back, done = scan_steps(scan_b, False)

    def back_intra(n, carry):
        rows = row_block(n)
        for h in range(HEADS):
            lanes = slice(h * DV, (h + 1) * DV)
            entries = slice(16 * h, 16 * h + 16)
            qh = qt_ref[entries, rows]
            kh = kt_ref[entries, rows]
            g = gh[rows, lanes]
            v = conv[rows, lanes]
            sc = tn(kh, qh)
            ds = jnp.where(mask_t, nt(v, g) * (0.25 + sc * (1.0 / 16)), 0.0).astype(bf16)
            att = jnp.where(mask_t, 1.0 + sc * (0.25 + sc * (1.0 / 32)), 0.0).astype(bf16)
            wide[rows, lanes] = nn(att, g)
            across = phi_back(nt(prev[n, h], g), qx, t2, h, rows)
            gq_ref[entries, rows] = (nn(kh, ds) + across).astype(bf16)
            dx[entries, rows] = nt(qh, ds)
        return carry

    pair()
    lax.fori_loop(0, 1, back_intra, 0)
    along_y()
    hand_on(0)
    lax.fori_loop(1, 3, back_intra, 0)
    along_x()
    hand_on(1)
    lax.fori_loop(3, 4, back_intra, 0)
    back()
    gw_second(0)
    done()

    def suffix(t, carry):
        n = NB - 1 - t
        for h in range(HEADS):
            state = ent_b[h]
            ent_b[h] = state + bg[n, h]
            fw[n, h] = (state * wts).astype(bf16)
        return carry

    lax.fori_loop(0, NB, suffix, 0)

    def back_finish(n, carry):
        rows = row_block(n)
        for h in range(HEADS):
            lanes = slice(h * DV, (h + 1) * DV)
            entries = slice(16 * h, 16 * h + 16)
            wide[rows, lanes] += tn(phi(kx, h, rows), fw[n, h])
            across = phi_back(nt(fw[n, h], conv[rows, lanes]), kx, t2, h, rows)
            gk_ref[entries, rows] = (dx[entries, rows] + across).astype(bf16)
        return carry

    lax.fori_loop(0, 1, back_finish, 0)
    edge_rows[...] = wide[0:8, :]
    edge_back = go(edge_rows, halo_back, hsem.at[2], hsem.at[3], before, z)
    lax.fori_loop(1, NB, back_finish, 0)
    edge_back.wait_recv()
    inside = jnp.where(s < 31, 1.0, 0.0).astype(f32)
    wide[ROWS : ROWS + 8, :] = halo_back[...] * inside
    for n in range(NB):
        at = n * BLOCK
        acc = cw_ref[0:1, :] * wide[at : at + BLOCK, :]
        for j in (1, 2):
            acc = acc + cw_ref[j : j + 1, :] * wide[at + j : at + j + BLOCK, :]
        gv_ref[at : at + BLOCK, :] = acc.astype(bf16)

    gw_third(0)
    ag["l", 2].wait_recv()
    ag["l", 3].wait_recv()
    gw_term(3)
    ag["r", 0].wait_recv()
    ag["r", 1].wait_recv()
    gw_term(1)
    gw_first(3)
    gw_first(1)
    mix((1, 3), False, False)
    gw_second(3)
    gw_second(1)
    for h in range(HEADS):
        ag["f", h].wait_recv()
    gw_term(2)
    gw_third(3)
    gw_third(1)
    gw_first(2)
    mix((2,), False, True)
    gw_second(2)
    gw_third(2)
    gw_done()
    for copy in sends:
        copy.wait_send()


def on_device(query, key_feat, values, conv_w, gain, w_out, cotangent):
    vm = pl.BlockSpec(memory_space=pltpu.VMEM)
    hbm = pl.BlockSpec(memory_space=pl.ANY)
    dma = pltpu.SemaphoreType.DMA
    vmem = pltpu.VMEM
    mixed, gq, gk, gv, gw = pl.pallas_call(
        kernel,
        out_shape=(
            jax.ShapeDtypeStruct((ROWS, FEAT), bf16),
            jax.ShapeDtypeStruct((HEADS * FD, ROWS), bf16),
            jax.ShapeDtypeStruct((HEADS * FD, ROWS), bf16),
            jax.ShapeDtypeStruct((ROWS, CH), bf16),
            jax.ShapeDtypeStruct((128, CH), bf16),
        ),
        in_specs=[vm] * 5 + [hbm] * 2,
        out_specs=(vm,) * 5,
        scratch_shapes=[
            vmem((16, CH), bf16),
            vmem((8, CH), f32),
            vmem((8, CH), f32),
            vmem((ROWS + 8, CH), f32),
            vmem((HEADS, 32, ROWS), f32),
            vmem((HEADS, 32, ROWS), f32),
            vmem((ROWS, CH), bf16),
            vmem((NB, HEADS, NF, DV), f32),
            vmem((ROWS, CH), f32),
            vmem((NB, HEADS, NF, DV), bf16),
            vmem((4, HEADS, ROWS, DV), bf16),
            vmem((4, FEAT, CH), bf16),
            vmem((ROWS, FEAT), bf16),
            vmem((FEAT, ROWS), bf16),
            vmem((ROWS, CH), bf16),
            vmem((ROWS, CH), bf16),
            vmem((ROWS, CH), bf16),
            vmem((512, CH), bf16),
            vmem((512, CH), bf16),
            vmem((ROWS, CH), bf16),
            vmem((ROWS, CH), bf16),
            vmem((2, 4, 4, 128, CH), bf16),
            vmem((4, 4, 128, CH), bf16),
            vmem((4, 4, 128, CH), bf16),
            vmem((4, 3, 4, 32, 256), bf16),
            vmem((4, 3, 128, 256), bf16),
            vmem((4, 4, 32, 256), bf16),
            vmem((4, 128, 256), bf16),
            vmem((4, 3, 32, 256), bf16),
            vmem((4, 3, 32, 256), bf16),
            vmem((4, 32, CH), bf16),
            vmem((ROWS, FEAT), f32),
            vmem((ROWS, CH), bf16),
            vmem((NB, HEADS, NF, DV), f32),
            vmem((NB, HEADS, NF, DV), bf16),
            vmem((HEADS * FD, ROWS), f32),
            vmem((7, 32, BLOCK), f32),
            dma((2,)),
            dma((4,)),
            dma((18,)),
            dma((18,)),
            dma((65,)),
            dma((65,)),
            dma((52,)),
            dma((52,)),
            dma((4,)),
            dma((4,)),
        ]
        + SCAN_SCRATCH * 2,
        compiler_params=pltpu.CompilerParams(
            collective_id=0, has_side_effects=True, vmem_limit_bytes=VMEM_LIMIT
        ),
        name="sublayer",
    )(query.T, key_feat.T, values, conv_w, gain.reshape(1, CH), w_out, cotangent)
    return mixed, gq.T, gk.T, gv, gw


def solution(mesh):
    both = P("seq", "head")
    return jax.shard_map(
        on_device,
        mesh=mesh,
        in_specs=(both, both, both, P(None, "head"), P("head"), P(None, "head"), both),
        out_specs=(both,) * 5,
        check_vma=False,
    )
```

```python
import functools

import jax
import jax.numpy as jnp
from jax import lax
from jax.experimental import pallas as pl
from jax.experimental.pallas import tpu as pltpu
from jax.sharding import PartitionSpec as P

f32 = jnp.float32
bf16 = jnp.bfloat16
FD = 16
BLOCK = 256
ROWS = 1024
HEADS = 4
NB = ROWS // BLOCK
DV = 128
CH = HEADS * DV
FEAT = 1024
NF = 160
EPSILON = 1e-05
VMEM_LIMIT = 60 * 1024 * 1024


def nn(a, b):
    return lax.dot_general(a, b, (((1,), (0,)), ((), ())), preferred_element_type=f32)


def nt(a, b):
    return lax.dot_general(a, b, (((1,), (1,)), ((), ())), preferred_element_type=f32)


def tn(a, b):
    return lax.dot_general(a, b, (((0,), (0,)), ((), ())), preferred_element_type=f32)


def place():
    s = lax.axis_index("seq")
    z = lax.axis_index("head")
    return s, z, s // 8, (s // 2) % 4, s % 2


def seq_of(x, y, c):
    return (x * 4 + y) * 2 + c


def remote(src, dst, send_sem, recv_sem, seq, head):
    copy = pltpu.make_async_remote_copy(
        src_ref=src,
        dst_ref=dst,
        send_sem=send_sem,
        recv_sem=recv_sem,
        device_id={"seq": seq, "head": head},
        device_id_type=pl.DeviceIdType.MESH,
    )
    copy.start()
    return copy


def greet(devices):
    barrier = pltpu.get_barrier_semaphore()
    for seq, head in devices:
        pl.semaphore_signal(
            barrier, inc=1, device_id={"seq": seq, "head": head}, device_id_type=pl.DeviceIdType.MESH
        )
    pl.semaphore_wait(barrier, len(devices))


def plane_peers(s, z, x, y, c):
    out = [(seq_of(x, y, 1 - c), z)]
    for j in (1, 2, 3):
        out.append((seq_of((x + j) % 4, y, c), z))
        out.append((seq_of(x, (y + j) % 4, c), z))
    return out


def spread(xt_ref, x2_ref):
    for h in range(HEADS):
        x = xt_ref[16 * h : 16 * h + 16, :].astype(f32)
        x2_ref[h, 0:16, :] = x
        x2_ref[h, 16:32, :] = x


def phi(x2_ref, h, cols):
    x = x2_ref[h, 0:16, cols]
    parts = [x * x]
    for d in range(1, 8):
        parts.append(x * x2_ref[h, d : d + 16, cols])
    parts.append(x[0:8] * x2_ref[h, 8:16, cols])
    parts.append((lax.broadcasted_iota(jnp.int32, (8, BLOCK), 0) == 0).astype(f32))
    parts.append(x)
    return jnp.concatenate(parts, axis=0).astype(bf16)


def phi_back(g, x2_ref, t2_ref, h, cols):
    x = x2_ref[h, 0:16, cols]
    acc = g[144:160] + 2.0 * g[0:16] * x
    for d in range(1, 8):
        gd = g[16 * d : 16 * d + 16]
        acc = acc + gd * x2_ref[h, d : d + 16, cols]
        t = gd * x
        t2_ref[d - 1, 0:16, :] = t
        t2_ref[d - 1, 16:32, :] = t
        acc = acc + t2_ref[d - 1, 16 - d : 32 - d, :]
    g8 = g[128:136]
    low = g8 * x2_ref[h, 8:16, cols]
    high = g8 * x[0:8]
    return acc + jnp.concatenate([low, high], axis=0)


def weights():
    r = lax.broadcasted_iota(jnp.int32, (NF, DV), 0)
    return jnp.where(
        r < 16, 1.0 / 32, jnp.where(r < 136, 1.0 / 16, jnp.where(r < 144, 1.0, 0.25))
    ).astype(f32)


def lower():
    r = lax.broadcasted_iota(jnp.int32, (BLOCK, BLOCK), 0)
    c = lax.broadcasted_iota(jnp.int32, (BLOCK, BLOCK), 1)
    return r >= c


SCAN_SCRATCH = [
    pltpu.VMEM((HEADS, NF, DV), f32),
    pltpu.VMEM((2, NF, DV), f32),
    pltpu.VMEM((2, NF, DV), bf16),
    pltpu.VMEM((3, 2, NF, DV), bf16),
    pltpu.VMEM((2, NF, DV), bf16),
    pltpu.VMEM((3, 2, NF, DV), bf16),
    pltpu.VMEM((2, NF, DV), f32),
    pltpu.VMEM((2, NF, DV), f32),
    pltpu.VMEM((2, NF, DV), f32),
    pltpu.VMEM((HEADS, NF, DV), f32),
    pltpu.SemaphoreType.DMA((8,)),
    pltpu.SemaphoreType.DMA((8,)),
]


def scan_steps(refs, forward):
    tot, ra, ys, yr, xs, xr, py, fs, fr, ent, ssem, rsem = refs
    s, z, x, y, c = place()
    sibling = seq_of(x, y, 1 - c)
    mine = pl.ds(2 * c, 2)
    copies = {}

    def counts(me, j):
        met = (me - j >= 0) if forward else (me - j < 0)
        return jnp.where(met, 1.0, 0.0).astype(f32)

    def pair():
        copies["a"] = remote(tot.at[pl.ds(2 * (1 - c), 2)], ra, ssem.at[0], rsem.at[0], sibling, z)

    def along_y():
        copies["a"].wait_recv()
        ys[...] = (tot[mine] + ra[...]).astype(bf16)
        for j in (1, 2, 3):
            copies["y", j] = remote(
                ys, yr.at[j - 1], ssem.at[j], rsem.at[j], seq_of(x, (y + j) % 4, c), z
            )

    def along_x():
        row = tot[mine] + ra[...]
        before = jnp.zeros((2, NF, DV), f32)
        for j in (1, 3, 2):
            copies["y", j].wait_recv()
            got = yr[j - 1].astype(f32)
            row = row + got
            before = before + got * counts(y, j)
        xs[...] = row.astype(bf16)
        py[...] = before
        for j in (1, 2, 3):
            copies["x", j] = remote(
                xs, xr.at[j - 1], ssem.at[3 + j], rsem.at[3 + j], seq_of((x + j) % 4, y, c), z
            )

    def back():
        before = py[...]
        for j in (1, 3, 2):
            copies["x", j].wait_recv()
            before = before + xr[j - 1].astype(f32) * counts(x, j)
        first = jnp.where(c == 0, 1.0, 0.0).astype(f32)
        other = first if forward else 1.0 - first
        fs[...] = before + tot[mine] * other
        ent[mine] = before + ra[...] * (1.0 - other)
        copies["f"] = remote(fs, fr, ssem.at[7], rsem.at[7], sibling, z)

    def done():
        copies["f"].wait_recv()
        ent[pl.ds(2 * (1 - c), 2)] = fr[...]
        for copy in copies.values():
            copy.wait_send()

    return pair, along_y, along_x, back, done


SLOT = {2: 0, 1: 1, 3: 2, 0: 3}
GROUPS = ((2,), (1, 3))
FILL = 256
REST = ROWS - FILL
HALF = REST // 2
UNITS = {
    "0": (0, (0, 1, 2, 3), 0, 256),
    "1": (1, (0, 1, 2, 3), 0, 256),
    "3": (3, (0, 1, 2, 3), 0, 256),
    "2a": (2, (0, 2), 0, 128),
    "2b": (2, (1, 3), 128, 128),
}


def row_block(n):
    return pl.ds(pl.multiple_of(n * BLOCK, BLOCK), BLOCK)


def kernel(
    qt_ref, kt_ref, cw_ref, gain_ref, v_hbm, w_hbm, cot_hbm,
    mixed_hbm, gq_hbm, gk_hbm, gv_hbm, gw_ref,
    halo, halo_back, edge_rows, wide, qx, kx, conv, st, hid, prev, oall,
    wt, cot, cott, opp, to_r, to_l, opp_l, opp_r, from_r, from_l, cf, gf,
    pool, r1, gsum, p1a, p1b, s2a, s2b, p2a, p2b, fin, macc,
    gh, bg, fw, dx, t2, vbuf, mixv, gqv, gkv,
    lsem, fsem, osem, hsem, zs, zr, ws, wr, gs, gr, ms, mr, *scans,
):
    s, z, x, y, c = place()
    right, left = (z + 1) % 4, (z + 3) % 4
    sibling = seq_of(x, y, 1 - c)
    after, before = (s + 1) % 32, (s + 31) % 32
    sends = []

    def go(*args):
        copy = remote(*args)
        sends.append(copy)
        return copy

    def load(src, dst, sem):
        copy = pltpu.make_async_copy(src, dst, sem)
        copy.start()
        return copy

    load_v = load(v_hbm, vbuf, lsem.at[2])
    load_cot = load(cot_hbm, cot, lsem.at[0])
    load_w = load(
        w_hbm.at[pl.ds(pl.multiple_of(z * FEAT, FEAT), FEAT)], wt.at[SLOT[0]], lsem.at[1]
    )

    barrier = pltpu.get_barrier_semaphore()

    def signal(seq, head):
        pl.semaphore_signal(
            barrier, inc=1, device_id={"seq": seq, "head": head}, device_id_type=pl.DeviceIdType.MESH
        )

    known = plane_peers(s, z, x, y, c) + [(s, (z + k) % 4) for k in (1, 2, 3)]
    known += [(after, z), (before, z)]
    known += [(seq_of(z, y, c), (z + k) % 4) for k in (1, 2, 3)]
    known += [(seq_of((x + j) % 4, y, c), x) for j in (1, 2, 3)]
    for seq, head in known:
        signal(seq, head)
    stays = x == z

    @pl.when(jnp.logical_not(stays))
    def _():
        signal(seq_of(z, y, c), z)
        signal(s, x)

    spread(kt_ref, kx)
    spread(qt_ref, qx)
    pl.semaphore_wait(barrier, len(known) + jnp.where(stays, 0, 2))

    row = c * 512 + x * 128 + y * 32
    wz = {}
    for k in (2, 1, 3):
        there = (z + k) % 4
        wz[k] = go(
            w_hbm.at[pl.ds(pl.multiple_of(there * FEAT + row, 32), 32)],
            wt.at[SLOT[4 - k], pl.ds(pl.multiple_of(row, 32), 32)],
            ws.at[k - 1],
            wr.at[k - 1],
            s,
            there,
        )
    edge = go(v_hbm.at[pl.ds(ROWS - 16, 16)], halo, hsem.at[0], hsem.at[1], after, z)

    cz = {}
    for i, (lo, up) in enumerate(((0, 0), (128, 128))):
        here = pl.ds(REST + lo, 128)
        cz["l", i] = go(
            cot_hbm.at[here], cf.at[2, pl.ds(lo, 128)], zs.at[18 + i], zr.at[18 + i], s, right
        )
        lo = 128 - lo
        here = pl.ds(REST + lo, 128)
        cz["r", i] = go(
            cot_hbm.at[here], cf.at[0, pl.ds(lo, 128)], zs.at[20 + i], zr.at[20 + i], s, left
        )
    others = []
    for k in (1, 2, 3):
        for t in range(8):
            at = pl.multiple_of((z + k) % 4 * FEAT + 128 * t, 128)
            others.append(
                load(
                    w_hbm.at[pl.ds(at, 128)],
                    pool.at[2 * (k - 1) + t // 4, t % 4],
                    fsem.at[8 * (k - 1) + t],
                )
            )

    def cot_on():
        cz["l", 0].wait_recv()
        a = pl.ds(0, 128)
        cz["f", 0] = go(cf.at[2, a], cf.at[1, a], zs.at[22], zr.at[22], s, right)
        cz["r", 0].wait_recv()
        b = pl.ds(128, 128)
        cz["f", 1] = go(cf.at[0, b], cf.at[1, b], zs.at[23], zr.at[23], s, left)

    def piece(group, px, py, half):
        at = pl.multiple_of(c * 512 + px * 128 + py * 32, 32)
        slots = pl.ds(0, 1) if group == 0 else pl.ds(1, 2)
        return wt.at[slots, pl.ds(at, 32), pl.ds(half * 256, 256)]

    w1, w2, w3 = {}, {}, {}

    def w_first(group):
        for k in GROUPS[group]:
            wz[4 - k].wait_recv()
        at = 3 + 31 * group
        for j in (1, 2, 3):
            own = piece(group, x, y, 0)
            i = at + j - 1
            w1[group, 0, j] = go(own, own, ws.at[i], wr.at[i], seq_of((x + j) % 4, y, c), z)
            own = piece(group, x, y, 1)
            i = at + j + 2
            w1[group, 1, j] = go(own, own, ws.at[i], wr.at[i], seq_of(x, (y + j) % 4, c), z)

    def w_second(group):
        at = 9 + 31 * group
        for i in (0, 1, 3, 2):
            for half in (0, 1):
                if i:
                    w1[group, half, i].wait_recv()
                if half == 0:
                    block = piece(group, (x - i + 4) % 4, y, 0)
                else:
                    block = piece(group, x, (y - i + 4) % 4, 1)
                for j in (1, 2, 3):
                    to = seq_of(x, (y + j) % 4, c) if half == 0 else seq_of((x + j) % 4, y, c)
                    w2[group, half, i, j] = go(block, block, ws.at[at], wr.at[at], to, z)
                    at += 1

    def w_third(group):
        for (which, *_), copy in w2.items():
            if which == group:
                copy.wait_recv()
        slots = pl.ds(0, 1) if group == 0 else pl.ds(1, 2)
        half = wt.at[slots, pl.ds(pl.multiple_of(c * 512, 512), 512)]
        i = 33 + 31 * group
        w3[group] = go(half, half, ws.at[i], wr.at[i], sibling, z)

    w_first(0)
    load_v.wait()
    wide[8 : 8 + ROWS, :] = vbuf[...].astype(f32)
    w_first(1)
    edge.wait_recv()
    inside = jnp.where(s > 0, 1.0, 0.0).astype(f32)
    wide[0:8, :] = halo[...].astype(f32)[8:16] * inside

    def convolve(n):
        at = 8 + n * BLOCK
        acc = cw_ref[0:1, :] * wide[at : at + BLOCK, :]
        for j in (1, 2):
            acc = acc + cw_ref[j : j + 1, :] * wide[at - j : at - j + BLOCK, :]
        conv[n * BLOCK : (n + 1) * BLOCK, :] = acc.astype(bf16)

    convolve(0)
    w_second(0)
    for n in (1, 2, 3):
        convolve(n)
    cot_on()
    w_second(1)
    load_cot.wait()

    def flip(b, carry):
        cott[:, row_block(b)] = jnp.transpose(cot[row_block(b), :], (1, 0))
        return carry

    lax.fori_loop(0, NB, flip, 0)
    w_third(0)

    scan_a, scan_b = scans[: len(scans) // 2], scans[len(scans) // 2 :]
    tot, ent = scan_a[0], scan_a[9]
    tot[...] = jnp.zeros_like(tot)

    def states(n, carry):
        rows = row_block(n)
        for h in range(HEADS):
            own = nn(phi(kx, h, rows), conv[rows, h * DV : (h + 1) * DV])
            st[n, h] = own
            tot[h] += own
        return carry

    lax.fori_loop(0, NB, states, 0)
    pair, along_y, along_x, back, done = scan_steps(scan_a, True)
    pair()

    def third(half, i):
        return pl.ds(pl.multiple_of(half * HALF + i * (HALF // 2), HALF // 2), HALF // 2)

    def fill(k, dst, half):
        def part(i, carry):
            rows = third(half, i)
            dst[rows, :] = nn(cot[rows, :], wt[SLOT[k]]).astype(bf16)
            return carry

        lax.fori_loop(0, 2, part, 0)

    half_a, half_b = pl.ds(0, HALF), pl.ds(HALF, HALF)
    rs = {}
    w3[0].wait_recv()
    fill(2, opp, 0)
    rs["or"] = go(opp.at[half_a], opp_l, zs.at[12], zr.at[12], s, right)
    fill(2, opp, 1)
    rs["ol"] = go(opp.at[half_b], opp_r, zs.at[13], zr.at[13], s, left)
    w_third(1)
    along_y()
    mask = lower()
    mask_t = jnp.logical_not(mask) | (
        lax.broadcasted_iota(jnp.int32, (BLOCK, BLOCK), 0)
        == lax.broadcasted_iota(jnp.int32, (BLOCK, BLOCK), 1)
    )

    def intra(n, carry):
        rows = row_block(n)
        for h in range(HEADS):
            entries = slice(16 * h, 16 * h + 16)
            sc = tn(qt_ref[entries, rows], kt_ref[entries, rows])
            att = jnp.where(mask, 1.0 + sc * (0.25 + sc * (1.0 / 32)), 0.0).astype(bf16)
            hid[rows, h * DV : (h + 1) * DV] = nn(att, conv[rows, h * DV : (h + 1) * DV])
        return carry

    lax.fori_loop(0, 2, intra, 0)
    w3[1].wait_recv()
    fill(1, to_r, 1)
    rs["dr"] = go(to_r.at[half_b], from_l.at[half_b], zs.at[14], zr.at[14], s, right)
    fill(3, to_l, 0)
    rs["dl"] = go(to_l.at[half_a], from_r.at[half_a], zs.at[15], zr.at[15], s, left)
    along_x()
    lax.fori_loop(2, 4, intra, 0)
    back()
    done()
    wts = weights()

    def finish(n, carry):
        rows = row_block(n)
        for h in range(HEADS):
            lanes = slice(h * DV, (h + 1) * DV)
            state = ent[h]
            ent[h] = state + st[n, h]
            before_block = (state * wts).astype(bf16)
            prev[n, h] = before_block
            hidden = hid[rows, lanes] + tn(phi(qx, h, rows), before_block)
            hid[rows, lanes] = hidden
            scale = lax.rsqrt(jnp.mean(hidden * hidden, axis=-1, keepdims=True) + EPSILON)
            oall[0, h, rows, :] = (hidden * scale * gain_ref[0:1, lanes]).astype(bf16)
        return carry

    lax.fori_loop(0, NB, finish, 0)

    load_w.wait()
    for copy in others:
        copy.wait()
    cz["l", 1].wait_recv()
    cz["r", 1].wait_recv()
    cz["f", 0].wait_recv()
    cz["f", 1].wait_recv()
    gf[...] = nn(cot[REST:ROWS, :], wt[SLOT[0]])
    for k in (1, 2, 3):
        for t in (0, 1):
            block = pool[2 * (k - 1) + t].reshape(512, CH)
            gf[...] += nn(cf[k - 1, :, 512 * t : 512 * t + 512], block)

    def add_in(k, dst, got, half):
        def part(i, carry):
            rows, here = third(half, i), third(0, i)
            term = nn(cot[rows, :], wt[SLOT[k]]) + got[here, :].astype(f32)
            dst[rows, :] = term.astype(bf16)
            return carry

        lax.fori_loop(0, 2, part, 0)

    rs["or"].wait_recv()
    add_in(1, to_r, opp_l, 0)
    rs["ar"] = go(to_r.at[half_a], from_l.at[half_a], zs.at[16], zr.at[16], s, right)
    rs["ol"].wait_recv()
    add_in(3, to_l, opp_r, 1)
    rs["al"] = go(to_l.at[half_b], from_r.at[half_b], zs.at[17], zr.at[17], s, left)

    ag = {}
    for h in range(HEADS):
        ag["l", h] = go(oall.at[0, h], oall.at[3, h], zs.at[h], zr.at[h], s, right)
        e = (h + 2) % 4
        ag["r", e] = go(oall.at[0, e], oall.at[1, e], zs.at[4 + e], zr.at[4 + e], s, left)

    def hand_on(h):
        ag["l", h].wait_recv()
        ag["f", h] = go(oall.at[3, h], oall.at[2, h], zs.at[8 + h], zr.at[8 + h], s, right)
        e = h + 2
        ag["r", e].wait_recv()
        ag["f", e] = go(oall.at[1, e], oall.at[2, e], zs.at[8 + e], zr.at[8 + e], s, left)

    def joined(k, rows, heads):
        return jnp.concatenate([oall[k, h, rows, :] for h in heads], axis=1)

    g1, g2, g3, g4 = {}, {}, {}, {}
    sem0 = {name: 16 * i for i, name in enumerate(UNITS)}

    def gw_term(u, split=False):
        k, heads, off, w = UNITS[u]
        cols = pl.ds(2 * off, 2 * w)
        i = sem0[u]

        def part(t, carry):
            term = nn(cott[row_block(t), :], joined(k, slice(None), heads)).astype(bf16)
            pool[k, t, :, cols] = term[0:128]
            pool[4 + k, t, :, cols] = term[128:256]
            return carry

        if split:
            g1[u] = []
            for t in range(4):
                part(t, 0)
                g1[u].append(
                    go(
                        pool.at[4 * (1 - c) + k, t, :, cols],
                        r1.at[k, t, :, cols], gs.at[i + t], gr.at[i + t], sibling, z,
                    )
                )
        else:
            lax.fori_loop(0, 4, part, 0)
            theirs = pool.at[4 * (1 - c) + k, :, :, cols]
            g1[u] = [go(theirs, r1.at[k, :, :, cols], gs.at[i], gr.at[i], sibling, z)]

    def gw_first(u):
        k, heads, off, w = UNITS[u]
        cols = slice(2 * off, 2 * off + 2 * w)
        for copy in g1[u]:
            copy.wait_recv()

        def part(t, carry):
            both = pool[4 * c + k, t, :, cols].astype(f32) + r1[k, t, :, cols].astype(f32)
            gsum[k, t, :, cols] = both.astype(bf16)
            return carry

        lax.fori_loop(0, 4, part, 0)
        for j in (2, 1, 3):
            nx, ny = (x + j) % 4, (y + j) % 4
            i = sem0[u] + 4 + j - 1
            rows = pl.ds(pl.multiple_of(nx * 32, 32), 32)
            g2[u, 0, j] = go(
                gsum.at[k, :, rows, pl.ds(2 * off, w)],
                p1a.at[k, j - 1, :, :, pl.ds(off, w)], gs.at[i], gr.at[i], seq_of(nx, y, c), z,
            )
            i += 3
            g2[u, 1, j] = go(
                gsum.at[k, ny, :, pl.ds(2 * off + w, w)],
                p1b.at[k, j - 1, :, pl.ds(off, w)], gs.at[i], gr.at[i], seq_of(x, ny, c), z,
            )

    my_rows = pl.ds(pl.multiple_of(x * 32, 32), 32)

    def gw_second(u):
        k, heads, off, w = UNITS[u]
        cols = slice(off, off + w)
        sum_a = gsum[k, :, my_rows, 2 * off : 2 * off + w].astype(f32)
        sum_b = gsum[k, y, :, 2 * off + w : 2 * off + 2 * w].astype(f32)
        for j in (1, 3, 2):
            g2[u, 0, j].wait_recv()
            sum_a = sum_a + p1a[k, j - 1, :, :, cols].astype(f32)
            g2[u, 1, j].wait_recv()
            sum_b = sum_b + p1b[k, j - 1, :, cols].astype(f32)
        s2a[k, :, :, cols] = sum_a.astype(bf16)
        s2b[k, :, cols] = sum_b.astype(bf16)
        for j in (2, 1, 3):
            nx, ny = (x + j) % 4, (y + j) % 4
            i = sem0[u] + 10 + j - 1
            rows = pl.ds(pl.multiple_of(nx * 32, 32), 32)
            here = pl.ds(off, w)
            g3[u, 0, j] = go(
                s2a.at[k, ny, :, here],
                p2a.at[k, j - 1, :, here], gs.at[i], gr.at[i], seq_of(x, ny, c), z,
            )
            i += 3
            g3[u, 1, j] = go(
                s2b.at[k, rows, here],
                p2b.at[k, j - 1, :, here], gs.at[i], gr.at[i], seq_of(nx, y, c), z,
            )

    def gw_third(u):
        k, heads, off, w = UNITS[u]
        cols = slice(off, off + w)
        sum_a = s2a[k, y, :, cols].astype(f32)
        sum_b = s2b[k, my_rows, cols].astype(f32)
        for j in (1, 3, 2):
            g3[u, 0, j].wait_recv()
            sum_a = sum_a + p2a[k, j - 1, :, cols].astype(f32)
            g3[u, 1, j].wait_recv()
            sum_b = sum_b + p2b[k, j - 1, :, cols].astype(f32)
        fin[k, :, cols] = sum_a.astype(bf16)
        fin[k, :, 256 + off : 256 + off + w] = sum_b.astype(bf16)

    def gw_move(k):
        def move():
            return pltpu.make_async_remote_copy(
                src_ref=fin.at[k],
                dst_ref=gw_ref.at[my_rows],
                send_sem=ms.at[k],
                recv_sem=mr.at[x],
                device_id={"seq": seq_of(z, y, c), "head": (z + k) % 4},
                device_id_type=pl.DeviceIdType.MESH,
            )

        if k:
            g4[k] = move
            move().start()
        else:

            @pl.when(stays)
            def _():
                gw_ref[my_rows, :] = fin[0]

            @pl.when(jnp.logical_not(stays))
            def _():
                move().start()
                move().wait_send()

    def gw_done():
        for k in (1, 2, 3):
            g4[k]().wait_send()
        for xs in range(4):

            @pl.when(jnp.logical_not(stays & (x == xs)))
            def _():
                pltpu.make_async_remote_copy(
                    src_ref=fin.at[0],
                    dst_ref=gw_ref.at[pl.ds(32 * xs, 32)],
                    send_sem=ms.at[0],
                    recv_sem=mr.at[xs],
                    device_id={"seq": seq_of(z, y, c), "head": (z + 1) % 4},
                    device_id_type=pl.DeviceIdType.MESH,
                ).wait_recv()

    out_copies = []

    def mix(parts, first, last):
        def part(b, carry):
            rows = row_block(b)
            for u in (0, 1):
                cols = slice(512 * u, 512 * u + 512)
                acc = None if first else macc[rows, cols]
                for k, heads in parts:
                    if len(heads) == HEADS:
                        rhs = wt[SLOT[k], cols, :]
                    else:
                        lanes = [slice(h * DV, (h + 1) * DV) for h in heads]
                        rhs = jnp.concatenate([wt[SLOT[k], cols, o] for o in lanes], axis=1)
                    term = nt(joined(k, rows, heads), rhs)
                    acc = term if acc is None else acc + term
                if last:
                    mixv[rows, cols] = acc.astype(bf16)
                else:
                    macc[rows, cols] = acc
            if last:
                pltpu.make_async_copy(mixv.at[rows], mixed_hbm.at[rows], osem.at[b]).start()
            return carry

        lax.fori_loop(0, NB, part, 0)
        if last:
            for b in range(NB):
                rows = pl.ds(b * BLOCK, BLOCK)
                out_copies.append(
                    pltpu.make_async_copy(mixv.at[rows], mixed_hbm.at[rows], osem.at[b])
                )

    every = (0, 1, 2, 3)
    gw_term("0")
    mix(((0, every),), True, False)
    gw_first("0")

    tot_b, ent_b = scan_b[0], scan_b[9]
    tot_b[...] = jnp.zeros_like(tot_b)

    def back_states(n, grad_out):
        rows = row_block(n)
        for h in range(HEADS):
            lanes = slice(h * DV, (h + 1) * DV)
            hidden = hid[rows, lanes]
            scale = lax.rsqrt(jnp.mean(hidden * hidden, axis=-1, keepdims=True) + EPSILON)
            normed = hidden * scale
            up = grad_out[:, lanes] * gain_ref[0:1, lanes]
            grad = scale * (up - normed * jnp.mean(up * normed, axis=-1, keepdims=True))
            grad = grad.astype(bf16)
            gh[rows, lanes] = grad
            own = nn(phi(qx, h, rows), grad)
            bg[n, h] = own
            tot_b[h] += own

    def back_rest(n, carry):
        rows = row_block(n)
        grad_out = nn(cot[rows, :], wt[SLOT[0]])
        grad_out = grad_out + from_r[rows, :].astype(f32) + from_l[rows, :].astype(f32)
        back_states(n, grad_out)
        return carry

    back_states(NB - 1, gf[...])
    for name in ("dr", "dl", "ar", "al"):
        rs[name].wait_recv()
    lax.fori_loop(0, NB - 1, back_rest, 0)
    pair, along_y, along_x, back, done = scan_steps(scan_b, False)

    def back_intra(n, carry):
        rows = row_block(n)
        for h in range(HEADS):
            lanes = slice(h * DV, (h + 1) * DV)
            entries = slice(16 * h, 16 * h + 16)
            qh = qt_ref[entries, rows]
            kh = kt_ref[entries, rows]
            g = gh[rows, lanes]
            v = conv[rows, lanes]
            sc = tn(kh, qh)
            ds = jnp.where(mask_t, nt(v, g) * (0.25 + sc * (1.0 / 16)), 0.0).astype(bf16)
            att = jnp.where(mask_t, 1.0 + sc * (0.25 + sc * (1.0 / 32)), 0.0).astype(bf16)
            wide[rows, lanes] = nn(att, g)
            across = phi_back(nt(prev[n, h], g), qx, t2, h, rows)
            gqv[entries, rows] = (nn(kh, ds) + across).astype(bf16)
            dx[entries, rows] = nt(qh, ds)
        return carry

    pair()
    lax.fori_loop(0, 1, back_intra, 0)
    along_y()
    hand_on(0)
    lax.fori_loop(1, 3, back_intra, 0)
    along_x()
    hand_on(1)
    lax.fori_loop(3, 4, back_intra, 0)
    back()
    gw_second("0")
    out_copies.append(load(gqv, gq_hbm, osem.at[4]))
    done()

    def suffix(t, carry):
        n = NB - 1 - t
        for h in range(HEADS):
            state = ent_b[h]
            ent_b[h] = state + bg[n, h]
            fw[n, h] = (state * wts).astype(bf16)
        return carry

    lax.fori_loop(0, NB, suffix, 0)

    def back_finish(n, carry):
        rows = row_block(n)
        for h in range(HEADS):
            lanes = slice(h * DV, (h + 1) * DV)
            entries = slice(16 * h, 16 * h + 16)
            wide[rows, lanes] += tn(phi(kx, h, rows), fw[n, h])
            across = phi_back(nt(fw[n, h], conv[rows, lanes]), kx, t2, h, rows)
            gkv[entries, rows] = (dx[entries, rows] + across).astype(bf16)
        return carry

    lax.fori_loop(0, 1, back_finish, 0)
    edge_rows[...] = wide[0:8, :]
    edge_back = go(edge_rows, halo_back, hsem.at[2], hsem.at[3], before, z)
    lax.fori_loop(1, NB, back_finish, 0)
    edge_back.wait_recv()
    inside = jnp.where(s < 31, 1.0, 0.0).astype(f32)
    wide[ROWS : ROWS + 8, :] = halo_back[...] * inside
    for n in range(NB):
        at = n * BLOCK
        acc = cw_ref[0:1, :] * wide[at : at + BLOCK, :]
        for j in (1, 2):
            acc = acc + cw_ref[j : j + 1, :] * wide[at + j : at + j + BLOCK, :]
        vbuf[at : at + BLOCK, :] = acc.astype(bf16)
    out_copies.append(load(gkv, gk_hbm, osem.at[5]))
    out_copies.append(load(vbuf, gv_hbm, osem.at[6]))

    gw_third("0")
    gw_move(0)
    ag["l", 2].wait_recv()
    ag["l", 3].wait_recv()
    gw_term("3")
    ag["r", 0].wait_recv()
    ag["r", 1].wait_recv()
    gw_term("1")
    gw_first("3")
    gw_first("1")
    mix(((1, every), (3, every)), False, False)
    gw_second("3")
    gw_second("1")
    ag["f", 0].wait_recv()
    ag["f", 2].wait_recv()
    gw_term("2a")
    mix(((2, (0, 2)),), False, False)
    gw_first("2a")
    gw_third("3")
    gw_move(3)
    gw_third("1")
    gw_move(1)
    ag["f", 1].wait_recv()
    ag["f", 3].wait_recv()
    gw_term("2b", True)
    gw_second("2a")
    gw_first("2b")
    mix(((2, (1, 3)),), False, True)
    gw_third("2a")
    gw_second("2b")
    gw_third("2b")
    gw_move(2)
    for copy in out_copies:
        copy.wait()
    gw_done()
    for copy in sends:
        copy.wait_send()


def hand_over_kernel(*refs):
    arrays, results, held, sem_in, sem_out = refs[:5], refs[5:10], refs[10:15], refs[15], refs[16]
    first, second = [], []
    for src, mid, dst in zip(arrays, held, results, strict=True):
        rows = max(src.shape[0] // 4, 32)
        for at in range(0, src.shape[0], rows):
            part = pl.ds(at, rows)
            i = len(first)
            first.append(pltpu.make_async_copy(src.at[part], mid.at[part], sem_in.at[i]))
            second.append(pltpu.make_async_copy(mid.at[part], dst.at[part], sem_out.at[i]))
    for copy in first:
        copy.start()
    for copy, onward in zip(first, second, strict=True):
        copy.wait()
        onward.start()
    for copy in second:
        copy.wait()


def hand_over(*arrays):
    hbm = pl.BlockSpec(memory_space=pl.ANY)
    return pl.pallas_call(
        hand_over_kernel,
        out_shape=tuple(jax.ShapeDtypeStruct(a.shape, a.dtype) for a in arrays),
        in_specs=[hbm] * 5,
        out_specs=(hbm,) * 5,
        scratch_shapes=[pltpu.VMEM(a.shape, a.dtype) for a in arrays]
        + [pltpu.SemaphoreType.DMA((20,))] * 2,
        compiler_params=pltpu.CompilerParams(vmem_limit_bytes=VMEM_LIMIT),
        name="hand_over",
    )(*arrays)


def on_device(query, key_feat, values, conv_w, gain, w_out, cotangent):
    vm = pl.BlockSpec(memory_space=pltpu.VMEM)
    hbm = pl.BlockSpec(memory_space=pl.ANY)
    dma = pltpu.SemaphoreType.DMA
    vmem = pltpu.VMEM
    mixed, gq, gk, gv, gw = pl.pallas_call(
        kernel,
        out_shape=(
            jax.ShapeDtypeStruct((ROWS, FEAT), bf16),
            jax.ShapeDtypeStruct((HEADS * FD, ROWS), bf16),
            jax.ShapeDtypeStruct((HEADS * FD, ROWS), bf16),
            jax.ShapeDtypeStruct((ROWS, CH), bf16),
            jax.ShapeDtypeStruct((128, CH), bf16),
        ),
        in_specs=[vm] * 4 + [hbm] * 3,
        out_specs=(hbm,) * 4 + (vm,),
        scratch_shapes=[
            vmem((16, CH), bf16),
            vmem((8, CH), f32),
            vmem((8, CH), f32),
            vmem((ROWS + 8, CH), f32),
            vmem((HEADS, 32, ROWS), f32),
            vmem((HEADS, 32, ROWS), f32),
            vmem((ROWS, CH), bf16),
            vmem((NB, HEADS, NF, DV), f32),
            vmem((ROWS, CH), f32),
            vmem((NB, HEADS, NF, DV), bf16),
            vmem((4, HEADS, ROWS, DV), bf16),
            vmem((4, FEAT, CH), bf16),
            vmem((ROWS, FEAT), bf16),
            vmem((FEAT, ROWS), bf16),
            vmem((REST, CH), bf16),
            vmem((REST, CH), bf16),
            vmem((REST, CH), bf16),
            vmem((HALF, CH), bf16),
            vmem((HALF, CH), bf16),
            vmem((REST, CH), bf16),
            vmem((REST, CH), bf16),
            vmem((3, FILL, FEAT), bf16),
            vmem((FILL, CH), f32),
            vmem((8, 4, 128, CH), bf16),
            vmem((4, 4, 128, CH), bf16),
            vmem((4, 4, 128, CH), bf16),
            vmem((4, 3, 4, 32, 256), bf16),
            vmem((4, 3, 128, 256), bf16),
            vmem((4, 4, 32, 256), bf16),
            vmem((4, 128, 256), bf16),
            vmem((4, 3, 32, 256), bf16),
            vmem((4, 3, 32, 256), bf16),
            vmem((4, 32, CH), bf16),
            vmem((ROWS, FEAT), f32),
            vmem((ROWS, CH), bf16),
            vmem((NB, HEADS, NF, DV), f32),
            vmem((NB, HEADS, NF, DV), bf16),
            vmem((HEADS * FD, ROWS), f32),
            vmem((7, 32, BLOCK), f32),
            vmem((ROWS, CH), bf16),
            vmem((ROWS, FEAT), bf16),
            vmem((HEADS * FD, ROWS), bf16),
            vmem((HEADS * FD, ROWS), bf16),
            dma((3,)),
            dma((24,)),
            dma((7,)),
            dma((4,)),
            dma((24,)),
            dma((24,)),
            dma((65,)),
            dma((65,)),
            dma((80,)),
            dma((80,)),
            dma((4,)),
            dma((4,)),
        ]
        + SCAN_SCRATCH * 2,
        compiler_params=pltpu.CompilerParams(
            collective_id=0, has_side_effects=True, vmem_limit_bytes=VMEM_LIMIT
        ),
        name="sublayer",
    )(query.T, key_feat.T, conv_w, gain.reshape(1, CH), values, w_out, cotangent)
    mixed, gq, gk, gv, gw = hand_over(mixed, gq, gk, gv, gw)
    return mixed, gq.T, gk.T, gv, gw


def solution(mesh):
    both = P("seq", "head")
    return jax.shard_map(
        on_device,
        mesh=mesh,
        in_specs=(both, both, both, P(None, "head"), P("head"), P(None, "head"), both),
        out_specs=(both,) * 5,
        check_vma=False,
    )
```

```python
import functools

import jax
import jax.numpy as jnp
from jax import lax
from jax.experimental import pallas as pl
from jax.experimental.pallas import tpu as pltpu
from jax.sharding import PartitionSpec as P

f32 = jnp.float32
bf16 = jnp.bfloat16
FD = 16
BLOCK = 256
ROWS = 1024
HEADS = 4
NB = ROWS // BLOCK
DV = 128
CH = HEADS * DV
FEAT = 1024
NF = 160
EPSILON = 1e-05
VMEM_LIMIT = 60 * 1024 * 1024


def nn(a, b):
    return lax.dot_general(a, b, (((1,), (0,)), ((), ())), preferred_element_type=f32)


def nt(a, b):
    return lax.dot_general(a, b, (((1,), (1,)), ((), ())), preferred_element_type=f32)


def tn(a, b):
    return lax.dot_general(a, b, (((0,), (0,)), ((), ())), preferred_element_type=f32)


def place():
    s = lax.axis_index("seq")
    z = lax.axis_index("head")
    return s, z, s // 8, (s // 2) % 4, s % 2


def seq_of(x, y, c):
    return (x * 4 + y) * 2 + c


def remote(src, dst, send_sem, recv_sem, seq, head):
    copy = pltpu.make_async_remote_copy(
        src_ref=src,
        dst_ref=dst,
        send_sem=send_sem,
        recv_sem=recv_sem,
        device_id={"seq": seq, "head": head},
        device_id_type=pl.DeviceIdType.MESH,
    )
    copy.start()
    return copy


def greet(devices):
    barrier = pltpu.get_barrier_semaphore()
    for seq, head in devices:
        pl.semaphore_signal(
            barrier, inc=1, device_id={"seq": seq, "head": head}, device_id_type=pl.DeviceIdType.MESH
        )
    pl.semaphore_wait(barrier, len(devices))


def plane_peers(s, z, x, y, c):
    out = [(seq_of(x, y, 1 - c), z)]
    for j in (1, 2, 3):
        out.append((seq_of((x + j) % 4, y, c), z))
        out.append((seq_of(x, (y + j) % 4, c), z))
    return out


def spread(xt_ref, x2_ref):
    for h in range(HEADS):
        x = xt_ref[16 * h : 16 * h + 16, :].astype(f32)
        x2_ref[h, 0:16, :] = x
        x2_ref[h, 16:32, :] = x


def phi(x2_ref, h, cols):
    x = x2_ref[h, 0:16, cols]
    parts = [x * x]
    for d in range(1, 8):
        parts.append(x * x2_ref[h, d : d + 16, cols])
    parts.append(x[0:8] * x2_ref[h, 8:16, cols])
    parts.append((lax.broadcasted_iota(jnp.int32, (8, BLOCK), 0) == 0).astype(f32))
    parts.append(x)
    return jnp.concatenate(parts, axis=0).astype(bf16)


def phi_back(g, x2_ref, t2_ref, h, cols):
    x = x2_ref[h, 0:16, cols]
    acc = g[144:160] + 2.0 * g[0:16] * x
    for d in range(1, 8):
        gd = g[16 * d : 16 * d + 16]
        acc = acc + gd * x2_ref[h, d : d + 16, cols]
        t = gd * x
        t2_ref[d - 1, 0:16, :] = t
        t2_ref[d - 1, 16:32, :] = t
        acc = acc + t2_ref[d - 1, 16 - d : 32 - d, :]
    g8 = g[128:136]
    low = g8 * x2_ref[h, 8:16, cols]
    high = g8 * x[0:8]
    return acc + jnp.concatenate([low, high], axis=0)


def weights():
    r = lax.broadcasted_iota(jnp.int32, (NF, DV), 0)
    return jnp.where(
        r < 16, 1.0 / 32, jnp.where(r < 136, 1.0 / 16, jnp.where(r < 144, 1.0, 0.25))
    ).astype(f32)


def lower():
    r = lax.broadcasted_iota(jnp.int32, (BLOCK, BLOCK), 0)
    c = lax.broadcasted_iota(jnp.int32, (BLOCK, BLOCK), 1)
    return r >= c


SCAN_SCRATCH = [
    pltpu.VMEM((HEADS, NF, DV), f32),
    pltpu.VMEM((2, NF, DV), f32),
    pltpu.VMEM((2, NF, DV), bf16),
    pltpu.VMEM((3, 2, NF, DV), bf16),
    pltpu.VMEM((2, NF, DV), bf16),
    pltpu.VMEM((3, 2, NF, DV), bf16),
    pltpu.VMEM((2, NF, DV), f32),
    pltpu.VMEM((2, NF, DV), f32),
    pltpu.VMEM((2, NF, DV), f32),
    pltpu.VMEM((HEADS, NF, DV), f32),
    pltpu.SemaphoreType.DMA((8,)),
    pltpu.SemaphoreType.DMA((8,)),
]


def scan_steps(refs, forward):
    tot, ra, ys, yr, xs, xr, py, fs, fr, ent, ssem, rsem = refs
    s, z, x, y, c = place()
    sibling = seq_of(x, y, 1 - c)
    mine = pl.ds(2 * c, 2)
    copies = {}

    def counts(me, j):
        met = (me - j >= 0) if forward else (me - j < 0)
        return jnp.where(met, 1.0, 0.0).astype(f32)

    def pair():
        copies["a"] = remote(tot.at[pl.ds(2 * (1 - c), 2)], ra, ssem.at[0], rsem.at[0], sibling, z)

    def along_y():
        copies["a"].wait_recv()
        ys[...] = (tot[mine] + ra[...]).astype(bf16)
        for j in (1, 2, 3):
            copies["y", j] = remote(
                ys, yr.at[j - 1], ssem.at[j], rsem.at[j], seq_of(x, (y + j) % 4, c), z
            )

    def along_x():
        row = tot[mine] + ra[...]
        before = jnp.zeros((2, NF, DV), f32)
        for j in (1, 3, 2):
            copies["y", j].wait_recv()
            got = yr[j - 1].astype(f32)
            row = row + got
            before = before + got * counts(y, j)
        xs[...] = row.astype(bf16)
        py[...] = before
        for j in (1, 2, 3):
            copies["x", j] = remote(
                xs, xr.at[j - 1], ssem.at[3 + j], rsem.at[3 + j], seq_of((x + j) % 4, y, c), z
            )

    def back():
        before = py[...]
        for j in (1, 3, 2):
            copies["x", j].wait_recv()
            before = before + xr[j - 1].astype(f32) * counts(x, j)
        first = jnp.where(c == 0, 1.0, 0.0).astype(f32)
        other = first if forward else 1.0 - first
        fs[...] = before + tot[mine] * other
        ent[mine] = before + ra[...] * (1.0 - other)
        copies["f"] = remote(fs, fr, ssem.at[7], rsem.at[7], sibling, z)

    def done():
        copies["f"].wait_recv()
        ent[pl.ds(2 * (1 - c), 2)] = fr[...]
        for copy in copies.values():
            copy.wait_send()

    return pair, along_y, along_x, back, done


SLOT = {2: 0, 1: 1, 3: 2, 0: 3}
GROUPS = ((2,), (1, 3))
FILL = 256
REST = ROWS - FILL
HALF = REST // 2
UNITS = {
    "0": (0, (0, 1, 2, 3), 0, 256),
    "1": (1, (0, 1, 2, 3), 0, 256),
    "3": (3, (0, 1, 2, 3), 0, 256),
    "2a": (2, (0, 2), 0, 128),
    "2b": (2, (1, 3), 128, 128),
}


def row_block(n):
    return pl.ds(pl.multiple_of(n * BLOCK, BLOCK), BLOCK)


def kernel(
    qt_ref, kt_ref, cw_ref, gain_ref, v_hbm, w_hbm, cot_hbm,
    mixed_hbm, gq_hbm, gk_hbm, gv_hbm, gw_ref,
    halo, halo_back, edge_rows, wide, qx, kx, conv, st, hid, prev, oall,
    wt, cot, cott, opp, to_r, to_l, opp_l, opp_r, from_r, from_l, cf, gf,
    pool, r1, gsum, p1a, p1b, s2a, s2b, p2a, p2b, fin, macc,
    gh, bg, fw, dx, t2, vbuf, mixv, gqv, gkv,
    lsem, fsem, osem, hsem, zs, zr, ws, wr, gs, gr, ms, mr, *scans,
):
    s, z, x, y, c = place()
    right, left = (z + 1) % 4, (z + 3) % 4
    sibling = seq_of(x, y, 1 - c)
    after, before = (s + 1) % 32, (s + 31) % 32
    sends = []

    def go(*args):
        copy = remote(*args)
        sends.append(copy)
        return copy

    def load(src, dst, sem):
        copy = pltpu.make_async_copy(src, dst, sem)
        copy.start()
        return copy

    load_v = load(v_hbm, vbuf, lsem.at[2])
    load_cot = load(cot_hbm, cot, lsem.at[0])
    load_w = load(
        w_hbm.at[pl.ds(pl.multiple_of(z * FEAT, FEAT), FEAT)], wt.at[SLOT[0]], lsem.at[1]
    )

    barrier = pltpu.get_barrier_semaphore()

    def signal(seq, head):
        pl.semaphore_signal(
            barrier, inc=1, device_id={"seq": seq, "head": head}, device_id_type=pl.DeviceIdType.MESH
        )

    known = plane_peers(s, z, x, y, c) + [(s, (z + k) % 4) for k in (1, 2, 3)]
    known += [(after, z), (before, z)]
    known += [(seq_of(z, y, c), (z + k) % 4) for k in (1, 2, 3)]
    known += [(seq_of((x + j) % 4, y, c), x) for j in (1, 2, 3)]
    for seq, head in known:
        signal(seq, head)
    stays = x == z

    @pl.when(jnp.logical_not(stays))
    def _():
        signal(seq_of(z, y, c), z)
        signal(s, x)

    spread(kt_ref, kx)
    spread(qt_ref, qx)
    pl.semaphore_wait(barrier, len(known) + jnp.where(stays, 0, 2))

    row = c * 512 + x * 128 + y * 32
    wz = {}
    for k in (2, 1, 3):
        there = (z + k) % 4
        wz[k] = go(
            w_hbm.at[pl.ds(pl.multiple_of(there * FEAT + row, 32), 32)],
            wt.at[SLOT[4 - k], pl.ds(pl.multiple_of(row, 32), 32)],
            ws.at[k - 1],
            wr.at[k - 1],
            s,
            there,
        )
    edge = go(v_hbm.at[pl.ds(ROWS - 16, 16)], halo, hsem.at[0], hsem.at[1], after, z)

    cz = {}
    for i, (lo, up) in enumerate(((0, 0), (128, 128))):
        here = pl.ds(REST + lo, 128)
        cz["l", i] = go(
            cot_hbm.at[here], cf.at[2, pl.ds(lo, 128)], zs.at[18 + i], zr.at[18 + i], s, right
        )
        lo = 128 - lo
        here = pl.ds(REST + lo, 128)
        cz["r", i] = go(
            cot_hbm.at[here], cf.at[0, pl.ds(lo, 128)], zs.at[20 + i], zr.at[20 + i], s, left
        )
    others = []
    for k in (1, 2, 3):
        for t in range(8):
            at = pl.multiple_of((z + k) % 4 * FEAT + 128 * t, 128)
            others.append(
                load(
                    w_hbm.at[pl.ds(at, 128)],
                    pool.at[2 * (k - 1) + t // 4, t % 4],
                    fsem.at[8 * (k - 1) + t],
                )
            )

    def cot_on():
        cz["l", 0].wait_recv()
        a = pl.ds(0, 128)
        cz["f", 0] = go(cf.at[2, a], cf.at[1, a], zs.at[22], zr.at[22], s, right)
        cz["r", 0].wait_recv()
        b = pl.ds(128, 128)
        cz["f", 1] = go(cf.at[0, b], cf.at[1, b], zs.at[23], zr.at[23], s, left)

    def piece(group, px, py, half):
        at = pl.multiple_of(c * 512 + px * 128 + py * 32, 32)
        slots = pl.ds(0, 1) if group == 0 else pl.ds(1, 2)
        return wt.at[slots, pl.ds(at, 32), pl.ds(half * 256, 256)]

    w1, w2, w3 = {}, {}, {}

    def w_first(group):
        for k in GROUPS[group]:
            wz[4 - k].wait_recv()
        at = 3 + 31 * group
        for j in (1, 2, 3):
            own = piece(group, x, y, 0)
            i = at + j - 1
            w1[group, 0, j] = go(own, own, ws.at[i], wr.at[i], seq_of((x + j) % 4, y, c), z)
            own = piece(group, x, y, 1)
            i = at + j + 2
            w1[group, 1, j] = go(own, own, ws.at[i], wr.at[i], seq_of(x, (y + j) % 4, c), z)

    def w_second(group):
        at = 9 + 31 * group
        for i in (0, 1, 3, 2):
            for half in (0, 1):
                if i:
                    w1[group, half, i].wait_recv()
                if half == 0:
                    block = piece(group, (x - i + 4) % 4, y, 0)
                else:
                    block = piece(group, x, (y - i + 4) % 4, 1)
                for j in (1, 2, 3):
                    to = seq_of(x, (y + j) % 4, c) if half == 0 else seq_of((x + j) % 4, y, c)
                    w2[group, half, i, j] = go(block, block, ws.at[at], wr.at[at], to, z)
                    at += 1

    def w_third(group):
        for (which, *_), copy in w2.items():
            if which == group:
                copy.wait_recv()
        slots = pl.ds(0, 1) if group == 0 else pl.ds(1, 2)
        half = wt.at[slots, pl.ds(pl.multiple_of(c * 512, 512), 512)]
        i = 33 + 31 * group
        w3[group] = go(half, half, ws.at[i], wr.at[i], sibling, z)

    w_first(0)
    load_v.wait()
    wide[8 : 8 + ROWS, :] = vbuf[...].astype(f32)
    w_first(1)
    edge.wait_recv()
    inside = jnp.where(s > 0, 1.0, 0.0).astype(f32)
    wide[0:8, :] = halo[...].astype(f32)[8:16] * inside

    def convolve(n):
        at = 8 + n * BLOCK
        acc = cw_ref[0:1, :] * wide[at : at + BLOCK, :]
        for j in (1, 2):
            acc = acc + cw_ref[j : j + 1, :] * wide[at - j : at - j + BLOCK, :]
        conv[n * BLOCK : (n + 1) * BLOCK, :] = acc.astype(bf16)

    convolve(0)
    w_second(0)
    for n in (1, 2, 3):
        convolve(n)
    cot_on()
    w_second(1)
    load_cot.wait()

    def flip(b, carry):
        cott[:, row_block(b)] = jnp.transpose(cot[row_block(b), :], (1, 0))
        return carry

    lax.fori_loop(0, NB, flip, 0)
    w_third(0)

    scan_a, scan_b = scans[: len(scans) // 2], scans[len(scans) // 2 :]
    tot, ent = scan_a[0], scan_a[9]
    tot[...] = jnp.zeros_like(tot)

    def states(n, carry):
        rows = row_block(n)
        for h in range(HEADS):
            own = nn(phi(kx, h, rows), conv[rows, h * DV : (h + 1) * DV])
            st[n, h] = own
            tot[h] += own
        return carry

    lax.fori_loop(0, NB, states, 0)
    pair, along_y, along_x, back, done = scan_steps(scan_a, True)
    pair()

    def third(half, i):
        return pl.ds(pl.multiple_of(half * HALF + i * (HALF // 2), HALF // 2), HALF // 2)

    def fill(k, dst, half):
        def part(i, carry):
            rows = third(half, i)
            dst[rows, :] = nn(cot[rows, :], wt[SLOT[k]]).astype(bf16)
            return carry

        lax.fori_loop(0, 2, part, 0)

    half_a, half_b = pl.ds(0, HALF), pl.ds(HALF, HALF)
    rs = {}
    w3[0].wait_recv()
    fill(2, opp, 0)
    rs["or"] = go(opp.at[half_a], opp_l, zs.at[12], zr.at[12], s, right)
    fill(2, opp, 1)
    rs["ol"] = go(opp.at[half_b], opp_r, zs.at[13], zr.at[13], s, left)
    w_third(1)
    along_y()
    mask = lower()
    mask_t = jnp.logical_not(mask) | (
        lax.broadcasted_iota(jnp.int32, (BLOCK, BLOCK), 0)
        == lax.broadcasted_iota(jnp.int32, (BLOCK, BLOCK), 1)
    )

    def intra(n, carry):
        rows = row_block(n)
        for h in range(HEADS):
            entries = slice(16 * h, 16 * h + 16)
            sc = tn(qt_ref[entries, rows], kt_ref[entries, rows])
            att = jnp.where(mask, 1.0 + sc * (0.25 + sc * (1.0 / 32)), 0.0).astype(bf16)
            hid[rows, h * DV : (h + 1) * DV] = nn(att, conv[rows, h * DV : (h + 1) * DV])
        return carry

    lax.fori_loop(0, 2, intra, 0)
    w3[1].wait_recv()
    fill(1, to_r, 1)
    rs["dr"] = go(to_r.at[half_b], from_l.at[half_b], zs.at[14], zr.at[14], s, right)
    fill(3, to_l, 0)
    rs["dl"] = go(to_l.at[half_a], from_r.at[half_a], zs.at[15], zr.at[15], s, left)
    along_x()
    lax.fori_loop(2, 4, intra, 0)
    back()
    done()
    wts = weights()

    def finish(n, carry):
        rows = row_block(n)
        for h in range(HEADS):
            lanes = slice(h * DV, (h + 1) * DV)
            state = ent[h]
            ent[h] = state + st[n, h]
            before_block = (state * wts).astype(bf16)
            prev[n, h] = before_block
            hidden = hid[rows, lanes] + tn(phi(qx, h, rows), before_block)
            hid[rows, lanes] = hidden
            scale = lax.rsqrt(jnp.mean(hidden * hidden, axis=-1, keepdims=True) + EPSILON)
            oall[0, h, rows, :] = (hidden * scale * gain_ref[0:1, lanes]).astype(bf16)
        return carry

    lax.fori_loop(0, NB, finish, 0)

    load_w.wait()
    for copy in others:
        copy.wait()
    cz["l", 1].wait_recv()
    cz["r", 1].wait_recv()
    cz["f", 0].wait_recv()
    cz["f", 1].wait_recv()
    gf[...] = nn(cot[REST:ROWS, :], wt[SLOT[0]])
    for k in (1, 2, 3):
        for t in (0, 1):
            block = pool[2 * (k - 1) + t].reshape(512, CH)
            gf[...] += nn(cf[k - 1, :, 512 * t : 512 * t + 512], block)

    def add_in(k, dst, got, half):
        def part(i, carry):
            rows, here = third(half, i), third(0, i)
            term = nn(cot[rows, :], wt[SLOT[k]]) + got[here, :].astype(f32)
            dst[rows, :] = term.astype(bf16)
            return carry

        lax.fori_loop(0, 2, part, 0)

    rs["or"].wait_recv()
    add_in(1, to_r, opp_l, 0)
    rs["ar"] = go(to_r.at[half_a], from_l.at[half_a], zs.at[16], zr.at[16], s, right)
    rs["ol"].wait_recv()
    add_in(3, to_l, opp_r, 1)
    rs["al"] = go(to_l.at[half_b], from_r.at[half_b], zs.at[17], zr.at[17], s, left)

    ag = {}
    for h in range(HEADS):
        ag["l", h] = go(oall.at[0, h], oall.at[3, h], zs.at[h], zr.at[h], s, right)
        e = (h + 2) % 4
        ag["r", e] = go(oall.at[0, e], oall.at[1, e], zs.at[4 + e], zr.at[4 + e], s, left)

    def hand_on(h):
        ag["l", h].wait_recv()
        ag["f", h] = go(oall.at[3, h], oall.at[2, h], zs.at[8 + h], zr.at[8 + h], s, right)
        e = h + 2
        ag["r", e].wait_recv()
        ag["f", e] = go(oall.at[1, e], oall.at[2, e], zs.at[8 + e], zr.at[8 + e], s, left)

    def joined(k, rows, heads):
        return jnp.concatenate([oall[k, h, rows, :] for h in heads], axis=1)

    g1, g2, g3, g4 = {}, {}, {}, {}
    sem0 = {name: 16 * i for i, name in enumerate(UNITS)}

    def gw_term(u, split=False):
        k, heads, off, w = UNITS[u]
        cols = pl.ds(2 * off, 2 * w)
        i = sem0[u]

        def part(t, carry):
            term = nn(cott[row_block(t), :], joined(k, slice(None), heads)).astype(bf16)
            pool[k, t, :, cols] = term[0:128]
            pool[4 + k, t, :, cols] = term[128:256]
            return carry

        if split:
            g1[u] = []
            for t in range(4):
                part(t, 0)
                g1[u].append(
                    go(
                        pool.at[4 * (1 - c) + k, t, :, cols],
                        r1.at[k, t, :, cols], gs.at[i + t], gr.at[i + t], sibling, z,
                    )
                )
        else:
            lax.fori_loop(0, 4, part, 0)
            theirs = pool.at[4 * (1 - c) + k, :, :, cols]
            g1[u] = [go(theirs, r1.at[k, :, :, cols], gs.at[i], gr.at[i], sibling, z)]

    def gw_first(u):
        k, heads, off, w = UNITS[u]
        cols = slice(2 * off, 2 * off + 2 * w)
        for copy in g1[u]:
            copy.wait_recv()

        def part(t, carry):
            both = pool[4 * c + k, t, :, cols].astype(f32) + r1[k, t, :, cols].astype(f32)
            gsum[k, t, :, cols] = both.astype(bf16)
            return carry

        lax.fori_loop(0, 4, part, 0)
        for j in (2, 1, 3):
            nx, ny = (x + j) % 4, (y + j) % 4
            i = sem0[u] + 4 + j - 1
            rows = pl.ds(pl.multiple_of(nx * 32, 32), 32)
            g2[u, 0, j] = go(
                gsum.at[k, :, rows, pl.ds(2 * off, w)],
                p1a.at[k, j - 1, :, :, pl.ds(off, w)], gs.at[i], gr.at[i], seq_of(nx, y, c), z,
            )
            i += 3
            g2[u, 1, j] = go(
                gsum.at[k, ny, :, pl.ds(2 * off + w, w)],
                p1b.at[k, j - 1, :, pl.ds(off, w)], gs.at[i], gr.at[i], seq_of(x, ny, c), z,
            )

    my_rows = pl.ds(pl.multiple_of(x * 32, 32), 32)

    def gw_second(u):
        k, heads, off, w = UNITS[u]
        cols = slice(off, off + w)
        sum_a = gsum[k, :, my_rows, 2 * off : 2 * off + w].astype(f32)
        sum_b = gsum[k, y, :, 2 * off + w : 2 * off + 2 * w].astype(f32)
        for j in (1, 3, 2):
            g2[u, 0, j].wait_recv()
            sum_a = sum_a + p1a[k, j - 1, :, :, cols].astype(f32)
            g2[u, 1, j].wait_recv()
            sum_b = sum_b + p1b[k, j - 1, :, cols].astype(f32)
        s2a[k, :, :, cols] = sum_a.astype(bf16)
        s2b[k, :, cols] = sum_b.astype(bf16)
        for j in (2, 1, 3):
            nx, ny = (x + j) % 4, (y + j) % 4
            i = sem0[u] + 10 + j - 1
            rows = pl.ds(pl.multiple_of(nx * 32, 32), 32)
            here = pl.ds(off, w)
            g3[u, 0, j] = go(
                s2a.at[k, ny, :, here],
                p2a.at[k, j - 1, :, here], gs.at[i], gr.at[i], seq_of(x, ny, c), z,
            )
            i += 3
            g3[u, 1, j] = go(
                s2b.at[k, rows, here],
                p2b.at[k, j - 1, :, here], gs.at[i], gr.at[i], seq_of(nx, y, c), z,
            )

    def gw_third(u):
        k, heads, off, w = UNITS[u]
        cols = slice(off, off + w)
        sum_a = s2a[k, y, :, cols].astype(f32)
        sum_b = s2b[k, my_rows, cols].astype(f32)
        for j in (1, 3, 2):
            g3[u, 0, j].wait_recv()
            sum_a = sum_a + p2a[k, j - 1, :, cols].astype(f32)
            g3[u, 1, j].wait_recv()
            sum_b = sum_b + p2b[k, j - 1, :, cols].astype(f32)
        fin[k, :, cols] = sum_a.astype(bf16)
        fin[k, :, 256 + off : 256 + off + w] = sum_b.astype(bf16)

    def gw_move(k):
        def move():
            return pltpu.make_async_remote_copy(
                src_ref=fin.at[k],
                dst_ref=gw_ref.at[my_rows],
                send_sem=ms.at[k],
                recv_sem=mr.at[x],
                device_id={"seq": seq_of(z, y, c), "head": (z + k) % 4},
                device_id_type=pl.DeviceIdType.MESH,
            )

        if k:
            g4[k] = move
            move().start()
        else:

            @pl.when(stays)
            def _():
                gw_ref[my_rows, :] = fin[0]

            @pl.when(jnp.logical_not(stays))
            def _():
                move().start()
                move().wait_send()

    def gw_done():
        for k in (1, 2, 3):
            g4[k]().wait_send()
        for xs in range(4):

            @pl.when(jnp.logical_not(stays & (x == xs)))
            def _():
                pltpu.make_async_remote_copy(
                    src_ref=fin.at[0],
                    dst_ref=gw_ref.at[pl.ds(32 * xs, 32)],
                    send_sem=ms.at[0],
                    recv_sem=mr.at[xs],
                    device_id={"seq": seq_of(z, y, c), "head": (z + 1) % 4},
                    device_id_type=pl.DeviceIdType.MESH,
                ).wait_recv()

    out_copies = []

    def mix(parts, first, last, lo=0, hi=NB):
        def part(b, carry):
            rows = row_block(b)
            for u in (0, 1):
                cols = slice(512 * u, 512 * u + 512)
                acc = None if first else macc[rows, cols]
                for k, heads in parts:
                    if len(heads) == HEADS:
                        rhs = wt[SLOT[k], cols, :]
                    else:
                        lanes = [slice(h * DV, (h + 1) * DV) for h in heads]
                        rhs = jnp.concatenate([wt[SLOT[k], cols, o] for o in lanes], axis=1)
                    term = nt(joined(k, rows, heads), rhs)
                    acc = term if acc is None else acc + term
                if last:
                    mixv[rows, cols] = acc.astype(bf16)
                else:
                    macc[rows, cols] = acc
            if last:
                pltpu.make_async_copy(mixv.at[rows], mixed_hbm.at[rows], osem.at[b]).start()
            return carry

        lax.fori_loop(lo, hi, part, 0)
        if last:
            for b in range(lo, hi):
                rows = pl.ds(b * BLOCK, BLOCK)
                out_copies.append(
                    pltpu.make_async_copy(mixv.at[rows], mixed_hbm.at[rows], osem.at[b])
                )

    every = (0, 1, 2, 3)
    gw_term("0")
    mix(((0, every),), True, False)
    gw_first("0")

    tot_b, ent_b = scan_b[0], scan_b[9]
    tot_b[...] = jnp.zeros_like(tot_b)

    def back_states(n, grad_out):
        rows = row_block(n)
        for h in range(HEADS):
            lanes = slice(h * DV, (h + 1) * DV)
            hidden = hid[rows, lanes]
            scale = lax.rsqrt(jnp.mean(hidden * hidden, axis=-1, keepdims=True) + EPSILON)
            normed = hidden * scale
            up = grad_out[:, lanes] * gain_ref[0:1, lanes]
            grad = scale * (up - normed * jnp.mean(up * normed, axis=-1, keepdims=True))
            grad = grad.astype(bf16)
            gh[rows, lanes] = grad
            own = nn(phi(qx, h, rows), grad)
            bg[n, h] = own
            tot_b[h] += own

    def back_rest(n, carry):
        rows = row_block(n)
        grad_out = nn(cot[rows, :], wt[SLOT[0]])
        grad_out = grad_out + from_r[rows, :].astype(f32) + from_l[rows, :].astype(f32)
        back_states(n, grad_out)
        return carry

    back_states(NB - 1, gf[...])
    for name in ("dr", "dl", "ar", "al"):
        rs[name].wait_recv()
    lax.fori_loop(0, NB - 1, back_rest, 0)
    pair, along_y, along_x, back, done = scan_steps(scan_b, False)

    def back_intra(n, carry):
        rows = row_block(n)
        for h in range(HEADS):
            lanes = slice(h * DV, (h + 1) * DV)
            entries = slice(16 * h, 16 * h + 16)
            qh = qt_ref[entries, rows]
            kh = kt_ref[entries, rows]
            g = gh[rows, lanes]
            v = conv[rows, lanes]
            sc = tn(kh, qh)
            ds = jnp.where(mask_t, nt(v, g) * (0.25 + sc * (1.0 / 16)), 0.0).astype(bf16)
            att = jnp.where(mask_t, 1.0 + sc * (0.25 + sc * (1.0 / 32)), 0.0).astype(bf16)
            wide[rows, lanes] = nn(att, g)
            across = phi_back(nt(prev[n, h], g), qx, t2, h, rows)
            gqv[entries, rows] = (nn(kh, ds) + across).astype(bf16)
            dx[entries, rows] = nt(qh, ds)
        return carry

    pair()
    lax.fori_loop(0, 1, back_intra, 0)
    along_y()
    hand_on(0)
    lax.fori_loop(1, 3, back_intra, 0)
    along_x()
    hand_on(1)
    lax.fori_loop(3, 4, back_intra, 0)
    back()
    gw_second("0")
    out_copies.append(load(gqv, gq_hbm, osem.at[4]))
    done()

    def suffix(t, carry):
        n = NB - 1 - t
        for h in range(HEADS):
            state = ent_b[h]
            ent_b[h] = state + bg[n, h]
            fw[n, h] = (state * wts).astype(bf16)
        return carry

    lax.fori_loop(0, NB, suffix, 0)

    def back_finish(n, carry):
        rows = row_block(n)
        for h in range(HEADS):
            lanes = slice(h * DV, (h + 1) * DV)
            entries = slice(16 * h, 16 * h + 16)
            wide[rows, lanes] += tn(phi(kx, h, rows), fw[n, h])
            across = phi_back(nt(fw[n, h], conv[rows, lanes]), kx, t2, h, rows)
            gkv[entries, rows] = (dx[entries, rows] + across).astype(bf16)
        return carry

    lax.fori_loop(0, 1, back_finish, 0)
    edge_rows[...] = wide[0:8, :]
    edge_back = go(edge_rows, halo_back, hsem.at[2], hsem.at[3], before, z)
    lax.fori_loop(1, NB, back_finish, 0)
    edge_back.wait_recv()
    inside = jnp.where(s < 31, 1.0, 0.0).astype(f32)
    wide[ROWS : ROWS + 8, :] = halo_back[...] * inside
    for n in range(NB):
        at = n * BLOCK
        acc = cw_ref[0:1, :] * wide[at : at + BLOCK, :]
        for j in (1, 2):
            acc = acc + cw_ref[j : j + 1, :] * wide[at + j : at + j + BLOCK, :]
        vbuf[at : at + BLOCK, :] = acc.astype(bf16)
    out_copies.append(load(gkv, gk_hbm, osem.at[5]))
    out_copies.append(load(vbuf, gv_hbm, osem.at[6]))

    gw_third("0")
    gw_move(0)
    ag["l", 2].wait_recv()
    ag["l", 3].wait_recv()
    gw_term("3")
    ag["r", 0].wait_recv()
    ag["r", 1].wait_recv()
    gw_term("1")
    gw_first("3")
    gw_first("1")
    ag["f", 0].wait_recv()
    ag["f", 2].wait_recv()
    gw_term("2a")
    mix(((1, every), (3, every)), False, False)
    gw_second("3")
    gw_second("1")
    gw_first("2a")
    ag["f", 1].wait_recv()
    ag["f", 3].wait_recv()
    gw_term("2b", True)
    mix(((2, every),), False, True, 0, 2)
    gw_first("2b")
    mix(((2, every),), False, True, 2, 4)
    gw_second("2a")
    gw_third("3")
    gw_move(3)
    gw_third("1")
    gw_move(1)
    gw_second("2b")
    gw_third("2a")
    gw_third("2b")
    gw_move(2)
    for copy in out_copies:
        copy.wait()
    gw_done()
    for copy in sends:
        copy.wait_send()


def hand_over_kernel(*refs):
    arrays, results, held, sem_in, sem_out = refs[:5], refs[5:10], refs[10:15], refs[15], refs[16]
    first, second = [], []
    for src, mid, dst in zip(arrays, held, results, strict=True):
        rows = max(src.shape[0] // 4, 32)
        for at in range(0, src.shape[0], rows):
            part = pl.ds(at, rows)
            i = len(first)
            first.append(pltpu.make_async_copy(src.at[part], mid.at[part], sem_in.at[i]))
            second.append(pltpu.make_async_copy(mid.at[part], dst.at[part], sem_out.at[i]))
    for copy in first:
        copy.start()
    for copy, onward in zip(first, second, strict=True):
        copy.wait()
        onward.start()
    for copy in second:
        copy.wait()


def hand_over(*arrays):
    hbm = pl.BlockSpec(memory_space=pl.ANY)
    return pl.pallas_call(
        hand_over_kernel,
        out_shape=tuple(jax.ShapeDtypeStruct(a.shape, a.dtype) for a in arrays),
        in_specs=[hbm] * 5,
        out_specs=(hbm,) * 5,
        scratch_shapes=[pltpu.VMEM(a.shape, a.dtype) for a in arrays]
        + [pltpu.SemaphoreType.DMA((20,))] * 2,
        compiler_params=pltpu.CompilerParams(vmem_limit_bytes=VMEM_LIMIT),
        name="hand_over",
    )(*arrays)


def on_device(query, key_feat, values, conv_w, gain, w_out, cotangent):
    vm = pl.BlockSpec(memory_space=pltpu.VMEM)
    hbm = pl.BlockSpec(memory_space=pl.ANY)
    dma = pltpu.SemaphoreType.DMA
    vmem = pltpu.VMEM
    mixed, gq, gk, gv, gw = pl.pallas_call(
        kernel,
        out_shape=(
            jax.ShapeDtypeStruct((ROWS, FEAT), bf16),
            jax.ShapeDtypeStruct((HEADS * FD, ROWS), bf16),
            jax.ShapeDtypeStruct((HEADS * FD, ROWS), bf16),
            jax.ShapeDtypeStruct((ROWS, CH), bf16),
            jax.ShapeDtypeStruct((128, CH), bf16),
        ),
        in_specs=[vm] * 4 + [hbm] * 3,
        out_specs=(hbm,) * 4 + (vm,),
        scratch_shapes=[
            vmem((16, CH), bf16),
            vmem((8, CH), f32),
            vmem((8, CH), f32),
            vmem((ROWS + 8, CH), f32),
            vmem((HEADS, 32, ROWS), f32),
            vmem((HEADS, 32, ROWS), f32),
            vmem((ROWS, CH), bf16),
            vmem((NB, HEADS, NF, DV), f32),
            vmem((ROWS, CH), f32),
            vmem((NB, HEADS, NF, DV), bf16),
            vmem((4, HEADS, ROWS, DV), bf16),
            vmem((4, FEAT, CH), bf16),
            vmem((ROWS, FEAT), bf16),
            vmem((FEAT, ROWS), bf16),
            vmem((REST, CH), bf16),
            vmem((REST, CH), bf16),
            vmem((REST, CH), bf16),
            vmem((HALF, CH), bf16),
            vmem((HALF, CH), bf16),
            vmem((REST, CH), bf16),
            vmem((REST, CH), bf16),
            vmem((3, FILL, FEAT), bf16),
            vmem((FILL, CH), f32),
            vmem((8, 4, 128, CH), bf16),
            vmem((4, 4, 128, CH), bf16),
            vmem((4, 4, 128, CH), bf16),
            vmem((4, 3, 4, 32, 256), bf16),
            vmem((4, 3, 128, 256), bf16),
            vmem((4, 4, 32, 256), bf16),
            vmem((4, 128, 256), bf16),
            vmem((4, 3, 32, 256), bf16),
            vmem((4, 3, 32, 256), bf16),
            vmem((4, 32, CH), bf16),
            vmem((ROWS, FEAT), f32),
            vmem((ROWS, CH), bf16),
            vmem((NB, HEADS, NF, DV), f32),
            vmem((NB, HEADS, NF, DV), bf16),
            vmem((HEADS * FD, ROWS), f32),
            vmem((7, 32, BLOCK), f32),
            vmem((ROWS, CH), bf16),
            vmem((ROWS, FEAT), bf16),
            vmem((HEADS * FD, ROWS), bf16),
            vmem((HEADS * FD, ROWS), bf16),
            dma((3,)),
            dma((24,)),
            dma((7,)),
            dma((4,)),
            dma((24,)),
            dma((24,)),
            dma((65,)),
            dma((65,)),
            dma((80,)),
            dma((80,)),
            dma((4,)),
            dma((4,)),
        ]
        + SCAN_SCRATCH * 2,
        compiler_params=pltpu.CompilerParams(
            collective_id=0, has_side_effects=True, vmem_limit_bytes=VMEM_LIMIT
        ),
        name="sublayer",
    )(query.T, key_feat.T, conv_w, gain.reshape(1, CH), values, w_out, cotangent)
    mixed, gq, gk, gv, gw = hand_over(mixed, gq, gk, gv, gw)
    return mixed, gq.T, gk.T, gv, gw


def solution(mesh):
    both = P("seq", "head")
    return jax.shard_map(
        on_device,
        mesh=mesh,
        in_specs=(both, both, both, P(None, "head"), P("head"), P(None, "head"), both),
        out_specs=(both,) * 5,
        check_vma=False,
    )
```

```python
import functools

import jax
import jax.numpy as jnp
from jax import lax
from jax.experimental import pallas as pl
from jax.experimental.pallas import tpu as pltpu
from jax.sharding import PartitionSpec as P

f32 = jnp.float32
bf16 = jnp.bfloat16
FD = 16
BLOCK = 256
ROWS = 1024
HEADS = 4
NB = ROWS // BLOCK
DV = 128
CH = HEADS * DV
FEAT = 1024
NF = 160
EPSILON = 1e-05
VMEM_LIMIT = 60 * 1024 * 1024


def nn(a, b):
    return lax.dot_general(a, b, (((1,), (0,)), ((), ())), preferred_element_type=f32)


def nt(a, b):
    return lax.dot_general(a, b, (((1,), (1,)), ((), ())), preferred_element_type=f32)


def tn(a, b):
    return lax.dot_general(a, b, (((0,), (0,)), ((), ())), preferred_element_type=f32)


def place():
    s = lax.axis_index("seq")
    z = lax.axis_index("head")
    return s, z, s // 8, (s // 2) % 4, s % 2


def seq_of(x, y, c):
    return (x * 4 + y) * 2 + c


def remote(src, dst, send_sem, recv_sem, seq, head):
    copy = pltpu.make_async_remote_copy(
        src_ref=src,
        dst_ref=dst,
        send_sem=send_sem,
        recv_sem=recv_sem,
        device_id={"seq": seq, "head": head},
        device_id_type=pl.DeviceIdType.MESH,
    )
    copy.start()
    return copy


def greet(devices):
    barrier = pltpu.get_barrier_semaphore()
    for seq, head in devices:
        pl.semaphore_signal(
            barrier, inc=1, device_id={"seq": seq, "head": head}, device_id_type=pl.DeviceIdType.MESH
        )
    pl.semaphore_wait(barrier, len(devices))


def plane_peers(s, z, x, y, c):
    out = [(seq_of(x, y, 1 - c), z)]
    for j in (1, 2, 3):
        out.append((seq_of((x + j) % 4, y, c), z))
        out.append((seq_of(x, (y + j) % 4, c), z))
    return out


def spread(xt_ref, x2_ref):
    for h in range(HEADS):
        x = xt_ref[16 * h : 16 * h + 16, :].astype(f32)
        x2_ref[h, 0:16, :] = x
        x2_ref[h, 16:32, :] = x


def phi(x2_ref, h, cols):
    x = x2_ref[h, 0:16, cols]
    parts = [x * x]
    for d in range(1, 8):
        parts.append(x * x2_ref[h, d : d + 16, cols])
    parts.append(x[0:8] * x2_ref[h, 8:16, cols])
    parts.append((lax.broadcasted_iota(jnp.int32, (8, BLOCK), 0) == 0).astype(f32))
    parts.append(x)
    return jnp.concatenate(parts, axis=0).astype(bf16)


def phi_back(g, x2_ref, t2_ref, h, cols):
    x = x2_ref[h, 0:16, cols]
    acc = g[144:160] + 2.0 * g[0:16] * x
    for d in range(1, 8):
        gd = g[16 * d : 16 * d + 16]
        acc = acc + gd * x2_ref[h, d : d + 16, cols]
        t = gd * x
        t2_ref[d - 1, 0:16, :] = t
        t2_ref[d - 1, 16:32, :] = t
        acc = acc + t2_ref[d - 1, 16 - d : 32 - d, :]
    g8 = g[128:136]
    low = g8 * x2_ref[h, 8:16, cols]
    high = g8 * x[0:8]
    return acc + jnp.concatenate([low, high], axis=0)


def weights():
    r = lax.broadcasted_iota(jnp.int32, (NF, DV), 0)
    return jnp.where(
        r < 16, 1.0 / 32, jnp.where(r < 136, 1.0 / 16, jnp.where(r < 144, 1.0, 0.25))
    ).astype(f32)


def lower():
    r = lax.broadcasted_iota(jnp.int32, (BLOCK, BLOCK), 0)
    c = lax.broadcasted_iota(jnp.int32, (BLOCK, BLOCK), 1)
    return r >= c


SCAN_SCRATCH = [
    pltpu.VMEM((HEADS, NF, DV), f32),
    pltpu.VMEM((2, NF, DV), f32),
    pltpu.VMEM((2, NF, DV), bf16),
    pltpu.VMEM((3, 2, NF, DV), bf16),
    pltpu.VMEM((2, NF, DV), bf16),
    pltpu.VMEM((3, 2, NF, DV), bf16),
    pltpu.VMEM((2, NF, DV), f32),
    pltpu.VMEM((2, NF, DV), f32),
    pltpu.VMEM((2, NF, DV), f32),
    pltpu.VMEM((HEADS, NF, DV), f32),
    pltpu.SemaphoreType.DMA((8,)),
    pltpu.SemaphoreType.DMA((8,)),
]


def scan_steps(refs, forward):
    tot, ra, ys, yr, xs, xr, py, fs, fr, ent, ssem, rsem = refs
    s, z, x, y, c = place()
    sibling = seq_of(x, y, 1 - c)
    mine = pl.ds(2 * c, 2)
    copies = {}

    def counts(me, j):
        met = (me - j >= 0) if forward else (me - j < 0)
        return jnp.where(met, 1.0, 0.0).astype(f32)

    def pair():
        copies["a"] = remote(tot.at[pl.ds(2 * (1 - c), 2)], ra, ssem.at[0], rsem.at[0], sibling, z)

    def along_y():
        copies["a"].wait_recv()
        ys[...] = (tot[mine] + ra[...]).astype(bf16)
        for j in (1, 2, 3):
            copies["y", j] = remote(
                ys, yr.at[j - 1], ssem.at[j], rsem.at[j], seq_of(x, (y + j) % 4, c), z
            )

    def along_x():
        row = tot[mine] + ra[...]
        before = jnp.zeros((2, NF, DV), f32)
        for j in (1, 3, 2):
            copies["y", j].wait_recv()
            got = yr[j - 1].astype(f32)
            row = row + got
            before = before + got * counts(y, j)
        xs[...] = row.astype(bf16)
        py[...] = before
        for j in (1, 2, 3):
            copies["x", j] = remote(
                xs, xr.at[j - 1], ssem.at[3 + j], rsem.at[3 + j], seq_of((x + j) % 4, y, c), z
            )

    def back():
        before = py[...]
        for j in (1, 3, 2):
            copies["x", j].wait_recv()
            before = before + xr[j - 1].astype(f32) * counts(x, j)
        first = jnp.where(c == 0, 1.0, 0.0).astype(f32)
        other = first if forward else 1.0 - first
        fs[...] = before + tot[mine] * other
        ent[mine] = before + ra[...] * (1.0 - other)
        copies["f"] = remote(fs, fr, ssem.at[7], rsem.at[7], sibling, z)

    def done():
        copies["f"].wait_recv()
        ent[pl.ds(2 * (1 - c), 2)] = fr[...]
        for copy in copies.values():
            copy.wait_send()

    return pair, along_y, along_x, back, done


SLOT = {2: 0, 1: 1, 3: 2, 0: 3}
GROUPS = ((2,), (1, 3))
FILL = 256
REST = ROWS - FILL
HALF = REST // 2
UNITS = {
    "0": (0, (0, 1, 2, 3), 0, 256),
    "1": (1, (0, 1, 2, 3), 0, 256),
    "3": (3, (0, 1, 2, 3), 0, 256),
    "2a": (2, (0, 2), 0, 128),
    "2b": (2, (1, 3), 128, 128),
}


def row_block(n):
    return pl.ds(pl.multiple_of(n * BLOCK, BLOCK), BLOCK)


def kernel(
    qt_hbm, kt_hbm, cw_hbm, gain_hbm, v_hbm, w_hbm, cot_hbm,
    mixed_hbm, gq_hbm, gk_hbm, gv_hbm, gw_hbm,
    halo, halo_back, edge_rows, wide, qx, kx, conv, st, hid, prev, oall,
    wt, cot, cott, opp, to_r, to_l, opp_l, opp_r, from_r, from_l, cf, gf,
    pool, r1, gsum, p1a, p1b, s2a, s2b, p2a, p2b, fin, macc,
    gh, bg, fw, dx, t2, vbuf, mixv, gqv, gkv, qt_ref, kt_ref, cw_ref, gain_ref,
    lsem, fsem, osem, hsem, zs, zr, ws, wr, gs, gr, ms, mr, *scans,
):
    s, z, x, y, c = place()
    right, left = (z + 1) % 4, (z + 3) % 4
    sibling = seq_of(x, y, 1 - c)
    after, before = (s + 1) % 32, (s + 31) % 32
    sends = []

    def go(*args):
        copy = remote(*args)
        sends.append(copy)
        return copy

    def load(src, dst, sem):
        copy = pltpu.make_async_copy(src, dst, sem)
        copy.start()
        return copy

    small = [
        load(src, dst, lsem.at[3 + i])
        for i, (src, dst) in enumerate(
            ((kt_hbm, kt_ref), (qt_hbm, qt_ref), (cw_hbm, cw_ref), (gain_hbm, gain_ref))
        )
    ]
    load_v = load(v_hbm, vbuf, lsem.at[2])
    load_cot = load(cot_hbm, cot, lsem.at[0])
    load_w = load(
        w_hbm.at[pl.ds(pl.multiple_of(z * FEAT, FEAT), FEAT)], wt.at[SLOT[0]], lsem.at[1]
    )

    barrier = pltpu.get_barrier_semaphore()

    def signal(seq, head):
        pl.semaphore_signal(
            barrier, inc=1, device_id={"seq": seq, "head": head}, device_id_type=pl.DeviceIdType.MESH
        )

    known = plane_peers(s, z, x, y, c) + [(s, (z + k) % 4) for k in (1, 2, 3)]
    known += [(after, z), (before, z)]
    known += [(seq_of(z, y, c), (z + k) % 4) for k in (1, 2, 3)]
    known += [(seq_of((x + j) % 4, y, c), x) for j in (1, 2, 3)]
    for seq, head in known:
        signal(seq, head)
    stays = x == z

    @pl.when(jnp.logical_not(stays))
    def _():
        signal(seq_of(z, y, c), z)
        signal(s, x)

    for copy in small:
        copy.wait()
    spread(kt_ref, kx)
    spread(qt_ref, qx)
    pl.semaphore_wait(barrier, len(known) + jnp.where(stays, 0, 2))

    row = c * 512 + x * 128 + y * 32
    wz = {}
    for k in (2, 1, 3):
        there = (z + k) % 4
        wz[k] = go(
            w_hbm.at[pl.ds(pl.multiple_of(there * FEAT + row, 32), 32)],
            wt.at[SLOT[4 - k], pl.ds(pl.multiple_of(row, 32), 32)],
            ws.at[k - 1],
            wr.at[k - 1],
            s,
            there,
        )
    edge = go(v_hbm.at[pl.ds(ROWS - 16, 16)], halo, hsem.at[0], hsem.at[1], after, z)

    cz = {}
    for i, (lo, up) in enumerate(((0, 0), (128, 128))):
        here = pl.ds(REST + lo, 128)
        cz["l", i] = go(
            cot_hbm.at[here], cf.at[2, pl.ds(lo, 128)], zs.at[18 + i], zr.at[18 + i], s, right
        )
        lo = 128 - lo
        here = pl.ds(REST + lo, 128)
        cz["r", i] = go(
            cot_hbm.at[here], cf.at[0, pl.ds(lo, 128)], zs.at[20 + i], zr.at[20 + i], s, left
        )
    others = []
    for k in (1, 2, 3):
        for t in range(8):
            at = pl.multiple_of((z + k) % 4 * FEAT + 128 * t, 128)
            others.append(
                load(
                    w_hbm.at[pl.ds(at, 128)],
                    pool.at[2 * (k - 1) + t // 4, t % 4],
                    fsem.at[8 * (k - 1) + t],
                )
            )

    def cot_on():
        cz["l", 0].wait_recv()
        a = pl.ds(0, 128)
        cz["f", 0] = go(cf.at[2, a], cf.at[1, a], zs.at[22], zr.at[22], s, right)
        cz["r", 0].wait_recv()
        b = pl.ds(128, 128)
        cz["f", 1] = go(cf.at[0, b], cf.at[1, b], zs.at[23], zr.at[23], s, left)

    def piece(group, px, py, half):
        at = pl.multiple_of(c * 512 + px * 128 + py * 32, 32)
        slots = pl.ds(0, 1) if group == 0 else pl.ds(1, 2)
        return wt.at[slots, pl.ds(at, 32), pl.ds(half * 256, 256)]

    w1, w2, w3 = {}, {}, {}

    def w_first(group):
        for k in GROUPS[group]:
            wz[4 - k].wait_recv()
        at = 3 + 31 * group
        for j in (1, 2, 3):
            own = piece(group, x, y, 0)
            i = at + j - 1
            w1[group, 0, j] = go(own, own, ws.at[i], wr.at[i], seq_of((x + j) % 4, y, c), z)
            own = piece(group, x, y, 1)
            i = at + j + 2
            w1[group, 1, j] = go(own, own, ws.at[i], wr.at[i], seq_of(x, (y + j) % 4, c), z)

    def w_second(group):
        at = 9 + 31 * group
        for i in (0, 1, 3, 2):
            for half in (0, 1):
                if i:
                    w1[group, half, i].wait_recv()
                if half == 0:
                    block = piece(group, (x - i + 4) % 4, y, 0)
                else:
                    block = piece(group, x, (y - i + 4) % 4, 1)
                for j in (1, 2, 3):
                    to = seq_of(x, (y + j) % 4, c) if half == 0 else seq_of((x + j) % 4, y, c)
                    w2[group, half, i, j] = go(block, block, ws.at[at], wr.at[at], to, z)
                    at += 1

    def w_third(group):
        for (which, *_), copy in w2.items():
            if which == group:
                copy.wait_recv()
        slots = pl.ds(0, 1) if group == 0 else pl.ds(1, 2)
        half = wt.at[slots, pl.ds(pl.multiple_of(c * 512, 512), 512)]
        i = 33 + 31 * group
        w3[group] = go(half, half, ws.at[i], wr.at[i], sibling, z)

    w_first(0)
    load_v.wait()
    wide[8 : 8 + ROWS, :] = vbuf[...].astype(f32)
    w_first(1)
    edge.wait_recv()
    inside = jnp.where(s > 0, 1.0, 0.0).astype(f32)
    wide[0:8, :] = halo[...].astype(f32)[8:16] * inside

    def convolve(n):
        at = 8 + n * BLOCK
        acc = cw_ref[0:1, :] * wide[at : at + BLOCK, :]
        for j in (1, 2):
            acc = acc + cw_ref[j : j + 1, :] * wide[at - j : at - j + BLOCK, :]
        conv[n * BLOCK : (n + 1) * BLOCK, :] = acc.astype(bf16)

    convolve(0)
    w_second(0)
    for n in (1, 2, 3):
        convolve(n)
    cot_on()
    w_second(1)
    load_cot.wait()

    def flip(b, carry):
        cott[:, row_block(b)] = jnp.transpose(cot[row_block(b), :], (1, 0))
        return carry

    lax.fori_loop(0, NB, flip, 0)
    w_third(0)

    scan_a, scan_b = scans[: len(scans) // 2], scans[len(scans) // 2 :]
    tot, ent = scan_a[0], scan_a[9]
    tot[...] = jnp.zeros_like(tot)

    def states(n, carry):
        rows = row_block(n)
        for h in range(HEADS):
            own = nn(phi(kx, h, rows), conv[rows, h * DV : (h + 1) * DV])
            st[n, h] = own
            tot[h] += own
        return carry

    lax.fori_loop(0, NB, states, 0)
    pair, along_y, along_x, back, done = scan_steps(scan_a, True)
    pair()

    def third(half, i):
        return pl.ds(pl.multiple_of(half * HALF + i * (HALF // 2), HALF // 2), HALF // 2)

    def fill(k, dst, half):
        def part(i, carry):
            rows = third(half, i)
            dst[rows, :] = nn(cot[rows, :], wt[SLOT[k]]).astype(bf16)
            return carry

        lax.fori_loop(0, 2, part, 0)

    half_a, half_b = pl.ds(0, HALF), pl.ds(HALF, HALF)
    rs = {}
    w3[0].wait_recv()
    fill(2, opp, 0)
    rs["or"] = go(opp.at[half_a], opp_l, zs.at[12], zr.at[12], s, right)
    fill(2, opp, 1)
    rs["ol"] = go(opp.at[half_b], opp_r, zs.at[13], zr.at[13], s, left)
    w_third(1)
    along_y()
    mask = lower()
    mask_t = jnp.logical_not(mask) | (
        lax.broadcasted_iota(jnp.int32, (BLOCK, BLOCK), 0)
        == lax.broadcasted_iota(jnp.int32, (BLOCK, BLOCK), 1)
    )

    def intra(n, carry):
        rows = row_block(n)
        for h in range(HEADS):
            entries = slice(16 * h, 16 * h + 16)
            sc = tn(qt_ref[entries, rows], kt_ref[entries, rows])
            att = jnp.where(mask, 1.0 + sc * (0.25 + sc * (1.0 / 32)), 0.0).astype(bf16)
            hid[rows, h * DV : (h + 1) * DV] = nn(att, conv[rows, h * DV : (h + 1) * DV])
        return carry

    lax.fori_loop(0, 2, intra, 0)
    w3[1].wait_recv()
    fill(1, to_r, 1)
    rs["dr"] = go(to_r.at[half_b], from_l.at[half_b], zs.at[14], zr.at[14], s, right)
    fill(3, to_l, 0)
    rs["dl"] = go(to_l.at[half_a], from_r.at[half_a], zs.at[15], zr.at[15], s, left)
    along_x()
    lax.fori_loop(2, 4, intra, 0)
    back()
    done()
    wts = weights()

    def finish(n, carry):
        rows = row_block(n)
        for h in range(HEADS):
            lanes = slice(h * DV, (h + 1) * DV)
            state = ent[h]
            ent[h] = state + st[n, h]
            before_block = (state * wts).astype(bf16)
            prev[n, h] = before_block
            hidden = hid[rows, lanes] + tn(phi(qx, h, rows), before_block)
            hid[rows, lanes] = hidden
            scale = lax.rsqrt(jnp.mean(hidden * hidden, axis=-1, keepdims=True) + EPSILON)
            oall[0, h, rows, :] = (hidden * scale * gain_ref[0:1, lanes]).astype(bf16)
        return carry

    lax.fori_loop(0, NB, finish, 0)

    load_w.wait()
    for copy in others:
        copy.wait()
    cz["l", 1].wait_recv()
    cz["r", 1].wait_recv()
    cz["f", 0].wait_recv()
    cz["f", 1].wait_recv()
    gf[...] = nn(cot[REST:ROWS, :], wt[SLOT[0]])
    for k in (1, 2, 3):
        for t in (0, 1):
            block = pool[2 * (k - 1) + t].reshape(512, CH)
            gf[...] += nn(cf[k - 1, :, 512 * t : 512 * t + 512], block)

    def add_in(k, dst, got, half):
        def part(i, carry):
            rows, here = third(half, i), third(0, i)
            term = nn(cot[rows, :], wt[SLOT[k]]) + got[here, :].astype(f32)
            dst[rows, :] = term.astype(bf16)
            return carry

        lax.fori_loop(0, 2, part, 0)

    rs["or"].wait_recv()
    add_in(1, to_r, opp_l, 0)
    rs["ar"] = go(to_r.at[half_a], from_l.at[half_a], zs.at[16], zr.at[16], s, right)
    rs["ol"].wait_recv()
    add_in(3, to_l, opp_r, 1)
    rs["al"] = go(to_l.at[half_b], from_r.at[half_b], zs.at[17], zr.at[17], s, left)

    ag = {}
    for h in range(HEADS):
        ag["l", h] = go(oall.at[0, h], oall.at[3, h], zs.at[h], zr.at[h], s, right)
        e = (h + 2) % 4
        ag["r", e] = go(oall.at[0, e], oall.at[1, e], zs.at[4 + e], zr.at[4 + e], s, left)

    def hand_on(h):
        ag["l", h].wait_recv()
        ag["f", h] = go(oall.at[3, h], oall.at[2, h], zs.at[8 + h], zr.at[8 + h], s, right)
        e = h + 2
        ag["r", e].wait_recv()
        ag["f", e] = go(oall.at[1, e], oall.at[2, e], zs.at[8 + e], zr.at[8 + e], s, left)

    def joined(k, rows, heads):
        return jnp.concatenate([oall[k, h, rows, :] for h in heads], axis=1)

    g1, g2, g3, g4 = {}, {}, {}, {}
    sem0 = {name: 16 * i for i, name in enumerate(UNITS)}

    def gw_term(u, split=False):
        k, heads, off, w = UNITS[u]
        cols = pl.ds(2 * off, 2 * w)
        i = sem0[u]

        def part(t, carry):
            term = nn(cott[row_block(t), :], joined(k, slice(None), heads)).astype(bf16)
            pool[k, t, :, cols] = term[0:128]
            pool[4 + k, t, :, cols] = term[128:256]
            return carry

        if split:
            g1[u] = []
            for t in range(4):
                part(t, 0)
                g1[u].append(
                    go(
                        pool.at[4 * (1 - c) + k, t, :, cols],
                        r1.at[k, t, :, cols], gs.at[i + t], gr.at[i + t], sibling, z,
                    )
                )
        else:
            lax.fori_loop(0, 4, part, 0)
            theirs = pool.at[4 * (1 - c) + k, :, :, cols]
            g1[u] = [go(theirs, r1.at[k, :, :, cols], gs.at[i], gr.at[i], sibling, z)]

    def gw_first(u):
        k, heads, off, w = UNITS[u]
        cols = slice(2 * off, 2 * off + 2 * w)
        for copy in g1[u]:
            copy.wait_recv()

        def part(t, carry):
            both = pool[4 * c + k, t, :, cols].astype(f32) + r1[k, t, :, cols].astype(f32)
            gsum[k, t, :, cols] = both.astype(bf16)
            return carry

        lax.fori_loop(0, 4, part, 0)
        for j in (2, 1, 3):
            nx, ny = (x + j) % 4, (y + j) % 4
            i = sem0[u] + 4 + j - 1
            rows = pl.ds(pl.multiple_of(nx * 32, 32), 32)
            g2[u, 0, j] = go(
                gsum.at[k, :, rows, pl.ds(2 * off, w)],
                p1a.at[k, j - 1, :, :, pl.ds(off, w)], gs.at[i], gr.at[i], seq_of(nx, y, c), z,
            )
            i += 3
            g2[u, 1, j] = go(
                gsum.at[k, ny, :, pl.ds(2 * off + w, w)],
                p1b.at[k, j - 1, :, pl.ds(off, w)], gs.at[i], gr.at[i], seq_of(x, ny, c), z,
            )

    my_rows = pl.ds(pl.multiple_of(x * 32, 32), 32)

    def gw_second(u):
        k, heads, off, w = UNITS[u]
        cols = slice(off, off + w)
        sum_a = gsum[k, :, my_rows, 2 * off : 2 * off + w].astype(f32)
        sum_b = gsum[k, y, :, 2 * off + w : 2 * off + 2 * w].astype(f32)
        for j in (1, 3, 2):
            g2[u, 0, j].wait_recv()
            sum_a = sum_a + p1a[k, j - 1, :, :, cols].astype(f32)
            g2[u, 1, j].wait_recv()
            sum_b = sum_b + p1b[k, j - 1, :, cols].astype(f32)
        s2a[k, :, :, cols] = sum_a.astype(bf16)
        s2b[k, :, cols] = sum_b.astype(bf16)
        for j in (2, 1, 3):
            nx, ny = (x + j) % 4, (y + j) % 4
            i = sem0[u] + 10 + j - 1
            rows = pl.ds(pl.multiple_of(nx * 32, 32), 32)
            here = pl.ds(off, w)
            g3[u, 0, j] = go(
                s2a.at[k, ny, :, here],
                p2a.at[k, j - 1, :, here], gs.at[i], gr.at[i], seq_of(x, ny, c), z,
            )
            i += 3
            g3[u, 1, j] = go(
                s2b.at[k, rows, here],
                p2b.at[k, j - 1, :, here], gs.at[i], gr.at[i], seq_of(nx, y, c), z,
            )

    def gw_third(u):
        k, heads, off, w = UNITS[u]
        cols = slice(off, off + w)
        sum_a = s2a[k, y, :, cols].astype(f32)
        sum_b = s2b[k, my_rows, cols].astype(f32)
        for j in (1, 3, 2):
            g3[u, 0, j].wait_recv()
            sum_a = sum_a + p2a[k, j - 1, :, cols].astype(f32)
            g3[u, 1, j].wait_recv()
            sum_b = sum_b + p2b[k, j - 1, :, cols].astype(f32)
        fin[k, :, cols] = sum_a.astype(bf16)
        fin[k, :, 256 + off : 256 + off + w] = sum_b.astype(bf16)

    def gw_move(k):
        def move():
            return pltpu.make_async_remote_copy(
                src_ref=fin.at[k],
                dst_ref=gw_hbm.at[my_rows],
                send_sem=ms.at[k],
                recv_sem=mr.at[x],
                device_id={"seq": seq_of(z, y, c), "head": (z + k) % 4},
                device_id_type=pl.DeviceIdType.MESH,
            )

        if k:
            g4[k] = move
            move().start()
        else:

            @pl.when(stays)
            def _():
                load(fin.at[0], gw_hbm.at[my_rows], ms.at[0]).wait()

            @pl.when(jnp.logical_not(stays))
            def _():
                move().start()
                move().wait_send()

    def gw_done():
        for k in (1, 2, 3):
            g4[k]().wait_send()
        for xs in range(4):

            @pl.when(jnp.logical_not(stays & (x == xs)))
            def _():
                pltpu.make_async_remote_copy(
                    src_ref=fin.at[0],
                    dst_ref=gw_hbm.at[pl.ds(32 * xs, 32)],
                    send_sem=ms.at[0],
                    recv_sem=mr.at[xs],
                    device_id={"seq": seq_of(z, y, c), "head": (z + 1) % 4},
                    device_id_type=pl.DeviceIdType.MESH,
                ).wait_recv()

    out_copies = []

    def mix(parts, first, last, lo=0, hi=NB):
        def part(b, carry):
            rows = row_block(b)
            for u in (0, 1):
                cols = slice(512 * u, 512 * u + 512)
                acc = None if first else macc[rows, cols]
                for k, heads in parts:
                    if len(heads) == HEADS:
                        rhs = wt[SLOT[k], cols, :]
                    else:
                        lanes = [slice(h * DV, (h + 1) * DV) for h in heads]
                        rhs = jnp.concatenate([wt[SLOT[k], cols, o] for o in lanes], axis=1)
                    term = nt(joined(k, rows, heads), rhs)
                    acc = term if acc is None else acc + term
                if last:
                    mixv[rows, cols] = acc.astype(bf16)
                else:
                    macc[rows, cols] = acc
            if last:
                pltpu.make_async_copy(mixv.at[rows], mixed_hbm.at[rows], osem.at[b]).start()
            return carry

        lax.fori_loop(lo, hi, part, 0)
        if last:
            for b in range(lo, hi):
                rows = pl.ds(b * BLOCK, BLOCK)
                out_copies.append(
                    pltpu.make_async_copy(mixv.at[rows], mixed_hbm.at[rows], osem.at[b])
                )

    every = (0, 1, 2, 3)
    gw_term("0")
    mix(((0, every),), True, False)
    gw_first("0")

    tot_b, ent_b = scan_b[0], scan_b[9]
    tot_b[...] = jnp.zeros_like(tot_b)

    def back_states(n, grad_out):
        rows = row_block(n)
        for h in range(HEADS):
            lanes = slice(h * DV, (h + 1) * DV)
            hidden = hid[rows, lanes]
            scale = lax.rsqrt(jnp.mean(hidden * hidden, axis=-1, keepdims=True) + EPSILON)
            normed = hidden * scale
            up = grad_out[:, lanes] * gain_ref[0:1, lanes]
            grad = scale * (up - normed * jnp.mean(up * normed, axis=-1, keepdims=True))
            grad = grad.astype(bf16)
            gh[rows, lanes] = grad
            own = nn(phi(qx, h, rows), grad)
            bg[n, h] = own
            tot_b[h] += own

    def back_rest(n, carry):
        rows = row_block(n)
        grad_out = nn(cot[rows, :], wt[SLOT[0]])
        grad_out = grad_out + from_r[rows, :].astype(f32) + from_l[rows, :].astype(f32)
        back_states(n, grad_out)
        return carry

    back_states(NB - 1, gf[...])
    for name in ("dr", "dl", "ar", "al"):
        rs[name].wait_recv()
    lax.fori_loop(0, NB - 1, back_rest, 0)
    pair, along_y, along_x, back, done = scan_steps(scan_b, False)

    def back_intra(n, carry):
        rows = row_block(n)
        for h in range(HEADS):
            lanes = slice(h * DV, (h + 1) * DV)
            entries = slice(16 * h, 16 * h + 16)
            qh = qt_ref[entries, rows]
            kh = kt_ref[entries, rows]
            g = gh[rows, lanes]
            v = conv[rows, lanes]
            sc = tn(kh, qh)
            ds = jnp.where(mask_t, nt(v, g) * (0.25 + sc * (1.0 / 16)), 0.0).astype(bf16)
            att = jnp.where(mask_t, 1.0 + sc * (0.25 + sc * (1.0 / 32)), 0.0).astype(bf16)
            wide[rows, lanes] = nn(att, g)
            across = phi_back(nt(prev[n, h], g), qx, t2, h, rows)
            gqv[entries, rows] = (nn(kh, ds) + across).astype(bf16)
            dx[entries, rows] = nt(qh, ds)
        return carry

    pair()
    lax.fori_loop(0, 1, back_intra, 0)
    along_y()
    hand_on(0)
    lax.fori_loop(1, 3, back_intra, 0)
    along_x()
    hand_on(1)
    lax.fori_loop(3, 4, back_intra, 0)
    back()
    gw_second("0")
    out_copies.append(load(gqv, gq_hbm, osem.at[4]))
    done()

    def suffix(t, carry):
        n = NB - 1 - t
        for h in range(HEADS):
            state = ent_b[h]
            ent_b[h] = state + bg[n, h]
            fw[n, h] = (state * wts).astype(bf16)
        return carry

    lax.fori_loop(0, NB, suffix, 0)

    def back_finish(n, carry):
        rows = row_block(n)
        for h in range(HEADS):
            lanes = slice(h * DV, (h + 1) * DV)
            entries = slice(16 * h, 16 * h + 16)
            wide[rows, lanes] += tn(phi(kx, h, rows), fw[n, h])
            across = phi_back(nt(fw[n, h], conv[rows, lanes]), kx, t2, h, rows)
            gkv[entries, rows] = (dx[entries, rows] + across).astype(bf16)
        return carry

    lax.fori_loop(0, 1, back_finish, 0)
    edge_rows[...] = wide[0:8, :]
    edge_back = go(edge_rows, halo_back, hsem.at[2], hsem.at[3], before, z)
    lax.fori_loop(1, NB, back_finish, 0)
    edge_back.wait_recv()
    inside = jnp.where(s < 31, 1.0, 0.0).astype(f32)
    wide[ROWS : ROWS + 8, :] = halo_back[...] * inside
    for n in range(NB):
        at = n * BLOCK
        acc = cw_ref[0:1, :] * wide[at : at + BLOCK, :]
        for j in (1, 2):
            acc = acc + cw_ref[j : j + 1, :] * wide[at + j : at + j + BLOCK, :]
        vbuf[at : at + BLOCK, :] = acc.astype(bf16)
    out_copies.append(load(gkv, gk_hbm, osem.at[5]))
    out_copies.append(load(vbuf, gv_hbm, osem.at[6]))

    gw_third("0")
    gw_move(0)
    ag["l", 2].wait_recv()
    ag["l", 3].wait_recv()
    gw_term("3")
    ag["r", 0].wait_recv()
    ag["r", 1].wait_recv()
    gw_term("1")
    gw_first("3")
    gw_first("1")
    ag["f", 0].wait_recv()
    ag["f", 2].wait_recv()
    gw_term("2a")
    mix(((1, every), (3, every)), False, False)
    gw_second("3")
    gw_second("1")
    gw_first("2a")
    ag["f", 1].wait_recv()
    ag["f", 3].wait_recv()
    gw_term("2b", True)
    mix(((2, every),), False, True, 0, 2)
    gw_first("2b")
    mix(((2, every),), False, True, 2, 4)
    gw_second("2a")
    gw_third("3")
    gw_move(3)
    gw_third("1")
    gw_move(1)
    gw_second("2b")
    gw_third("2a")
    gw_third("2b")
    gw_move(2)
    for copy in out_copies:
        copy.wait()
    gw_done()
    for copy in sends:
        copy.wait_send()


def hand_over_kernel(*refs):
    arrays, results, held, sem_in, sem_out = refs[:5], refs[5:10], refs[10:15], refs[15], refs[16]
    first, second = [], []
    for src, mid, dst in zip(arrays, held, results, strict=True):
        rows = max(src.shape[0] // 8, 32)
        for at in range(0, src.shape[0], rows):
            part = pl.ds(at, rows)
            i = len(first)
            first.append(pltpu.make_async_copy(src.at[part], mid.at[part], sem_in.at[i]))
            second.append(pltpu.make_async_copy(mid.at[part], dst.at[part], sem_out.at[i]))
    for copy in first:
        copy.start()
    for copy, onward in zip(first, second, strict=True):
        copy.wait()
        onward.start()
    for copy in second:
        copy.wait()


def hand_over(*arrays):
    hbm = pl.BlockSpec(memory_space=pl.ANY)
    return pl.pallas_call(
        hand_over_kernel,
        out_shape=tuple(jax.ShapeDtypeStruct(a.shape, a.dtype) for a in arrays),
        in_specs=[hbm] * 5,
        out_specs=(hbm,) * 5,
        scratch_shapes=[pltpu.VMEM(a.shape, a.dtype) for a in arrays]
        + [pltpu.SemaphoreType.DMA((24,))] * 2,
        compiler_params=pltpu.CompilerParams(vmem_limit_bytes=VMEM_LIMIT),
        name="hand_over",
    )(*arrays)


def on_device(query, key_feat, values, conv_w, gain, w_out, cotangent):
    hbm = pl.BlockSpec(memory_space=pl.ANY)
    dma = pltpu.SemaphoreType.DMA
    vmem = pltpu.VMEM
    mixed, gq, gk, gv, gw = pl.pallas_call(
        kernel,
        out_shape=(
            jax.ShapeDtypeStruct((ROWS, FEAT), bf16),
            jax.ShapeDtypeStruct((HEADS * FD, ROWS), bf16),
            jax.ShapeDtypeStruct((HEADS * FD, ROWS), bf16),
            jax.ShapeDtypeStruct((ROWS, CH), bf16),
            jax.ShapeDtypeStruct((128, CH), bf16),
        ),
        in_specs=[hbm] * 7,
        out_specs=(hbm,) * 5,
        scratch_shapes=[
            vmem((16, CH), bf16),
            vmem((8, CH), f32),
            vmem((8, CH), f32),
            vmem((ROWS + 8, CH), f32),
            vmem((HEADS, 32, ROWS), f32),
            vmem((HEADS, 32, ROWS), f32),
            vmem((ROWS, CH), bf16),
            vmem((NB, HEADS, NF, DV), f32),
            vmem((ROWS, CH), f32),
            vmem((NB, HEADS, NF, DV), bf16),
            vmem((4, HEADS, ROWS, DV), bf16),
            vmem((4, FEAT, CH), bf16),
            vmem((ROWS, FEAT), bf16),
            vmem((FEAT, ROWS), bf16),
            vmem((REST, CH), bf16),
            vmem((REST, CH), bf16),
            vmem((REST, CH), bf16),
            vmem((HALF, CH), bf16),
            vmem((HALF, CH), bf16),
            vmem((REST, CH), bf16),
            vmem((REST, CH), bf16),
            vmem((3, FILL, FEAT), bf16),
            vmem((FILL, CH), f32),
            vmem((8, 4, 128, CH), bf16),
            vmem((4, 4, 128, CH), bf16),
            vmem((4, 4, 128, CH), bf16),
            vmem((4, 3, 4, 32, 256), bf16),
            vmem((4, 3, 128, 256), bf16),
            vmem((4, 4, 32, 256), bf16),
            vmem((4, 128, 256), bf16),
            vmem((4, 3, 32, 256), bf16),
            vmem((4, 3, 32, 256), bf16),
            vmem((4, 32, CH), bf16),
            vmem((ROWS, FEAT), f32),
            vmem((ROWS, CH), bf16),
            vmem((NB, HEADS, NF, DV), f32),
            vmem((NB, HEADS, NF, DV), bf16),
            vmem((HEADS * FD, ROWS), f32),
            vmem((7, 32, BLOCK), f32),
            vmem((ROWS, CH), bf16),
            vmem((ROWS, FEAT), bf16),
            vmem((HEADS * FD, ROWS), bf16),
            vmem((HEADS * FD, ROWS), bf16),
            vmem((HEADS * FD, ROWS), bf16),
            vmem((HEADS * FD, ROWS), bf16),
            vmem((3, CH), f32),
            vmem((1, CH), f32),
            dma((7,)),
            dma((24,)),
            dma((7,)),
            dma((4,)),
            dma((24,)),
            dma((24,)),
            dma((65,)),
            dma((65,)),
            dma((80,)),
            dma((80,)),
            dma((4,)),
            dma((4,)),
        ]
        + SCAN_SCRATCH * 2,
        compiler_params=pltpu.CompilerParams(
            collective_id=0, has_side_effects=True, vmem_limit_bytes=VMEM_LIMIT
        ),
        name="sublayer",
    )(query.T, key_feat.T, conv_w, gain.reshape(1, CH), values, w_out, cotangent)
    mixed, gq, gk, gv, gw = hand_over(mixed, gq, gk, gv, gw)
    return mixed, gq.T, gk.T, gv, gw


def solution(mesh):
    both = P("seq", "head")
    return jax.shard_map(
        on_device,
        mesh=mesh,
        in_specs=(both, both, both, P(None, "head"), P("head"), P(None, "head"), both),
        out_specs=(both,) * 5,
        check_vma=False,
    )
```

```python
import functools

import jax
import jax.numpy as jnp
from jax import lax
from jax.experimental import pallas as pl
from jax.experimental.pallas import tpu as pltpu
from jax.sharding import PartitionSpec as P

f32 = jnp.float32
bf16 = jnp.bfloat16
FD = 16
BLOCK = 256
ROWS = 1024
HEADS = 4
NB = ROWS // BLOCK
DV = 128
CH = HEADS * DV
FEAT = 1024
NF = 160
EPSILON = 1e-05
VMEM_LIMIT = 60 * 1024 * 1024


def nn(a, b):
    return lax.dot_general(a, b, (((1,), (0,)), ((), ())), preferred_element_type=f32)


def nt(a, b):
    return lax.dot_general(a, b, (((1,), (1,)), ((), ())), preferred_element_type=f32)


def tn(a, b):
    return lax.dot_general(a, b, (((0,), (0,)), ((), ())), preferred_element_type=f32)


def place():
    s = lax.axis_index("seq")
    z = lax.axis_index("head")
    return s, z, s // 8, (s // 2) % 4, s % 2


def seq_of(x, y, c):
    return (x * 4 + y) * 2 + c


def remote(src, dst, send_sem, recv_sem, seq, head):
    copy = pltpu.make_async_remote_copy(
        src_ref=src,
        dst_ref=dst,
        send_sem=send_sem,
        recv_sem=recv_sem,
        device_id={"seq": seq, "head": head},
        device_id_type=pl.DeviceIdType.MESH,
    )
    copy.start()
    return copy


def greet(devices):
    barrier = pltpu.get_barrier_semaphore()
    for seq, head in devices:
        pl.semaphore_signal(
            barrier, inc=1, device_id={"seq": seq, "head": head}, device_id_type=pl.DeviceIdType.MESH
        )
    pl.semaphore_wait(barrier, len(devices))


def plane_peers(s, z, x, y, c):
    out = [(seq_of(x, y, 1 - c), z)]
    for j in (1, 2, 3):
        out.append((seq_of((x + j) % 4, y, c), z))
        out.append((seq_of(x, (y + j) % 4, c), z))
    return out


def spread(xt_ref, x2_ref):
    for h in range(HEADS):
        x = xt_ref[16 * h : 16 * h + 16, :].astype(f32)
        x2_ref[h, 0:16, :] = x
        x2_ref[h, 16:32, :] = x


def phi(x2_ref, h, cols):
    x = x2_ref[h, 0:16, cols]
    parts = [x * x]
    for d in range(1, 8):
        parts.append(x * x2_ref[h, d : d + 16, cols])
    parts.append(x[0:8] * x2_ref[h, 8:16, cols])
    parts.append((lax.broadcasted_iota(jnp.int32, (8, BLOCK), 0) == 0).astype(f32))
    parts.append(x)
    return jnp.concatenate(parts, axis=0).astype(bf16)


def phi_back(g, x2_ref, t2_ref, h, cols):
    x = x2_ref[h, 0:16, cols]
    acc = g[144:160] + 2.0 * g[0:16] * x
    for d in range(1, 8):
        gd = g[16 * d : 16 * d + 16]
        acc = acc + gd * x2_ref[h, d : d + 16, cols]
        t = gd * x
        t2_ref[d - 1, 0:16, :] = t
        t2_ref[d - 1, 16:32, :] = t
        acc = acc + t2_ref[d - 1, 16 - d : 32 - d, :]
    g8 = g[128:136]
    low = g8 * x2_ref[h, 8:16, cols]
    high = g8 * x[0:8]
    return acc + jnp.concatenate([low, high], axis=0)


def weights():
    r = lax.broadcasted_iota(jnp.int32, (NF, DV), 0)
    return jnp.where(
        r < 16, 1.0 / 32, jnp.where(r < 136, 1.0 / 16, jnp.where(r < 144, 1.0, 0.25))
    ).astype(f32)


def lower():
    r = lax.broadcasted_iota(jnp.int32, (BLOCK, BLOCK), 0)
    c = lax.broadcasted_iota(jnp.int32, (BLOCK, BLOCK), 1)
    return r >= c


SCAN_SCRATCH = [
    pltpu.VMEM((HEADS, NF, DV), f32),
    pltpu.VMEM((2, NF, DV), f32),
    pltpu.VMEM((2, NF, DV), bf16),
    pltpu.VMEM((3, 2, NF, DV), bf16),
    pltpu.VMEM((2, NF, DV), bf16),
    pltpu.VMEM((3, 2, NF, DV), bf16),
    pltpu.VMEM((2, NF, DV), f32),
    pltpu.VMEM((2, NF, DV), f32),
    pltpu.VMEM((2, NF, DV), f32),
    pltpu.VMEM((HEADS, NF, DV), f32),
    pltpu.SemaphoreType.DMA((8,)),
    pltpu.SemaphoreType.DMA((8,)),
]


def scan_steps(refs, forward):
    tot, ra, ys, yr, xs, xr, py, fs, fr, ent, ssem, rsem = refs
    s, z, x, y, c = place()
    sibling = seq_of(x, y, 1 - c)
    mine = pl.ds(2 * c, 2)
    copies = {}

    def counts(me, j):
        met = (me - j >= 0) if forward else (me - j < 0)
        return jnp.where(met, 1.0, 0.0).astype(f32)

    def pair():
        copies["a"] = remote(tot.at[pl.ds(2 * (1 - c), 2)], ra, ssem.at[0], rsem.at[0], sibling, z)

    def along_y():
        copies["a"].wait_recv()
        ys[...] = (tot[mine] + ra[...]).astype(bf16)
        for j in (1, 2, 3):
            copies["y", j] = remote(
                ys, yr.at[j - 1], ssem.at[j], rsem.at[j], seq_of(x, (y + j) % 4, c), z
            )

    def along_x():
        row = tot[mine] + ra[...]
        before = jnp.zeros((2, NF, DV), f32)
        for j in (1, 3, 2):
            copies["y", j].wait_recv()
            got = yr[j - 1].astype(f32)
            row = row + got
            before = before + got * counts(y, j)
        xs[...] = row.astype(bf16)
        py[...] = before
        for j in (1, 2, 3):
            copies["x", j] = remote(
                xs, xr.at[j - 1], ssem.at[3 + j], rsem.at[3 + j], seq_of((x + j) % 4, y, c), z
            )

    def back():
        before = py[...]
        for j in (1, 3, 2):
            copies["x", j].wait_recv()
            before = before + xr[j - 1].astype(f32) * counts(x, j)
        first = jnp.where(c == 0, 1.0, 0.0).astype(f32)
        other = first if forward else 1.0 - first
        fs[...] = before + tot[mine] * other
        ent[mine] = before + ra[...] * (1.0 - other)
        copies["f"] = remote(fs, fr, ssem.at[7], rsem.at[7], sibling, z)

    def done():
        copies["f"].wait_recv()
        ent[pl.ds(2 * (1 - c), 2)] = fr[...]
        for copy in copies.values():
            copy.wait_send()

    return pair, along_y, along_x, back, done


SLOT = {2: 0, 1: 1, 3: 2, 0: 3}
GROUPS = ((2,), (1, 3))
FILL = 192
REST = ROWS - FILL
HALF = REST // 2
PART = FILL // 2
UNITS = {
    "0": (0, (0, 1, 2, 3), 0, 256),
    "1": (1, (0, 1, 2, 3), 0, 256),
    "3": (3, (0, 1, 2, 3), 0, 256),
    "2a": (2, (0, 2), 0, 128),
    "2b": (2, (1, 3), 128, 128),
}


def row_block(n):
    return pl.ds(pl.multiple_of(n * BLOCK, BLOCK), BLOCK)


def kernel(
    qt_hbm, kt_hbm, cw_hbm, gain_hbm, v_hbm, w_hbm, cot_hbm,
    mixed_hbm, gq_hbm, gk_hbm, gv_hbm, gw_hbm,
    halo, halo_back, edge_rows, wide, qx, kx, conv, st, hid, prev, oall,
    wt, cot, cott, opp, to_r, to_l, opp_l, opp_r, from_r, from_l, cf, gf,
    pool, r1, gsum, p1a, p1b, s2a, s2b, p2a, p2b, fin, macc,
    gh, bg, fw, dx, t2, vbuf, mixv, gqv, gkv, qt_ref, kt_ref, cw_ref, gain_ref,
    lsem, fsem, osem, hsem, zs, zr, ws, wr, gs, gr, ms, mr, *scans,
):
    s, z, x, y, c = place()
    right, left = (z + 1) % 4, (z + 3) % 4
    sibling = seq_of(x, y, 1 - c)
    after, before = (s + 1) % 32, (s + 31) % 32
    sends = []

    def go(*args):
        copy = remote(*args)
        sends.append(copy)
        return copy

    def load(src, dst, sem):
        copy = pltpu.make_async_copy(src, dst, sem)
        copy.start()
        return copy

    small = [
        load(src, dst, lsem.at[3 + i])
        for i, (src, dst) in enumerate(
            ((kt_hbm, kt_ref), (qt_hbm, qt_ref), (cw_hbm, cw_ref), (gain_hbm, gain_ref))
        )
    ]
    load_v = load(v_hbm, vbuf, lsem.at[2])
    load_cot = load(cot_hbm, cot, lsem.at[0])
    load_w = load(
        w_hbm.at[pl.ds(pl.multiple_of(z * FEAT, FEAT), FEAT)], wt.at[SLOT[0]], lsem.at[1]
    )

    barrier = pltpu.get_barrier_semaphore()

    def signal(seq, head):
        pl.semaphore_signal(
            barrier, inc=1, device_id={"seq": seq, "head": head}, device_id_type=pl.DeviceIdType.MESH
        )

    known = plane_peers(s, z, x, y, c) + [(s, (z + k) % 4) for k in (1, 2, 3)]
    known += [(after, z), (before, z)]
    known += [(seq_of(z, y, c), (z + k) % 4) for k in (1, 2, 3)]
    known += [(seq_of((x + j) % 4, y, c), x) for j in (1, 2, 3)]
    for seq, head in known:
        signal(seq, head)
    stays = x == z

    @pl.when(jnp.logical_not(stays))
    def _():
        signal(seq_of(z, y, c), z)
        signal(s, x)

    for copy in small:
        copy.wait()
    spread(kt_ref, kx)
    spread(qt_ref, qx)
    pl.semaphore_wait(barrier, len(known) + jnp.where(stays, 0, 2))

    row = c * 512 + x * 128 + y * 32
    wz = {}
    for k in (2, 1, 3):
        there = (z + k) % 4
        wz[k] = go(
            w_hbm.at[pl.ds(pl.multiple_of(there * FEAT + row, 32), 32)],
            wt.at[SLOT[4 - k], pl.ds(pl.multiple_of(row, 32), 32)],
            ws.at[k - 1],
            wr.at[k - 1],
            s,
            there,
        )
    edge = go(v_hbm.at[pl.ds(ROWS - 16, 16)], halo, hsem.at[0], hsem.at[1], after, z)

    cz = {}
    for i, lo in enumerate((0, PART)):
        here = pl.ds(REST + lo, PART)
        cz["l", i] = go(
            cot_hbm.at[here], cf.at[2, pl.ds(lo, PART)], zs.at[18 + i], zr.at[18 + i], s, right
        )
        lo = PART - lo
        here = pl.ds(REST + lo, PART)
        cz["r", i] = go(
            cot_hbm.at[here], cf.at[0, pl.ds(lo, PART)], zs.at[20 + i], zr.at[20 + i], s, left
        )
    others = []
    for k in (1, 2, 3):
        for t in range(8):
            at = pl.multiple_of((z + k) % 4 * FEAT + 128 * t, 128)
            others.append(
                load(
                    w_hbm.at[pl.ds(at, 128)],
                    pool.at[2 * (k - 1) + t // 4, t % 4],
                    fsem.at[8 * (k - 1) + t],
                )
            )

    def cot_on():
        cz["l", 0].wait_recv()
        a = pl.ds(0, PART)
        cz["f", 0] = go(cf.at[2, a], cf.at[1, a], zs.at[22], zr.at[22], s, right)
        cz["r", 0].wait_recv()
        b = pl.ds(PART, PART)
        cz["f", 1] = go(cf.at[0, b], cf.at[1, b], zs.at[23], zr.at[23], s, left)

    def piece(group, px, py, half):
        at = pl.multiple_of(c * 512 + px * 128 + py * 32, 32)
        slots = pl.ds(0, 1) if group == 0 else pl.ds(1, 2)
        return wt.at[slots, pl.ds(at, 32), pl.ds(half * 256, 256)]

    w1, w2, w3 = {}, {}, {}

    def w_first(group):
        for k in GROUPS[group]:
            wz[4 - k].wait_recv()
        at = 3 + 31 * group
        for j in (1, 2, 3):
            own = piece(group, x, y, 0)
            i = at + j - 1
            w1[group, 0, j] = go(own, own, ws.at[i], wr.at[i], seq_of((x + j) % 4, y, c), z)
            own = piece(group, x, y, 1)
            i = at + j + 2
            w1[group, 1, j] = go(own, own, ws.at[i], wr.at[i], seq_of(x, (y + j) % 4, c), z)

    def w_second(group):
        at = 9 + 31 * group
        for i in (0, 1, 3, 2):
            for half in (0, 1):
                if i:
                    w1[group, half, i].wait_recv()
                if half == 0:
                    block = piece(group, (x - i + 4) % 4, y, 0)
                else:
                    block = piece(group, x, (y - i + 4) % 4, 1)
                for j in (1, 2, 3):
                    to = seq_of(x, (y + j) % 4, c) if half == 0 else seq_of((x + j) % 4, y, c)
                    w2[group, half, i, j] = go(block, block, ws.at[at], wr.at[at], to, z)
                    at += 1

    def w_third(group):
        for (which, *_), copy in w2.items():
            if which == group:
                copy.wait_recv()
        slots = pl.ds(0, 1) if group == 0 else pl.ds(1, 2)
        half = wt.at[slots, pl.ds(pl.multiple_of(c * 512, 512), 512)]
        i = 33 + 31 * group
        w3[group] = go(half, half, ws.at[i], wr.at[i], sibling, z)

    w_first(0)
    load_v.wait()
    wide[8 : 8 + ROWS, :] = vbuf[...].astype(f32)
    w_first(1)
    edge.wait_recv()
    inside = jnp.where(s > 0, 1.0, 0.0).astype(f32)
    wide[0:8, :] = halo[...].astype(f32)[8:16] * inside

    def convolve(n):
        at = 8 + n * BLOCK
        acc = cw_ref[0:1, :] * wide[at : at + BLOCK, :]
        for j in (1, 2):
            acc = acc + cw_ref[j : j + 1, :] * wide[at - j : at - j + BLOCK, :]
        conv[n * BLOCK : (n + 1) * BLOCK, :] = acc.astype(bf16)

    convolve(0)
    w_second(0)
    for n in (1, 2, 3):
        convolve(n)
    cot_on()
    w_third(0)
    w_second(1)
    load_cot.wait()

    scan_a, scan_b = scans[: len(scans) // 2], scans[len(scans) // 2 :]
    tot, ent = scan_a[0], scan_a[9]
    tot[...] = jnp.zeros_like(tot)

    def states(n, carry):
        rows = row_block(n)
        for h in range(HEADS):
            own = nn(phi(kx, h, rows), conv[rows, h * DV : (h + 1) * DV])
            st[n, h] = own
            tot[h] += own
        return carry

    lax.fori_loop(0, NB, states, 0)
    pair, along_y, along_x, back, done = scan_steps(scan_a, True)
    pair()

    def third(half, i):
        return pl.ds(pl.multiple_of(half * HALF + i * (HALF // 2), HALF // 2), HALF // 2)

    def fill(k, dst, half):
        def part(i, carry):
            rows = third(half, i)
            dst[rows, :] = nn(cot[rows, :], wt[SLOT[k]]).astype(bf16)
            return carry

        lax.fori_loop(0, 2, part, 0)

    half_a, half_b = pl.ds(0, HALF), pl.ds(HALF, HALF)
    rs = {}
    w3[0].wait_recv()
    fill(2, opp, 0)
    rs["or"] = go(opp.at[half_a], opp_l, zs.at[12], zr.at[12], s, right)
    fill(2, opp, 1)
    rs["ol"] = go(opp.at[half_b], opp_r, zs.at[13], zr.at[13], s, left)
    w_third(1)
    along_y()
    mask = lower()
    mask_t = jnp.logical_not(mask) | (
        lax.broadcasted_iota(jnp.int32, (BLOCK, BLOCK), 0)
        == lax.broadcasted_iota(jnp.int32, (BLOCK, BLOCK), 1)
    )

    def intra(n, carry):
        rows = row_block(n)
        for h in range(HEADS):
            entries = slice(16 * h, 16 * h + 16)
            sc = tn(qt_ref[entries, rows], kt_ref[entries, rows])
            att = jnp.where(mask, 1.0 + sc * (0.25 + sc * (1.0 / 32)), 0.0).astype(bf16)
            hid[rows, h * DV : (h + 1) * DV] = nn(att, conv[rows, h * DV : (h + 1) * DV])
        return carry

    lax.fori_loop(0, 2, intra, 0)
    w3[1].wait_recv()
    fill(1, to_r, 1)
    rs["dr"] = go(to_r.at[half_b], from_l.at[half_b], zs.at[14], zr.at[14], s, right)
    fill(3, to_l, 0)
    rs["dl"] = go(to_l.at[half_a], from_r.at[half_a], zs.at[15], zr.at[15], s, left)
    along_x()
    lax.fori_loop(2, 4, intra, 0)
    back()
    done()
    wts = weights()

    def finish(n, carry):
        rows = row_block(n)
        for h in range(HEADS):
            lanes = slice(h * DV, (h + 1) * DV)
            state = ent[h]
            ent[h] = state + st[n, h]
            before_block = (state * wts).astype(bf16)
            prev[n, h] = before_block
            hidden = hid[rows, lanes] + tn(phi(qx, h, rows), before_block)
            hid[rows, lanes] = hidden
            scale = lax.rsqrt(jnp.mean(hidden * hidden, axis=-1, keepdims=True) + EPSILON)
            oall[0, h, rows, :] = (hidden * scale * gain_ref[0:1, lanes]).astype(bf16)
        return carry

    lax.fori_loop(0, NB, finish, 0)

    load_w.wait()
    for copy in others:
        copy.wait()
    cz["l", 1].wait_recv()
    cz["r", 1].wait_recv()
    cz["f", 0].wait_recv()
    cz["f", 1].wait_recv()
    gf[...] = nn(cot[REST:ROWS, :], wt[SLOT[0]])
    for k in (1, 2, 3):
        for t in (0, 1):
            block = pool[2 * (k - 1) + t].reshape(512, CH)
            gf[...] += nn(cf[k - 1, :, 512 * t : 512 * t + 512], block)

    def add_in(k, dst, got, half):
        def part(i, carry):
            rows, here = third(half, i), third(0, i)
            term = nn(cot[rows, :], wt[SLOT[k]]) + got[here, :].astype(f32)
            dst[rows, :] = term.astype(bf16)
            return carry

        lax.fori_loop(0, 2, part, 0)

    rs["or"].wait_recv()
    add_in(1, to_r, opp_l, 0)
    rs["ar"] = go(to_r.at[half_a], from_l.at[half_a], zs.at[16], zr.at[16], s, right)
    rs["ol"].wait_recv()
    add_in(3, to_l, opp_r, 1)
    rs["al"] = go(to_l.at[half_b], from_r.at[half_b], zs.at[17], zr.at[17], s, left)

    ag = {}
    for h in range(HEADS):
        ag["l", h] = go(oall.at[0, h], oall.at[3, h], zs.at[h], zr.at[h], s, right)
        e = (h + 2) % 4
        ag["r", e] = go(oall.at[0, e], oall.at[1, e], zs.at[4 + e], zr.at[4 + e], s, left)

    def hand_on(h):
        ag["l", h].wait_recv()
        ag["f", h] = go(oall.at[3, h], oall.at[2, h], zs.at[8 + h], zr.at[8 + h], s, right)
        e = h + 2
        ag["r", e].wait_recv()
        ag["f", e] = go(oall.at[1, e], oall.at[2, e], zs.at[8 + e], zr.at[8 + e], s, left)

    def joined(k, rows, heads):
        return jnp.concatenate([oall[k, h, rows, :] for h in heads], axis=1)

    g1, g2, g3, g4 = {}, {}, {}, {}
    sem0 = {name: 16 * i for i, name in enumerate(UNITS)}

    def gw_term(u, split=False):
        k, heads, off, w = UNITS[u]
        cols = pl.ds(2 * off, 2 * w)
        i = sem0[u]

        def part(t, carry):
            term = nn(cott[row_block(t), :], joined(k, slice(None), heads)).astype(bf16)
            pool[k, t, :, cols] = term[0:128]
            pool[4 + k, t, :, cols] = term[128:256]
            return carry

        if split:
            g1[u] = []
            for t in range(4):
                part(t, 0)
                g1[u].append(
                    go(
                        pool.at[4 * (1 - c) + k, t, :, cols],
                        r1.at[k, t, :, cols], gs.at[i + t], gr.at[i + t], sibling, z,
                    )
                )
        else:
            lax.fori_loop(0, 4, part, 0)
            theirs = pool.at[4 * (1 - c) + k, :, :, cols]
            g1[u] = [go(theirs, r1.at[k, :, :, cols], gs.at[i], gr.at[i], sibling, z)]

    def gw_first(u):
        k, heads, off, w = UNITS[u]
        cols = slice(2 * off, 2 * off + 2 * w)
        for copy in g1[u]:
            copy.wait_recv()

        def part(t, carry):
            both = pool[4 * c + k, t, :, cols].astype(f32) + r1[k, t, :, cols].astype(f32)
            gsum[k, t, :, cols] = both.astype(bf16)
            return carry

        lax.fori_loop(0, 4, part, 0)
        for j in (2, 1, 3):
            nx, ny = (x + j) % 4, (y + j) % 4
            i = sem0[u] + 4 + j - 1
            rows = pl.ds(pl.multiple_of(nx * 32, 32), 32)
            g2[u, 0, j] = go(
                gsum.at[k, :, rows, pl.ds(2 * off, w)],
                p1a.at[k, j - 1, :, :, pl.ds(off, w)], gs.at[i], gr.at[i], seq_of(nx, y, c), z,
            )
            i += 3
            g2[u, 1, j] = go(
                gsum.at[k, ny, :, pl.ds(2 * off + w, w)],
                p1b.at[k, j - 1, :, pl.ds(off, w)], gs.at[i], gr.at[i], seq_of(x, ny, c), z,
            )

    my_rows = pl.ds(pl.multiple_of(x * 32, 32), 32)

    def gw_second(u):
        k, heads, off, w = UNITS[u]
        cols = slice(off, off + w)
        sum_a = gsum[k, :, my_rows, 2 * off : 2 * off + w].astype(f32)
        sum_b = gsum[k, y, :, 2 * off + w : 2 * off + 2 * w].astype(f32)
        for j in (1, 3, 2):
            g2[u, 0, j].wait_recv()
            sum_a = sum_a + p1a[k, j - 1, :, :, cols].astype(f32)
            g2[u, 1, j].wait_recv()
            sum_b = sum_b + p1b[k, j - 1, :, cols].astype(f32)
        s2a[k, :, :, cols] = sum_a.astype(bf16)
        s2b[k, :, cols] = sum_b.astype(bf16)
        for j in (2, 1, 3):
            nx, ny = (x + j) % 4, (y + j) % 4
            i = sem0[u] + 10 + j - 1
            rows = pl.ds(pl.multiple_of(nx * 32, 32), 32)
            here = pl.ds(off, w)
            g3[u, 0, j] = go(
                s2a.at[k, ny, :, here],
                p2a.at[k, j - 1, :, here], gs.at[i], gr.at[i], seq_of(x, ny, c), z,
            )
            i += 3
            g3[u, 1, j] = go(
                s2b.at[k, rows, here],
                p2b.at[k, j - 1, :, here], gs.at[i], gr.at[i], seq_of(nx, y, c), z,
            )

    def gw_third(u):
        k, heads, off, w = UNITS[u]
        cols = slice(off, off + w)
        sum_a = s2a[k, y, :, cols].astype(f32)
        sum_b = s2b[k, my_rows, cols].astype(f32)
        for j in (1, 3, 2):
            g3[u, 0, j].wait_recv()
            sum_a = sum_a + p2a[k, j - 1, :, cols].astype(f32)
            g3[u, 1, j].wait_recv()
            sum_b = sum_b + p2b[k, j - 1, :, cols].astype(f32)
        fin[k, :, cols] = sum_a.astype(bf16)
        fin[k, :, 256 + off : 256 + off + w] = sum_b.astype(bf16)

    def gw_move(k):
        def move():
            return pltpu.make_async_remote_copy(
                src_ref=fin.at[k],
                dst_ref=gw_hbm.at[my_rows],
                send_sem=ms.at[k],
                recv_sem=mr.at[x],
                device_id={"seq": seq_of(z, y, c), "head": (z + k) % 4},
                device_id_type=pl.DeviceIdType.MESH,
            )

        if k:
            g4[k] = move
            move().start()
        else:

            @pl.when(stays)
            def _():
                load(fin.at[0], gw_hbm.at[my_rows], ms.at[0]).wait()

            @pl.when(jnp.logical_not(stays))
            def _():
                move().start()
                move().wait_send()

    def gw_done():
        for k in (1, 2, 3):
            g4[k]().wait_send()
        for xs in range(4):

            @pl.when(jnp.logical_not(stays & (x == xs)))
            def _():
                pltpu.make_async_remote_copy(
                    src_ref=fin.at[0],
                    dst_ref=gw_hbm.at[pl.ds(32 * xs, 32)],
                    send_sem=ms.at[0],
                    recv_sem=mr.at[xs],
                    device_id={"seq": seq_of(z, y, c), "head": (z + 1) % 4},
                    device_id_type=pl.DeviceIdType.MESH,
                ).wait_recv()

    out_copies = []

    def mix(parts, first, last, lo=0, hi=NB):
        def part(b, carry):
            rows = row_block(b)
            for u in (0, 1):
                cols = slice(512 * u, 512 * u + 512)
                acc = None if first else macc[rows, cols]
                for k, heads in parts:
                    if len(heads) == HEADS:
                        rhs = wt[SLOT[k], cols, :]
                    else:
                        lanes = [slice(h * DV, (h + 1) * DV) for h in heads]
                        rhs = jnp.concatenate([wt[SLOT[k], cols, o] for o in lanes], axis=1)
                    term = nt(joined(k, rows, heads), rhs)
                    acc = term if acc is None else acc + term
                if last:
                    mixv[rows, cols] = acc.astype(bf16)
                else:
                    macc[rows, cols] = acc
            if last:
                pltpu.make_async_copy(mixv.at[rows], mixed_hbm.at[rows], osem.at[b]).start()
            return carry

        lax.fori_loop(lo, hi, part, 0)
        if last:
            for b in range(lo, hi):
                rows = pl.ds(b * BLOCK, BLOCK)
                out_copies.append(
                    pltpu.make_async_copy(mixv.at[rows], mixed_hbm.at[rows], osem.at[b])
                )

    every = (0, 1, 2, 3)
    def flip(b, carry):
        cott[:, row_block(b)] = jnp.transpose(cot[row_block(b), :], (1, 0))
        return carry

    lax.fori_loop(0, NB, flip, 0)
    gw_term("0")
    mix(((0, every),), True, False)
    gw_first("0")

    tot_b, ent_b = scan_b[0], scan_b[9]
    tot_b[...] = jnp.zeros_like(tot_b)

    def back_states(n, grad_out):
        rows = row_block(n)
        for h in range(HEADS):
            lanes = slice(h * DV, (h + 1) * DV)
            hidden = hid[rows, lanes]
            scale = lax.rsqrt(jnp.mean(hidden * hidden, axis=-1, keepdims=True) + EPSILON)
            normed = hidden * scale
            up = grad_out[:, lanes] * gain_ref[0:1, lanes]
            grad = scale * (up - normed * jnp.mean(up * normed, axis=-1, keepdims=True))
            grad = grad.astype(bf16)
            gh[rows, lanes] = grad
            own = nn(phi(qx, h, rows), grad)
            bg[n, h] = own
            tot_b[h] += own

    def back_rest(n, carry):
        rows = row_block(n)
        grad_out = nn(cot[rows, :], wt[SLOT[0]])
        grad_out = grad_out + from_r[rows, :].astype(f32) + from_l[rows, :].astype(f32)
        back_states(n, grad_out)
        return carry

    for name in ("dr", "dl", "ar", "al"):
        rs[name].wait_recv()
    lax.fori_loop(0, NB - 1, back_rest, 0)
    rows = slice((NB - 1) * BLOCK, REST)
    grad_out = nn(cot[rows, :], wt[SLOT[0]])
    grad_out = grad_out + from_r[rows, :].astype(f32) + from_l[rows, :].astype(f32)
    back_states(NB - 1, jnp.concatenate([grad_out, gf[...]], axis=0))
    pair, along_y, along_x, back, done = scan_steps(scan_b, False)

    def back_intra(n, carry):
        rows = row_block(n)
        for h in range(HEADS):
            lanes = slice(h * DV, (h + 1) * DV)
            entries = slice(16 * h, 16 * h + 16)
            qh = qt_ref[entries, rows]
            kh = kt_ref[entries, rows]
            g = gh[rows, lanes]
            v = conv[rows, lanes]
            sc = tn(kh, qh)
            ds = jnp.where(mask_t, nt(v, g) * (0.25 + sc * (1.0 / 16)), 0.0).astype(bf16)
            att = jnp.where(mask_t, 1.0 + sc * (0.25 + sc * (1.0 / 32)), 0.0).astype(bf16)
            wide[rows, lanes] = nn(att, g)
            across = phi_back(nt(prev[n, h], g), qx, t2, h, rows)
            gqv[entries, rows] = (nn(kh, ds) + across).astype(bf16)
            dx[entries, rows] = nt(qh, ds)
        return carry

    pair()
    lax.fori_loop(0, 1, back_intra, 0)
    along_y()
    hand_on(0)
    lax.fori_loop(1, 3, back_intra, 0)
    along_x()
    hand_on(1)
    lax.fori_loop(3, 4, back_intra, 0)
    back()
    gw_second("0")
    out_copies.append(load(gqv, gq_hbm, osem.at[4]))
    done()

    def suffix(t, carry):
        n = NB - 1 - t
        for h in range(HEADS):
            state = ent_b[h]
            ent_b[h] = state + bg[n, h]
            fw[n, h] = (state * wts).astype(bf16)
        return carry

    lax.fori_loop(0, NB, suffix, 0)

    def back_finish(n, carry):
        rows = row_block(n)
        for h in range(HEADS):
            lanes = slice(h * DV, (h + 1) * DV)
            entries = slice(16 * h, 16 * h + 16)
            wide[rows, lanes] += tn(phi(kx, h, rows), fw[n, h])
            across = phi_back(nt(fw[n, h], conv[rows, lanes]), kx, t2, h, rows)
            gkv[entries, rows] = (dx[entries, rows] + across).astype(bf16)
        return carry

    lax.fori_loop(0, 1, back_finish, 0)
    edge_rows[...] = wide[0:8, :]
    edge_back = go(edge_rows, halo_back, hsem.at[2], hsem.at[3], before, z)
    lax.fori_loop(1, NB, back_finish, 0)
    edge_back.wait_recv()
    inside = jnp.where(s < 31, 1.0, 0.0).astype(f32)
    wide[ROWS : ROWS + 8, :] = halo_back[...] * inside
    for n in range(NB):
        at = n * BLOCK
        acc = cw_ref[0:1, :] * wide[at : at + BLOCK, :]
        for j in (1, 2):
            acc = acc + cw_ref[j : j + 1, :] * wide[at + j : at + j + BLOCK, :]
        vbuf[at : at + BLOCK, :] = acc.astype(bf16)
    out_copies.append(load(gkv, gk_hbm, osem.at[5]))
    out_copies.append(load(vbuf, gv_hbm, osem.at[6]))

    gw_third("0")
    gw_move(0)
    ag["l", 2].wait_recv()
    ag["l", 3].wait_recv()
    gw_term("3")
    ag["r", 0].wait_recv()
    ag["r", 1].wait_recv()
    gw_term("1")
    gw_first("3")
    gw_first("1")
    ag["f", 0].wait_recv()
    ag["f", 2].wait_recv()
    gw_term("2a")
    mix(((1, every), (3, every)), False, False)
    gw_second("3")
    gw_second("1")
    gw_first("2a")
    ag["f", 1].wait_recv()
    ag["f", 3].wait_recv()
    gw_term("2b", True)
    mix(((2, every),), False, True, 0, 2)
    gw_first("2b")
    mix(((2, every),), False, True, 2, 4)
    gw_second("2a")
    gw_third("3")
    gw_move(3)
    gw_third("1")
    gw_move(1)
    gw_second("2b")
    gw_third("2a")
    gw_third("2b")
    gw_move(2)
    for copy in out_copies:
        copy.wait()
    gw_done()
    for copy in sends:
        copy.wait_send()


def hand_over_kernel(*refs):
    arrays, results, held, sem_in, sem_out = refs[:5], refs[5:10], refs[10:15], refs[15], refs[16]
    first, second = [], []
    for src, mid, dst in zip(arrays, held, results, strict=True):
        rows = max(src.shape[0] // 8, 32)
        for at in range(0, src.shape[0], rows):
            part = pl.ds(at, rows)
            i = len(first)
            first.append(pltpu.make_async_copy(src.at[part], mid.at[part], sem_in.at[i]))
            second.append(pltpu.make_async_copy(mid.at[part], dst.at[part], sem_out.at[i]))
    for copy in first:
        copy.start()
    for copy, onward in zip(first, second, strict=True):
        copy.wait()
        onward.start()
    for copy in second:
        copy.wait()


def hand_over(*arrays):
    hbm = pl.BlockSpec(memory_space=pl.ANY)
    return pl.pallas_call(
        hand_over_kernel,
        out_shape=tuple(jax.ShapeDtypeStruct(a.shape, a.dtype) for a in arrays),
        in_specs=[hbm] * 5,
        out_specs=(hbm,) * 5,
        scratch_shapes=[pltpu.VMEM(a.shape, a.dtype) for a in arrays]
        + [pltpu.SemaphoreType.DMA((24,))] * 2,
        compiler_params=pltpu.CompilerParams(vmem_limit_bytes=VMEM_LIMIT),
        name="hand_over",
    )(*arrays)


def on_device(query, key_feat, values, conv_w, gain, w_out, cotangent):
    hbm = pl.BlockSpec(memory_space=pl.ANY)
    dma = pltpu.SemaphoreType.DMA
    vmem = pltpu.VMEM
    mixed, gq, gk, gv, gw = pl.pallas_call(
        kernel,
        out_shape=(
            jax.ShapeDtypeStruct((ROWS, FEAT), bf16),
            jax.ShapeDtypeStruct((HEADS * FD, ROWS), bf16),
            jax.ShapeDtypeStruct((HEADS * FD, ROWS), bf16),
            jax.ShapeDtypeStruct((ROWS, CH), bf16),
            jax.ShapeDtypeStruct((128, CH), bf16),
        ),
        in_specs=[hbm] * 7,
        out_specs=(hbm,) * 5,
        scratch_shapes=[
            vmem((16, CH), bf16),
            vmem((8, CH), f32),
            vmem((8, CH), f32),
            vmem((ROWS + 8, CH), f32),
            vmem((HEADS, 32, ROWS), f32),
            vmem((HEADS, 32, ROWS), f32),
            vmem((ROWS, CH), bf16),
            vmem((NB, HEADS, NF, DV), f32),
            vmem((ROWS, CH), f32),
            vmem((NB, HEADS, NF, DV), bf16),
            vmem((4, HEADS, ROWS, DV), bf16),
            vmem((4, FEAT, CH), bf16),
            vmem((ROWS, FEAT), bf16),
            vmem((FEAT, ROWS), bf16),
            vmem((REST, CH), bf16),
            vmem((REST, CH), bf16),
            vmem((REST, CH), bf16),
            vmem((HALF, CH), bf16),
            vmem((HALF, CH), bf16),
            vmem((REST, CH), bf16),
            vmem((REST, CH), bf16),
            vmem((3, FILL, FEAT), bf16),
            vmem((FILL, CH), f32),
            vmem((8, 4, 128, CH), bf16),
            vmem((4, 4, 128, CH), bf16),
            vmem((4, 4, 128, CH), bf16),
            vmem((4, 3, 4, 32, 256), bf16),
            vmem((4, 3, 128, 256), bf16),
            vmem((4, 4, 32, 256), bf16),
            vmem((4, 128, 256), bf16),
            vmem((4, 3, 32, 256), bf16),
            vmem((4, 3, 32, 256), bf16),
            vmem((4, 32, CH), bf16),
            vmem((ROWS, FEAT), f32),
            vmem((ROWS, CH), bf16),
            vmem((NB, HEADS, NF, DV), f32),
            vmem((NB, HEADS, NF, DV), bf16),
            vmem((HEADS * FD, ROWS), f32),
            vmem((7, 32, BLOCK), f32),
            vmem((ROWS, CH), bf16),
            vmem((ROWS, FEAT), bf16),
            vmem((HEADS * FD, ROWS), bf16),
            vmem((HEADS * FD, ROWS), bf16),
            vmem((HEADS * FD, ROWS), bf16),
            vmem((HEADS * FD, ROWS), bf16),
            vmem((3, CH), f32),
            vmem((1, CH), f32),
            dma((7,)),
            dma((24,)),
            dma((7,)),
            dma((4,)),
            dma((24,)),
            dma((24,)),
            dma((65,)),
            dma((65,)),
            dma((80,)),
            dma((80,)),
            dma((4,)),
            dma((4,)),
        ]
        + SCAN_SCRATCH * 2,
        compiler_params=pltpu.CompilerParams(
            collective_id=0, has_side_effects=True, vmem_limit_bytes=VMEM_LIMIT
        ),
        name="sublayer",
    )(query.T, key_feat.T, conv_w, gain.reshape(1, CH), values, w_out, cotangent)
    mixed, gq, gk, gv, gw = hand_over(mixed, gq, gk, gv, gw)
    return mixed, gq.T, gk.T, gv, gw


def solution(mesh):
    both = P("seq", "head")
    return jax.shard_map(
        on_device,
        mesh=mesh,
        in_specs=(both, both, both, P(None, "head"), P("head"), P(None, "head"), both),
        out_specs=(both,) * 5,
        check_vma=False,
    )
```

```python
import functools

import jax
import jax.numpy as jnp
from jax import lax
from jax.experimental import pallas as pl
from jax.experimental.pallas import tpu as pltpu
from jax.sharding import PartitionSpec as P

f32 = jnp.float32
bf16 = jnp.bfloat16
FD = 16
BLOCK = 256
ROWS = 1024
HEADS = 4
NB = ROWS // BLOCK
DV = 128
CH = HEADS * DV
FEAT = 1024
NF = 160
EPSILON = 1e-05
VMEM_LIMIT = 60 * 1024 * 1024


def nn(a, b):
    return lax.dot_general(a, b, (((1,), (0,)), ((), ())), preferred_element_type=f32)


def nt(a, b):
    return lax.dot_general(a, b, (((1,), (1,)), ((), ())), preferred_element_type=f32)


def tn(a, b):
    return lax.dot_general(a, b, (((0,), (0,)), ((), ())), preferred_element_type=f32)


def place():
    s = lax.axis_index("seq")
    z = lax.axis_index("head")
    return s, z, s // 8, (s // 2) % 4, s % 2


def seq_of(x, y, c):
    return (x * 4 + y) * 2 + c


def remote(src, dst, send_sem, recv_sem, seq, head):
    copy = pltpu.make_async_remote_copy(
        src_ref=src,
        dst_ref=dst,
        send_sem=send_sem,
        recv_sem=recv_sem,
        device_id={"seq": seq, "head": head},
        device_id_type=pl.DeviceIdType.MESH,
    )
    copy.start()
    return copy


def greet(devices):
    barrier = pltpu.get_barrier_semaphore()
    for seq, head in devices:
        pl.semaphore_signal(
            barrier, inc=1, device_id={"seq": seq, "head": head}, device_id_type=pl.DeviceIdType.MESH
        )
    pl.semaphore_wait(barrier, len(devices))


def plane_peers(s, z, x, y, c):
    out = [(seq_of(x, y, 1 - c), z)]
    for j in (1, 2, 3):
        out.append((seq_of((x + j) % 4, y, c), z))
        out.append((seq_of(x, (y + j) % 4, c), z))
    return out


def spread(xt_ref, x2_ref):
    for h in range(HEADS):
        x = xt_ref[16 * h : 16 * h + 16, :].astype(f32)
        x2_ref[h, 0:16, :] = x
        x2_ref[h, 16:32, :] = x


def phi(x2_ref, h, cols):
    x = x2_ref[h, 0:16, cols]
    parts = [x * x]
    for d in range(1, 8):
        parts.append(x * x2_ref[h, d : d + 16, cols])
    parts.append(x[0:8] * x2_ref[h, 8:16, cols])
    parts.append((lax.broadcasted_iota(jnp.int32, (8, BLOCK), 0) == 0).astype(f32))
    parts.append(x)
    return jnp.concatenate(parts, axis=0).astype(bf16)


def phi_back(g, x2_ref, t2_ref, h, cols):
    x = x2_ref[h, 0:16, cols]
    acc = g[144:160] + 2.0 * g[0:16] * x
    for d in range(1, 8):
        gd = g[16 * d : 16 * d + 16]
        acc = acc + gd * x2_ref[h, d : d + 16, cols]
        t = gd * x
        t2_ref[d - 1, 0:16, :] = t
        t2_ref[d - 1, 16:32, :] = t
        acc = acc + t2_ref[d - 1, 16 - d : 32 - d, :]
    g8 = g[128:136]
    low = g8 * x2_ref[h, 8:16, cols]
    high = g8 * x[0:8]
    return acc + jnp.concatenate([low, high], axis=0)


def weights():
    r = lax.broadcasted_iota(jnp.int32, (NF, DV), 0)
    return jnp.where(
        r < 16, 1.0 / 32, jnp.where(r < 136, 1.0 / 16, jnp.where(r < 144, 1.0, 0.25))
    ).astype(f32)


def lower():
    r = lax.broadcasted_iota(jnp.int32, (BLOCK, BLOCK), 0)
    c = lax.broadcasted_iota(jnp.int32, (BLOCK, BLOCK), 1)
    return r >= c


SCAN_SCRATCH = [
    pltpu.VMEM((HEADS, NF, DV), f32),
    pltpu.VMEM((2, NF, DV), f32),
    pltpu.VMEM((2, NF, DV), bf16),
    pltpu.VMEM((3, 2, NF, DV), bf16),
    pltpu.VMEM((2, NF, DV), bf16),
    pltpu.VMEM((3, 2, NF, DV), bf16),
    pltpu.VMEM((2, NF, DV), f32),
    pltpu.VMEM((2, NF, DV), f32),
    pltpu.VMEM((2, NF, DV), f32),
    pltpu.VMEM((HEADS, NF, DV), f32),
    pltpu.SemaphoreType.DMA((8,)),
    pltpu.SemaphoreType.DMA((8,)),
]


def scan_steps(refs, forward):
    tot, ra, ys, yr, xs, xr, py, fs, fr, ent, ssem, rsem = refs
    s, z, x, y, c = place()
    sibling = seq_of(x, y, 1 - c)
    mine = pl.ds(2 * c, 2)
    copies = {}

    def counts(me, j):
        met = (me - j >= 0) if forward else (me - j < 0)
        return jnp.where(met, 1.0, 0.0).astype(f32)

    def pair():
        copies["a"] = remote(tot.at[pl.ds(2 * (1 - c), 2)], ra, ssem.at[0], rsem.at[0], sibling, z)

    def along_y():
        copies["a"].wait_recv()
        ys[...] = (tot[mine] + ra[...]).astype(bf16)
        for j in (1, 2, 3):
            copies["y", j] = remote(
                ys, yr.at[j - 1], ssem.at[j], rsem.at[j], seq_of(x, (y + j) % 4, c), z
            )

    def along_x():
        row = tot[mine] + ra[...]
        before = jnp.zeros((2, NF, DV), f32)
        for j in (1, 3, 2):
            copies["y", j].wait_recv()
            got = yr[j - 1].astype(f32)
            row = row + got
            before = before + got * counts(y, j)
        xs[...] = row.astype(bf16)
        py[...] = before
        for j in (1, 2, 3):
            copies["x", j] = remote(
                xs, xr.at[j - 1], ssem.at[3 + j], rsem.at[3 + j], seq_of((x + j) % 4, y, c), z
            )

    def back():
        before = py[...]
        for j in (1, 3, 2):
            copies["x", j].wait_recv()
            before = before + xr[j - 1].astype(f32) * counts(x, j)
        first = jnp.where(c == 0, 1.0, 0.0).astype(f32)
        other = first if forward else 1.0 - first
        fs[...] = before + tot[mine] * other
        ent[mine] = before + ra[...] * (1.0 - other)
        copies["f"] = remote(fs, fr, ssem.at[7], rsem.at[7], sibling, z)

    def done():
        copies["f"].wait_recv()
        ent[pl.ds(2 * (1 - c), 2)] = fr[...]
        for copy in copies.values():
            copy.wait_send()

    return pair, along_y, along_x, back, done


SLOT = {2: 0, 1: 1, 3: 2, 0: 3}
GROUPS = ((2,), (1, 3))
FILL = 256
REST = ROWS - FILL
HALF = REST // 2
UNITS = {
    "0": (0, (0, 1, 2, 3), 0, 256),
    "1": (1, (0, 1, 2, 3), 0, 256),
    "3": (3, (0, 1, 2, 3), 0, 256),
    "2a": (2, (0, 2), 0, 128),
    "2b": (2, (1, 3), 128, 128),
}


def row_block(n):
    return pl.ds(pl.multiple_of(n * BLOCK, BLOCK), BLOCK)


def kernel(
    qt_hbm, kt_hbm, cw_hbm, gain_hbm, v_hbm, w_hbm, cot_hbm,
    mixed_hbm, gq_hbm, gk_hbm, gv_hbm, gw_hbm,
    halo, halo_back, edge_rows, wide, qx, kx, conv, st, hid, prev, oall,
    wt, cot, cott, opp, to_r, to_l, opp_l, opp_r, from_r, from_l, cf, gf,
    pool, r1, gsum, p1a, p1b, s2a, s2b, p2a, p2b, fin, macc,
    gh, bg, fw, dx, t2, vbuf, mixv, gqv, gkv, qt_ref, kt_ref, cw_ref, gain_ref,
    lsem, fsem, osem, hsem, zs, zr, ws, wr, gs, gr, ms, mr, *scans,
):
    s, z, x, y, c = place()
    right, left = (z + 1) % 4, (z + 3) % 4
    sibling = seq_of(x, y, 1 - c)
    after, before = (s + 1) % 32, (s + 31) % 32
    sends = []

    def go(*args):
        copy = remote(*args)
        sends.append(copy)
        return copy

    def load(src, dst, sem):
        copy = pltpu.make_async_copy(src, dst, sem)
        copy.start()
        return copy

    small = [
        load(src, dst, lsem.at[3 + i])
        for i, (src, dst) in enumerate(
            ((kt_hbm, kt_ref), (qt_hbm, qt_ref), (cw_hbm, cw_ref), (gain_hbm, gain_ref))
        )
    ]
    load_v = load(v_hbm, vbuf, lsem.at[2])
    load_cot = load(cot_hbm, cot, lsem.at[0])
    load_w = load(
        w_hbm.at[pl.ds(pl.multiple_of(z * FEAT, FEAT), FEAT)], wt.at[SLOT[0]], lsem.at[1]
    )

    barrier = pltpu.get_barrier_semaphore()

    def signal(seq, head):
        pl.semaphore_signal(
            barrier, inc=1, device_id={"seq": seq, "head": head}, device_id_type=pl.DeviceIdType.MESH
        )

    known = plane_peers(s, z, x, y, c) + [(s, (z + k) % 4) for k in (1, 2, 3)]
    known += [(after, z), (before, z)]
    known += [(seq_of(z, y, c), (z + k) % 4) for k in (1, 2, 3)]
    known += [(seq_of((x + j) % 4, y, c), x) for j in (1, 2, 3)]
    for seq, head in known:
        signal(seq, head)
    stays = x == z

    @pl.when(jnp.logical_not(stays))
    def _():
        signal(seq_of(z, y, c), z)
        signal(s, x)

    for copy in small:
        copy.wait()
    spread(kt_ref, kx)
    spread(qt_ref, qx)
    pl.semaphore_wait(barrier, len(known) + jnp.where(stays, 0, 2))

    row = c * 512 + x * 128 + y * 32
    wz = {}
    for k in (2, 1, 3):
        there = (z + k) % 4
        wz[k] = go(
            w_hbm.at[pl.ds(pl.multiple_of(there * FEAT + row, 32), 32)],
            wt.at[SLOT[4 - k], pl.ds(pl.multiple_of(row, 32), 32)],
            ws.at[k - 1],
            wr.at[k - 1],
            s,
            there,
        )
    edge = go(v_hbm.at[pl.ds(ROWS - 16, 16)], halo, hsem.at[0], hsem.at[1], after, z)

    cz = {}
    for i, (lo, up) in enumerate(((0, 0), (128, 128))):
        here = pl.ds(REST + lo, 128)
        cz["l", i] = go(
            cot_hbm.at[here], cf.at[2, pl.ds(lo, 128)], zs.at[18 + i], zr.at[18 + i], s, right
        )
        lo = 128 - lo
        here = pl.ds(REST + lo, 128)
        cz["r", i] = go(
            cot_hbm.at[here], cf.at[0, pl.ds(lo, 128)], zs.at[20 + i], zr.at[20 + i], s, left
        )
    others = []
    for k in (1, 2, 3):
        for t in range(8):
            at = pl.multiple_of((z + k) % 4 * FEAT + 128 * t, 128)
            others.append(
                load(
                    w_hbm.at[pl.ds(at, 128)],
                    pool.at[2 * (k - 1) + t // 4, t % 4],
                    fsem.at[8 * (k - 1) + t],
                )
            )

    def cot_on():
        cz["l", 0].wait_recv()
        a = pl.ds(0, 128)
        cz["f", 0] = go(cf.at[2, a], cf.at[1, a], zs.at[22], zr.at[22], s, right)
        cz["r", 0].wait_recv()
        b = pl.ds(128, 128)
        cz["f", 1] = go(cf.at[0, b], cf.at[1, b], zs.at[23], zr.at[23], s, left)

    def piece(group, px, py, half):
        at = pl.multiple_of(c * 512 + px * 128 + py * 32, 32)
        slots = pl.ds(0, 1) if group == 0 else pl.ds(1, 2)
        return wt.at[slots, pl.ds(at, 32), pl.ds(half * 256, 256)]

    w1, w2, w3 = {}, {}, {}

    def w_first(group):
        for k in GROUPS[group]:
            wz[4 - k].wait_recv()
        at = 3 + 31 * group
        for j in (1, 2, 3):
            own = piece(group, x, y, 0)
            i = at + j - 1
            w1[group, 0, j] = go(own, own, ws.at[i], wr.at[i], seq_of((x + j) % 4, y, c), z)
            own = piece(group, x, y, 1)
            i = at + j + 2
            w1[group, 1, j] = go(own, own, ws.at[i], wr.at[i], seq_of(x, (y + j) % 4, c), z)

    def w_second(group):
        at = 9 + 31 * group
        for i in (0, 1, 3, 2):
            for half in (0, 1):
                if i:
                    w1[group, half, i].wait_recv()
                if half == 0:
                    block = piece(group, (x - i + 4) % 4, y, 0)
                else:
                    block = piece(group, x, (y - i + 4) % 4, 1)
                for j in (1, 2, 3):
                    to = seq_of(x, (y + j) % 4, c) if half == 0 else seq_of((x + j) % 4, y, c)
                    w2[group, half, i, j] = go(block, block, ws.at[at], wr.at[at], to, z)
                    at += 1

    def w_third(group):
        for (which, *_), copy in w2.items():
            if which == group:
                copy.wait_recv()
        slots = pl.ds(0, 1) if group == 0 else pl.ds(1, 2)
        half = wt.at[slots, pl.ds(pl.multiple_of(c * 512, 512), 512)]
        i = 33 + 31 * group
        w3[group] = go(half, half, ws.at[i], wr.at[i], sibling, z)

    w_first(0)
    load_v.wait()
    wide[8 : 8 + ROWS, :] = vbuf[...].astype(f32)
    w_first(1)
    edge.wait_recv()
    inside = jnp.where(s > 0, 1.0, 0.0).astype(f32)
    wide[0:8, :] = halo[...].astype(f32)[8:16] * inside

    def convolve(n):
        at = 8 + n * BLOCK
        acc = cw_ref[0:1, :] * wide[at : at + BLOCK, :]
        for j in (1, 2):
            acc = acc + cw_ref[j : j + 1, :] * wide[at - j : at - j + BLOCK, :]
        conv[n * BLOCK : (n + 1) * BLOCK, :] = acc.astype(bf16)

    convolve(0)
    w_second(0)
    for n in (1, 2, 3):
        convolve(n)
    cot_on()
    w_second(1)
    load_cot.wait()

    def flip(b, carry):
        cott[:, row_block(b)] = jnp.transpose(cot[row_block(b), :], (1, 0))
        return carry

    lax.fori_loop(0, NB, flip, 0)
    w_third(0)

    scan_a, scan_b = scans[: len(scans) // 2], scans[len(scans) // 2 :]
    tot, ent = scan_a[0], scan_a[9]
    tot[...] = jnp.zeros_like(tot)

    def states(n, carry):
        rows = row_block(n)
        for h in range(HEADS):
            own = nn(phi(kx, h, rows), conv[rows, h * DV : (h + 1) * DV])
            st[n, h] = own
            tot[h] += own
        return carry

    lax.fori_loop(0, NB, states, 0)
    pair, along_y, along_x, back, done = scan_steps(scan_a, True)
    pair()

    def third(half, i):
        return pl.ds(pl.multiple_of(half * HALF + i * (HALF // 2), HALF // 2), HALF // 2)

    def fill(k, dst, half):
        def part(i, carry):
            rows = third(half, i)
            dst[rows, :] = nn(cot[rows, :], wt[SLOT[k]]).astype(bf16)
            return carry

        lax.fori_loop(0, 2, part, 0)

    half_a, half_b = pl.ds(0, HALF), pl.ds(HALF, HALF)
    rs = {}
    w3[0].wait_recv()
    fill(2, opp, 0)
    rs["or"] = go(opp.at[half_a], opp_l, zs.at[12], zr.at[12], s, right)
    fill(2, opp, 1)
    rs["ol"] = go(opp.at[half_b], opp_r, zs.at[13], zr.at[13], s, left)
    w_third(1)
    along_y()
    mask = lower()
    mask_t = jnp.logical_not(mask) | (
        lax.broadcasted_iota(jnp.int32, (BLOCK, BLOCK), 0)
        == lax.broadcasted_iota(jnp.int32, (BLOCK, BLOCK), 1)
    )

    def intra(n, carry):
        rows = row_block(n)
        for h in range(HEADS):
            entries = slice(16 * h, 16 * h + 16)
            sc = tn(qt_ref[entries, rows], kt_ref[entries, rows])
            att = jnp.where(mask, 1.0 + sc * (0.25 + sc * (1.0 / 32)), 0.0).astype(bf16)
            hid[rows, h * DV : (h + 1) * DV] = nn(att, conv[rows, h * DV : (h + 1) * DV])
        return carry

    lax.fori_loop(0, 2, intra, 0)
    w3[1].wait_recv()
    fill(1, to_r, 1)
    rs["dr"] = go(to_r.at[half_b], from_l.at[half_b], zs.at[14], zr.at[14], s, right)
    fill(3, to_l, 0)
    rs["dl"] = go(to_l.at[half_a], from_r.at[half_a], zs.at[15], zr.at[15], s, left)
    along_x()
    lax.fori_loop(2, 4, intra, 0)
    back()
    done()
    wts = weights()

    def finish(n, carry):
        rows = row_block(n)
        for h in range(HEADS):
            lanes = slice(h * DV, (h + 1) * DV)
            state = ent[h]
            ent[h] = state + st[n, h]
            before_block = (state * wts).astype(bf16)
            prev[n, h] = before_block
            hidden = hid[rows, lanes] + tn(phi(qx, h, rows), before_block)
            hid[rows, lanes] = hidden
            scale = lax.rsqrt(jnp.mean(hidden * hidden, axis=-1, keepdims=True) + EPSILON)
            oall[0, h, rows, :] = (hidden * scale * gain_ref[0:1, lanes]).astype(bf16)
        return carry

    lax.fori_loop(0, NB, finish, 0)

    load_w.wait()
    for copy in others:
        copy.wait()
    cz["l", 1].wait_recv()
    cz["r", 1].wait_recv()
    cz["f", 0].wait_recv()
    cz["f", 1].wait_recv()
    gf[...] = nn(cot[REST:ROWS, :], wt[SLOT[0]])
    for k in (1, 2, 3):
        for t in (0, 1):
            block = pool[2 * (k - 1) + t].reshape(512, CH)
            gf[...] += nn(cf[k - 1, :, 512 * t : 512 * t + 512], block)

    def add_in(k, dst, got, half):
        def part(i, carry):
            rows, here = third(half, i), third(0, i)
            term = nn(cot[rows, :], wt[SLOT[k]]) + got[here, :].astype(f32)
            dst[rows, :] = term.astype(bf16)
            return carry

        lax.fori_loop(0, 2, part, 0)

    rs["or"].wait_recv()
    add_in(1, to_r, opp_l, 0)
    rs["ar"] = go(to_r.at[half_a], from_l.at[half_a], zs.at[16], zr.at[16], s, right)
    rs["ol"].wait_recv()
    add_in(3, to_l, opp_r, 1)
    rs["al"] = go(to_l.at[half_b], from_r.at[half_b], zs.at[17], zr.at[17], s, left)

    ag = {}
    for h in range(HEADS):
        ag["l", h] = go(oall.at[0, h], oall.at[3, h], zs.at[h], zr.at[h], s, right)
        e = (h + 2) % 4
        ag["r", e] = go(oall.at[0, e], oall.at[1, e], zs.at[4 + e], zr.at[4 + e], s, left)

    def hand_on(h):
        ag["l", h].wait_recv()
        ag["f", h] = go(oall.at[3, h], oall.at[2, h], zs.at[8 + h], zr.at[8 + h], s, right)
        e = h + 2
        ag["r", e].wait_recv()
        ag["f", e] = go(oall.at[1, e], oall.at[2, e], zs.at[8 + e], zr.at[8 + e], s, left)

    def joined(k, rows, heads):
        return jnp.concatenate([oall[k, h, rows, :] for h in heads], axis=1)

    g1, g2, g3, g4 = {}, {}, {}, {}
    sem0 = {name: 16 * i for i, name in enumerate(UNITS)}

    def gw_term(u, split=False):
        k, heads, off, w = UNITS[u]
        cols = pl.ds(2 * off, 2 * w)
        i = sem0[u]

        def part(t, carry):
            term = nn(cott[row_block(t), :], joined(k, slice(None), heads)).astype(bf16)
            pool[k, t, :, cols] = term[0:128]
            pool[4 + k, t, :, cols] = term[128:256]
            return carry

        if split:
            g1[u] = []
            for t in range(4):
                part(t, 0)
                g1[u].append(
                    go(
                        pool.at[4 * (1 - c) + k, t, :, cols],
                        r1.at[k, t, :, cols], gs.at[i + t], gr.at[i + t], sibling, z,
                    )
                )
        else:
            lax.fori_loop(0, 4, part, 0)
            theirs = pool.at[4 * (1 - c) + k, :, :, cols]
            g1[u] = [go(theirs, r1.at[k, :, :, cols], gs.at[i], gr.at[i], sibling, z)]

    def gw_first(u):
        k, heads, off, w = UNITS[u]
        cols = slice(2 * off, 2 * off + 2 * w)
        for copy in g1[u]:
            copy.wait_recv()

        def part(t, carry):
            both = pool[4 * c + k, t, :, cols].astype(f32) + r1[k, t, :, cols].astype(f32)
            gsum[k, t, :, cols] = both.astype(bf16)
            return carry

        lax.fori_loop(0, 4, part, 0)
        for j in (2, 1, 3):
            nx, ny = (x + j) % 4, (y + j) % 4
            i = sem0[u] + 4 + j - 1
            rows = pl.ds(pl.multiple_of(nx * 32, 32), 32)
            g2[u, 0, j] = go(
                gsum.at[k, :, rows, pl.ds(2 * off, w)],
                p1a.at[k, j - 1, :, :, pl.ds(off, w)], gs.at[i], gr.at[i], seq_of(nx, y, c), z,
            )
            i += 3
            g2[u, 1, j] = go(
                gsum.at[k, ny, :, pl.ds(2 * off + w, w)],
                p1b.at[k, j - 1, :, pl.ds(off, w)], gs.at[i], gr.at[i], seq_of(x, ny, c), z,
            )

    my_rows = pl.ds(pl.multiple_of(x * 32, 32), 32)

    def gw_second(u):
        k, heads, off, w = UNITS[u]
        cols = slice(off, off + w)
        sum_a = gsum[k, :, my_rows, 2 * off : 2 * off + w].astype(f32)
        sum_b = gsum[k, y, :, 2 * off + w : 2 * off + 2 * w].astype(f32)
        for j in (1, 3, 2):
            g2[u, 0, j].wait_recv()
            sum_a = sum_a + p1a[k, j - 1, :, :, cols].astype(f32)
            g2[u, 1, j].wait_recv()
            sum_b = sum_b + p1b[k, j - 1, :, cols].astype(f32)
        s2a[k, :, :, cols] = sum_a.astype(bf16)
        s2b[k, :, cols] = sum_b.astype(bf16)
        for j in (2, 1, 3):
            nx, ny = (x + j) % 4, (y + j) % 4
            i = sem0[u] + 10 + j - 1
            rows = pl.ds(pl.multiple_of(nx * 32, 32), 32)
            here = pl.ds(off, w)
            g3[u, 0, j] = go(
                s2a.at[k, ny, :, here],
                p2a.at[k, j - 1, :, here], gs.at[i], gr.at[i], seq_of(x, ny, c), z,
            )
            i += 3
            g3[u, 1, j] = go(
                s2b.at[k, rows, here],
                p2b.at[k, j - 1, :, here], gs.at[i], gr.at[i], seq_of(nx, y, c), z,
            )

    def gw_third(u):
        k, heads, off, w = UNITS[u]
        cols = slice(off, off + w)
        sum_a = s2a[k, y, :, cols].astype(f32)
        sum_b = s2b[k, my_rows, cols].astype(f32)
        for j in (1, 3, 2):
            g3[u, 0, j].wait_recv()
            sum_a = sum_a + p2a[k, j - 1, :, cols].astype(f32)
            g3[u, 1, j].wait_recv()
            sum_b = sum_b + p2b[k, j - 1, :, cols].astype(f32)
        fin[k, :, cols] = sum_a.astype(bf16)
        fin[k, :, 256 + off : 256 + off + w] = sum_b.astype(bf16)

    def gw_move(k):
        def move():
            return pltpu.make_async_remote_copy(
                src_ref=fin.at[k],
                dst_ref=gw_hbm.at[my_rows],
                send_sem=ms.at[k],
                recv_sem=mr.at[x],
                device_id={"seq": seq_of(z, y, c), "head": (z + k) % 4},
                device_id_type=pl.DeviceIdType.MESH,
            )

        if k:
            g4[k] = move
            move().start()
        else:

            @pl.when(stays)
            def _():
                load(fin.at[0], gw_hbm.at[my_rows], ms.at[0]).wait()

            @pl.when(jnp.logical_not(stays))
            def _():
                move().start()
                move().wait_send()

    def gw_done():
        for k in (1, 2, 3):
            g4[k]().wait_send()
        for xs in range(4):

            @pl.when(jnp.logical_not(stays & (x == xs)))
            def _():
                pltpu.make_async_remote_copy(
                    src_ref=fin.at[0],
                    dst_ref=gw_hbm.at[pl.ds(32 * xs, 32)],
                    send_sem=ms.at[0],
                    recv_sem=mr.at[xs],
                    device_id={"seq": seq_of(z, y, c), "head": (z + 1) % 4},
                    device_id_type=pl.DeviceIdType.MESH,
                ).wait_recv()

    out_copies = []

    def mix(parts, first, last, lo=0, hi=NB):
        def part(b, carry):
            rows = row_block(b)
            for u in (0, 1):
                cols = slice(512 * u, 512 * u + 512)
                acc = None if first else macc[rows, cols]
                for k, heads in parts:
                    if len(heads) == HEADS:
                        rhs = wt[SLOT[k], cols, :]
                    else:
                        lanes = [slice(h * DV, (h + 1) * DV) for h in heads]
                        rhs = jnp.concatenate([wt[SLOT[k], cols, o] for o in lanes], axis=1)
                    term = nt(joined(k, rows, heads), rhs)
                    acc = term if acc is None else acc + term
                if last:
                    mixv[rows, cols] = acc.astype(bf16)
                else:
                    macc[rows, cols] = acc
            if last:
                pltpu.make_async_copy(mixv.at[rows], mixed_hbm.at[rows], osem.at[b]).start()
            return carry

        lax.fori_loop(lo, hi, part, 0)
        if last:
            for b in range(lo, hi):
                rows = pl.ds(b * BLOCK, BLOCK)
                out_copies.append(
                    pltpu.make_async_copy(mixv.at[rows], mixed_hbm.at[rows], osem.at[b])
                )

    every = (0, 1, 2, 3)
    gw_term("0")
    mix(((0, every),), True, False)
    gw_first("0")

    tot_b, ent_b = scan_b[0], scan_b[9]
    tot_b[...] = jnp.zeros_like(tot_b)

    def back_states(n, grad_out):
        rows = row_block(n)
        for h in range(HEADS):
            lanes = slice(h * DV, (h + 1) * DV)
            hidden = hid[rows, lanes]
            scale = lax.rsqrt(jnp.mean(hidden * hidden, axis=-1, keepdims=True) + EPSILON)
            normed = hidden * scale
            up = grad_out[:, lanes] * gain_ref[0:1, lanes]
            grad = scale * (up - normed * jnp.mean(up * normed, axis=-1, keepdims=True))
            grad = grad.astype(bf16)
            gh[rows, lanes] = grad
            own = nn(phi(qx, h, rows), grad)
            bg[n, h] = own
            tot_b[h] += own

    def back_rest(n, carry):
        rows = row_block(n)
        grad_out = nn(cot[rows, :], wt[SLOT[0]])
        grad_out = grad_out + from_r[rows, :].astype(f32) + from_l[rows, :].astype(f32)
        back_states(n, grad_out)
        return carry

    back_states(NB - 1, gf[...])
    for name in ("dr", "dl", "ar", "al"):
        rs[name].wait_recv()
    lax.fori_loop(0, NB - 1, back_rest, 0)
    pair, along_y, along_x, back, done = scan_steps(scan_b, False)

    def back_intra(n, carry):
        rows = row_block(n)
        for h in range(HEADS):
            lanes = slice(h * DV, (h + 1) * DV)
            entries = slice(16 * h, 16 * h + 16)
            qh = qt_ref[entries, rows]
            kh = kt_ref[entries, rows]
            g = gh[rows, lanes]
            v = conv[rows, lanes]
            sc = tn(kh, qh)
            ds = jnp.where(mask_t, nt(v, g) * (0.25 + sc * (1.0 / 16)), 0.0).astype(bf16)
            att = jnp.where(mask_t, 1.0 + sc * (0.25 + sc * (1.0 / 32)), 0.0).astype(bf16)
            wide[rows, lanes] = nn(att, g)
            across = phi_back(nt(prev[n, h], g), qx, t2, h, rows)
            gqv[entries, rows] = (nn(kh, ds) + across).astype(bf16)
            dx[entries, rows] = nt(qh, ds)
        return carry

    pair()
    lax.fori_loop(0, 1, back_intra, 0)
    along_y()
    hand_on(0)
    lax.fori_loop(1, 3, back_intra, 0)
    along_x()
    hand_on(1)
    lax.fori_loop(3, 4, back_intra, 0)
    back()
    gw_second("0")
    out_copies.append(load(gqv, gq_hbm, osem.at[4]))
    done()

    def suffix(t, carry):
        n = NB - 1 - t
        for h in range(HEADS):
            state = ent_b[h]
            ent_b[h] = state + bg[n, h]
            fw[n, h] = (state * wts).astype(bf16)
        return carry

    lax.fori_loop(0, NB, suffix, 0)

    def back_finish(n, carry):
        rows = row_block(n)
        for h in range(HEADS):
            lanes = slice(h * DV, (h + 1) * DV)
            entries = slice(16 * h, 16 * h + 16)
            wide[rows, lanes] += tn(phi(kx, h, rows), fw[n, h])
            across = phi_back(nt(fw[n, h], conv[rows, lanes]), kx, t2, h, rows)
            gkv[entries, rows] = (dx[entries, rows] + across).astype(bf16)
        return carry

    lax.fori_loop(0, 1, back_finish, 0)
    edge_rows[...] = wide[0:8, :]
    edge_back = go(edge_rows, halo_back, hsem.at[2], hsem.at[3], before, z)
    lax.fori_loop(1, NB, back_finish, 0)
    edge_back.wait_recv()
    inside = jnp.where(s < 31, 1.0, 0.0).astype(f32)
    wide[ROWS : ROWS + 8, :] = halo_back[...] * inside
    for n in range(NB):
        at = n * BLOCK
        acc = cw_ref[0:1, :] * wide[at : at + BLOCK, :]
        for j in (1, 2):
            acc = acc + cw_ref[j : j + 1, :] * wide[at + j : at + j + BLOCK, :]
        vbuf[at : at + BLOCK, :] = acc.astype(bf16)
    out_copies.append(load(gkv, gk_hbm, osem.at[5]))
    out_copies.append(load(vbuf, gv_hbm, osem.at[6]))

    gw_third("0")
    gw_move(0)
    ag["l", 2].wait_recv()
    ag["l", 3].wait_recv()
    gw_term("3")
    ag["r", 0].wait_recv()
    ag["r", 1].wait_recv()
    gw_term("1")
    gw_first("3")
    gw_first("1")
    ag["f", 0].wait_recv()
    ag["f", 2].wait_recv()
    gw_term("2a")
    mix(((1, every), (3, every)), False, False, 0, 2)
    gw_second("3")
    gw_second("1")
    gw_first("2a")
    ag["f", 1].wait_recv()
    ag["f", 3].wait_recv()
    gw_term("2b", True)
    mix(((2, every),), False, True, 0, 2)
    gw_first("2b")
    mix(((1, every), (3, every), (2, every)), False, True, 2, 3)
    gw_second("2a")
    gw_third("3")
    gw_move(3)
    gw_third("1")
    gw_move(1)
    gw_second("2b")
    mix(((1, every), (3, every), (2, every)), False, True, 3, 4)
    gw_third("2a")
    gw_third("2b")
    gw_move(2)
    for copy in out_copies:
        copy.wait()
    gw_done()
    for copy in sends:
        copy.wait_send()


def hand_over_kernel(*refs):
    arrays, results, held, sem_in, sem_out = refs[:5], refs[5:10], refs[10:15], refs[15], refs[16]
    first, second = [], []
    for src, mid, dst in zip(arrays, held, results, strict=True):
        rows = max(src.shape[0] // 8, 32)
        for at in range(0, src.shape[0], rows):
            part = pl.ds(at, rows)
            i = len(first)
            first.append(pltpu.make_async_copy(src.at[part], mid.at[part], sem_in.at[i]))
            second.append(pltpu.make_async_copy(mid.at[part], dst.at[part], sem_out.at[i]))
    for copy in first:
        copy.start()
    for copy, onward in zip(first, second, strict=True):
        copy.wait()
        onward.start()
    for copy in second:
        copy.wait()


def hand_over(*arrays):
    hbm = pl.BlockSpec(memory_space=pl.ANY)
    return pl.pallas_call(
        hand_over_kernel,
        out_shape=tuple(jax.ShapeDtypeStruct(a.shape, a.dtype) for a in arrays),
        in_specs=[hbm] * 5,
        out_specs=(hbm,) * 5,
        scratch_shapes=[pltpu.VMEM(a.shape, a.dtype) for a in arrays]
        + [pltpu.SemaphoreType.DMA((24,))] * 2,
        compiler_params=pltpu.CompilerParams(vmem_limit_bytes=VMEM_LIMIT),
        name="hand_over",
    )(*arrays)


def on_device(query, key_feat, values, conv_w, gain, w_out, cotangent):
    hbm = pl.BlockSpec(memory_space=pl.ANY)
    dma = pltpu.SemaphoreType.DMA
    vmem = pltpu.VMEM
    mixed, gq, gk, gv, gw = pl.pallas_call(
        kernel,
        out_shape=(
            jax.ShapeDtypeStruct((ROWS, FEAT), bf16),
            jax.ShapeDtypeStruct((HEADS * FD, ROWS), bf16),
            jax.ShapeDtypeStruct((HEADS * FD, ROWS), bf16),
            jax.ShapeDtypeStruct((ROWS, CH), bf16),
            jax.ShapeDtypeStruct((128, CH), bf16),
        ),
        in_specs=[hbm] * 7,
        out_specs=(hbm,) * 5,
        scratch_shapes=[
            vmem((16, CH), bf16),
            vmem((8, CH), f32),
            vmem((8, CH), f32),
            vmem((ROWS + 8, CH), f32),
            vmem((HEADS, 32, ROWS), f32),
            vmem((HEADS, 32, ROWS), f32),
            vmem((ROWS, CH), bf16),
            vmem((NB, HEADS, NF, DV), f32),
            vmem((ROWS, CH), f32),
            vmem((NB, HEADS, NF, DV), bf16),
            vmem((4, HEADS, ROWS, DV), bf16),
            vmem((4, FEAT, CH), bf16),
            vmem((ROWS, FEAT), bf16),
            vmem((FEAT, ROWS), bf16),
            vmem((REST, CH), bf16),
            vmem((REST, CH), bf16),
            vmem((REST, CH), bf16),
            vmem((HALF, CH), bf16),
            vmem((HALF, CH), bf16),
            vmem((REST, CH), bf16),
            vmem((REST, CH), bf16),
            vmem((3, FILL, FEAT), bf16),
            vmem((FILL, CH), f32),
            vmem((8, 4, 128, CH), bf16),
            vmem((4, 4, 128, CH), bf16),
            vmem((4, 4, 128, CH), bf16),
            vmem((4, 3, 4, 32, 256), bf16),
            vmem((4, 3, 128, 256), bf16),
            vmem((4, 4, 32, 256), bf16),
            vmem((4, 128, 256), bf16),
            vmem((4, 3, 32, 256), bf16),
            vmem((4, 3, 32, 256), bf16),
            vmem((4, 32, CH), bf16),
            vmem((ROWS, FEAT), f32),
            vmem((ROWS, CH), bf16),
            vmem((NB, HEADS, NF, DV), f32),
            vmem((NB, HEADS, NF, DV), bf16),
            vmem((HEADS * FD, ROWS), f32),
            vmem((7, 32, BLOCK), f32),
            vmem((ROWS, CH), bf16),
            vmem((ROWS, FEAT), bf16),
            vmem((HEADS * FD, ROWS), bf16),
            vmem((HEADS * FD, ROWS), bf16),
            vmem((HEADS * FD, ROWS), bf16),
            vmem((HEADS * FD, ROWS), bf16),
            vmem((3, CH), f32),
            vmem((1, CH), f32),
            dma((7,)),
            dma((24,)),
            dma((7,)),
            dma((4,)),
            dma((24,)),
            dma((24,)),
            dma((65,)),
            dma((65,)),
            dma((80,)),
            dma((80,)),
            dma((4,)),
            dma((4,)),
        ]
        + SCAN_SCRATCH * 2,
        compiler_params=pltpu.CompilerParams(
            collective_id=0, has_side_effects=True, vmem_limit_bytes=VMEM_LIMIT
        ),
        name="sublayer",
    )(query.T, key_feat.T, conv_w, gain.reshape(1, CH), values, w_out, cotangent)
    mixed, gq, gk, gv, gw = hand_over(mixed, gq, gk, gv, gw)
    return mixed, gq.T, gk.T, gv, gw


def solution(mesh):
    both = P("seq", "head")
    return jax.shard_map(
        on_device,
        mesh=mesh,
        in_specs=(both, both, both, P(None, "head"), P("head"), P(None, "head"), both),
        out_specs=(both,) * 5,
        check_vma=False,
    )
```
